32 devices in a mesh: slab: 8 (over z, x), skip: 4 (over y, core).
Axes of the slice: x: 2, y: 2, z: 4, core: 2. Of those that a mesh axis runs over, the one named last changes fastest.
Arguments:
- decoder_tokens: bfloat16 [65536, 192], P(('slab', 'skip')), may hold values from -6 to 6
- skip_tokens: bfloat16 [65536, 192], P(('slab', 'skip')), may hold values from -6 to 6
- cotangent: bfloat16 [65536, 192], P(('slab', 'skip')), may hold values from -6 to 6
- extents: int32 [8], P('slab'), may hold values from 8 to 16
- assignment: int32 [8, 128], P('slab', 'skip'), may hold values from 0 to 127, as said below
- mat_master: float32 [32, 13824], P(('slab', 'skip'))
- mat_first: float32 [32, 13824], P(('slab', 'skip')), may hold values from -0.0024414062 to 0.0024414062
- mat_second: float32 [32, 13824], P(('slab', 'skip')), may hold values from 2.2384885e-09 to 8.953954e-09
- mat_average: float32 [32, 13824], P(('slab', 'skip'))
- vec_master: float32 [32, 72], P(('slab', 'skip'))
- vec_first: float32 [32, 72], P(('slab', 'skip')), may hold values from -0.0024414062 to 0.0024414062
- vec_second: float32 [32, 72], P(('slab', 'skip')), may hold values from 2.2384885e-09 to 8.953954e-09
- vec_average: float32 [32, 72], P(('slab', 'skip'))
- table_master: float32 [343, 6], replicated, may hold values from -4 to 4
- table_first: float32 [343, 6], replicated, may hold values from -0.0024414062 to 0.0024414062
- table_second: float32 [343, 6], replicated, may hold values from 2.2384885e-09 to 8.953954e-09
- table_average: float32 [343, 6], replicated, may hold values from -4 to 4
Outputs:
- layer_output: bfloat16 [65536, 192], P(('slab', 'skip'))
- grad_decoder: float32 [65536, 192], P(('slab', 'skip'))
- grad_skip: float32 [65536, 192], P(('slab', 'skip'))
- global_norm: float32 [], replicated
- mat_grad: float32 [32, 13824], P(('slab', 'skip'))
- mat_master_new: float32 [32, 13824], P(('slab', 'skip'))
- mat_first_new: float32 [32, 13824], P(('slab', 'skip'))
- mat_second_new: float32 [32, 13824], P(('slab', 'skip'))
- mat_average_new: float32 [32, 13824], P(('slab', 'skip'))
- mat_low: bfloat16 [32, 13824], P(('slab', 'skip'))
- vec_grad: float32 [32, 72], P(('slab', 'skip'))
- vec_master_new: float32 [32, 72], P(('slab', 'skip'))
- vec_first_new: float32 [32, 72], P(('slab', 'skip'))
- vec_second_new: float32 [32, 72], P(('slab', 'skip'))
- vec_average_new: float32 [32, 72], P(('slab', 'skip'))
- vec_low: bfloat16 [32, 72], P(('slab', 'skip'))
- table_grad: float32 [343, 6], replicated
- table_master_new: float32 [343, 6], replicated
- table_first_new: float32 [343, 6], replicated
- table_second_new: float32 [343, 6], replicated
- table_average_new: float32 [343, 6], replicated
- table_low: bfloat16 [343, 6], replicated
The draws below stay inside these ranges and needn't reach their ends.
Inputs may be any that keep to these rules, and one draw needn't show every extreme that they name: `assignment`: each row is a permutation of the slab's windows. The 32 entries held by one index of skip name at most 8 windows of any one aligned block of 32, and exactly 8 of some block.
All inputs are finite; a program needn't handle non-finite values.
Results may differ from the reference program's by a relative error of at most 0.012.
The reference program's roundings to bfloat16 on the way count: a program that leaves them out, or rounds other values in their place, can miss the bound.
Values may be sent and summed in bfloat16 or wider, within the bound.
No kernel may reach another device: no remote copies, remote signals or barrier semaphores. Data moves between devices by JAX's collectives and lax.ppermute only.
A program may use at most 128 MiB of HBM per device.

```python
import math
import jax
import jax.numpy as jnp
from jax import lax

C = 192
HEADS = 6
HEAD_DIM = 32
HIDDEN_SIZE = 768
WS = 4
DEPTH = 16
STEP = 10
WIN_DEV = 32
WTOK = 64
REL = 343
SLAB_WIN = 128
WINDOWS = 1024
TOKENS = 65536
MAT = 442368
VEC = 2304
PARAMS = 446730
N_SLAB = 8
DEVICES = 32


def matrix_pack(key):
    shapes = ((C, C, C), (C, 2 * C, C), (C, C, C // 8), (C, HIDDEN_SIZE, C), (HIDDEN_SIZE, C, HIDDEN_SIZE))
    pieces = []
    number = 0
    for row_count, column_count, fan_in in shapes:
        noise_draw = jax.random.normal(jax.random.fold_in(key, number), (row_count * column_count,), jnp.float32)
        pieces.append((noise_draw * fan_in ** (-0.5)).reshape(DEVICES, row_count * column_count // DEVICES))
        number = number + 1
    return jnp.concatenate(pieces, axis=1)


def vector_pack(key):
    width_ramp = 0.5 + jnp.arange(C, dtype=jnp.float32) / C

    def gain_draw(number):
        return width_ramp * jax.random.uniform(jax.random.fold_in(key, number), (C,), jnp.float32, 0.7, 1.4)

    def shift_draw(number, length):
        return 0.3 * jax.random.normal(jax.random.fold_in(key, number), (length,), jnp.float32)
    flat = jnp.concatenate([gain_draw(1), shift_draw(2, C), shift_draw(3, C), shift_draw(4, C), shift_draw(5, C), gain_draw(6), shift_draw(7, C), shift_draw(8, HIDDEN_SIZE), shift_draw(9, C)])
    return flat.reshape(DEVICES, VEC // DEVICES)


def draw_mat_master(key, part):
    key = jax.random.fold_in(key, 11)
    return matrix_pack(key)


def draw_mat_average(key, part):
    key = jax.random.fold_in(key, 12)
    return matrix_pack(key)


def draw_vec_master(key, part):
    key = jax.random.fold_in(key, 13)
    return vector_pack(key)


def draw_vec_average(key, part):
    key = jax.random.fold_in(key, 14)
    return vector_pack(key)


def draw_assignment(key, part):
    key = jax.random.fold_in(key, 15)
    owners = SLAB_WIN // WIN_DEV
    slab_count = WINDOWS // SLAB_WIN

    def device_order(device_key):
        return jax.random.permutation(device_key, WIN_DEV)

    def one_slab(slab_key):
        relabel = jax.random.permutation(jax.random.fold_in(slab_key, 1), owners)
        offsets = jax.vmap(device_order)(jax.random.split(jax.random.fold_in(slab_key, 2), owners))
        device_index = jnp.arange(owners, dtype=jnp.int32)[:, None]
        owner_index = relabel[(device_index + offsets) % owners].reshape(-1)
        hit_table = (owner_index[:, None] == jnp.arange(owners, dtype=jnp.int32)[None, :]).astype(jnp.int32)
        rank_within = jnp.sum((jnp.cumsum(hit_table, axis=0) - hit_table) * hit_table, axis=1)
        local_orders = jax.vmap(device_order)(jax.random.split(jax.random.fold_in(slab_key, 3), owners))
        return owner_index * WIN_DEV + local_orders[owner_index, rank_within]
    return jax.vmap(one_slab)(jax.random.split(key, slab_count)).astype(jnp.int32)


def with_ends(values, stream_key, smallest, largest):
    longest = values.shape.index(max(values.shape))
    spots = []
    for shift in (0, 1):
        where = [jax.random.randint(jax.random.fold_in(stream_key, axis), (), 0, length) for axis, length in enumerate(values.shape)]
        where[longest] = (where[longest] + shift) % values.shape[longest]
        spots.append(tuple(where))
    return values.at[spots[0]].set(smallest).at[spots[1]].set(largest)


def steps_of(key, shape, cuts, low, high):
    level, own = 1.0, jax.random.fold_in(key, 6)
    for position, parts in cuts:
        steps = jnp.exp(jax.random.uniform(jax.random.fold_in(own, position), (parts,), jnp.float32, low / len(cuts), high / len(cuts)))
        level = level * jnp.repeat(steps, shape[position] // parts).reshape([-1 if axis == position else 1 for axis in range(len(shape))])
    return level


def centred(key, dims, scale, bound, cuts=(), kind=jnp.bfloat16):
    drawn = scale * jax.random.normal(key, dims, jnp.float32)
    if cuts:
        drawn = drawn * steps_of(key, dims, cuts, -0.22, 0.18)
    return jnp.clip(drawn, -bound, bound).astype(kind)


def setup_inputs(seed: int = 0) -> dict:
    arg_keys = jax.random.split(jax.random.key(seed), 18)
    return {
        "decoder_tokens": centred(arg_keys[0], (TOKENS, C), 1.0, 6.0, ((0, 32),)),
        "skip_tokens": centred(arg_keys[1], (TOKENS, C), 1.0, 6.0, ((0, 32),)),
        "cotangent": centred(arg_keys[2], (TOKENS, C), 1.0, 6.0, ((0, 32),)),
        "extents": with_ends(jax.random.randint(arg_keys[3], (N_SLAB,), DEPTH // 2, DEPTH + 1), jax.random.fold_in(arg_keys[3], 1), DEPTH // 2, DEPTH).astype(jnp.int32),
        "assignment": draw_assignment(jax.random.fold_in(arg_keys[17], 71), 0),
        "mat_master": draw_mat_master(jax.random.fold_in(arg_keys[17], 71), 0),
        "mat_first": centred(arg_keys[6], (DEVICES, MAT // DEVICES), (0.11 * PARAMS ** -0.5), 0.0024414062, ((0, 32),), jnp.float32),
        "mat_second": jnp.clip(jnp.exp(math.log(8.953954022672406e-09) - 1.3862944 * jax.random.uniform(arg_keys[7], (DEVICES, MAT // DEVICES), jnp.float32) ** steps_of(arg_keys[7], (DEVICES, MAT // DEVICES), ((0, 32),), -0.2, 0.2)), 2.2384885056681014e-09, 8.953954022672406e-09),
        "mat_average": draw_mat_average(jax.random.fold_in(arg_keys[17], 71), 0),
        "vec_master": draw_vec_master(jax.random.fold_in(arg_keys[17], 71), 0),
        "vec_first": centred(arg_keys[10], (DEVICES, VEC // DEVICES), (0.11 * PARAMS ** -0.5), 0.0024414062, ((0, 32),), jnp.float32),
        "vec_second": jnp.clip(jnp.exp(math.log(8.953954022672406e-09) - 1.3862944 * jax.random.uniform(arg_keys[11], (DEVICES, VEC // DEVICES), jnp.float32) ** steps_of(arg_keys[11], (DEVICES, VEC // DEVICES), ((0, 32),), -0.2, 0.2)), 2.2384885056681014e-09, 8.953954022672406e-09),
        "vec_average": draw_vec_average(jax.random.fold_in(arg_keys[17], 71), 0),
        "table_master": centred(arg_keys[13], (REL, HEADS), 0.5, 4.0, (), jnp.float32),
        "table_first": centred(arg_keys[14], (REL, HEADS), (0.11 * PARAMS ** -0.5), 0.0024414062, (), jnp.float32),
        "table_second": jnp.clip(jnp.exp(jax.random.uniform(arg_keys[15], (REL, HEADS), jnp.float32, math.log(2.2384885056681014e-09), math.log(8.953954022672406e-09))), 2.2384885056681014e-09, 8.953954022672406e-09),
        "table_average": centred(arg_keys[16], (REL, HEADS), 0.5, 4.0, (), jnp.float32),
    }


EPS = 1e-05
MASK_FILL = -1000000000.0
CLIP = 1.0
BETA_ONE = 0.9
BETA_TWO = 0.999
RATE = 0.3
MATRIX_DECAY = 0.05
ADAM_EPS = 1e-08
EMA_RATE = 0.9

@jax.custom_vjp
def low(v):
    return lax.optimization_barrier(v.astype(jnp.bfloat16)).astype(jnp.float32)

@jax.custom_vjp
def low_back(v):
    return v

def low_keep(v):
    return (low(v), None)

def low_pass(kept, grad):
    return (grad,)

def back_keep(v):
    return (v, None)

def back_low(kept, grad):
    return (low(grad),)
low.defvjp(low_keep, low_pass)
low_back.defvjp(back_keep, back_low)

def round_both(value_in):
    return low(low_back(value_in))

def exact_dot(left, right):
    return jnp.dot(left, right, precision=lax.Precision.HIGHEST)

def unpack_matrices(packed):
    shapes = ((C, C), (C, 2 * C), (C, C), (C, HIDDEN_SIZE), (HIDDEN_SIZE, C))
    result = []
    offset = 0
    for row_count, column_count in shapes:
        piece_width = row_count * column_count // DEVICES
        result.append(packed[:, offset:offset + piece_width].reshape(row_count, column_count))
        offset = offset + piece_width
    return result

def unpack_vectors(packed):
    flat = packed.reshape(-1)
    lengths = (C, C, C, C, C, C, C, HIDDEN_SIZE, C)
    result = []
    offset = 0
    for length in lengths:
        result.append(flat[offset:offset + length])
        offset = offset + length
    return result

def relative_index():
    token_place = jnp.arange(WS ** 3, dtype=jnp.int32)
    span_size = 2 * WS - 1
    coordinates = (token_place // (WS * WS), token_place // WS % WS, token_place % WS)
    offsets = [coordinate[:, None] - coordinate[None, :] + WS - 1 for coordinate in coordinates]
    return ((offsets[0] * span_size + offsets[1]) * span_size + offsets[2]).astype(jnp.int32)

def window_valid(assignment, extents):
    depth_slot = assignment % (DEPTH // WS)
    layers = jnp.clip(extents[:, None] - WS * depth_slot, 0, WS)
    depth_index = (jnp.arange(WTOK, dtype=jnp.int32) // (WS * WS)).astype(jnp.int32)
    return jnp.where(depth_index[None, None, :] < layers[:, :, None], 1.0, 0.0).astype(jnp.float32)

def norm_rows(value_in, gain, shift):
    center = value_in - lax.optimization_barrier(jnp.mean(value_in, axis=-1, keepdims=True))
    scale = lax.rsqrt(lax.optimization_barrier(jnp.mean(center * center, axis=-1, keepdims=True)) + EPS)
    return center * scale * gain + shift

def slab_layer(weights, pieces):
    w_query, w_pair, w_output, w_up, w_down, gain_one, shift_one, bias_query, bias_value, bias_output, gain_two, shift_two, bias_up, bias_down, table_used = weights
    query_in, skip_in, token_valid = pieces
    scale_factor = HEAD_DIM ** (-0.5)
    query_norm = low(norm_rows(query_in, gain_one, shift_one))
    skip_norm = low(norm_rows(skip_in, gain_one, shift_one))
    query_rows = round_both((exact_dot(query_norm, w_query) + bias_query) * scale_factor)
    pair_rows = exact_dot(skip_norm, w_pair)
    key_rows = round_both(pair_rows[:, :C])
    value_rows = round_both(pair_rows[:, C:] + bias_value)
    split_shape = (SLAB_WIN, WTOK, HEADS, HEAD_DIM)
    raw_scores = jnp.einsum('wihd,wjhd->whij', query_rows.reshape(split_shape), key_rows.reshape(split_shape), precision=lax.Precision.HIGHEST)
    position_bias = table_used[relative_index()].transpose(2, 0, 1)
    key_fill = jnp.where(token_valid > 0, 0.0, MASK_FILL)[:, None, None, :]
    scores = low_back(raw_scores + position_bias[None] + key_fill)
    top_score = lax.optimization_barrier(jnp.max(scores, axis=-1, keepdims=True))
    exponent = jnp.exp(scores - top_score)
    probs = low(exponent / lax.optimization_barrier(jnp.sum(exponent, axis=-1, keepdims=True)))
    attended = jnp.einsum('whij,wjhd->wihd', probs, value_rows.reshape(split_shape), precision=lax.Precision.HIGHEST).reshape(SLAB_WIN * WTOK, C)
    attended = round_both(attended)
    branch = low_back(exact_dot(attended, w_output) + bias_output)
    middle = query_in + branch
    hidden_norm = low(norm_rows(middle, gain_two, shift_two))
    upper = low_back(exact_dot(hidden_norm, w_up) + bias_up)
    activated = low(jax.nn.gelu(upper, approximate=False))
    mlp_out = low_back(exact_dot(activated, w_down) + bias_down)
    return token_valid.reshape(-1, 1) * (middle + mlp_out)

def adamw_update(master, first, second, average, grad, factor, decay):
    clipped = grad * factor
    first_new = BETA_ONE * first + (1.0 - BETA_ONE) * clipped
    second_new = BETA_TWO * second + (1.0 - BETA_TWO) * clipped * clipped
    first_hat = first_new / (1.0 - BETA_ONE ** STEP)
    second_hat = second_new / (1.0 - BETA_TWO ** STEP)
    master_new = master - RATE * (first_hat / (jnp.sqrt(second_hat) + ADAM_EPS) + decay * master)
    average_new = EMA_RATE * average + (1.0 - EMA_RATE) * master_new
    return (clipped, master_new, first_new, second_new, average_new, master_new.astype(jnp.bfloat16))

def reference(decoder_tokens, skip_tokens, cotangent, extents, assignment, mat_master, mat_first, mat_second, mat_average, vec_master, vec_first, vec_second, vec_average, table_master, table_first, table_second, table_average):
    valid = window_valid(assignment, extents)
    checked = jax.checkpoint(slab_layer)

    def forward(query_in, skip_in, mat_used, vec_used, table_used):
        weights = tuple(unpack_matrices(mat_used)) + tuple(unpack_vectors(vec_used)) + (table_used,)
        query_slabs = query_in.reshape(N_SLAB, SLAB_WIN * WTOK, C)
        skip_windows = skip_in.reshape(N_SLAB, SLAB_WIN, WTOK, C)
        picked = jnp.take_along_axis(skip_windows, assignment[:, :, None, None].astype(jnp.int32), axis=1)
        picked = picked.reshape(N_SLAB, SLAB_WIN * WTOK, C)

        def one_slab(pieces):
            return checked(weights, pieces)
        result = lax.map(one_slab, (query_slabs, picked, valid))
        return result.reshape(TOKENS, C)
    layer_float, pullback = jax.vjp(forward, decoder_tokens.astype(jnp.float32), skip_tokens.astype(jnp.float32), mat_master.astype(jnp.bfloat16).astype(jnp.float32), vec_master.astype(jnp.bfloat16).astype(jnp.float32), table_master)
    grad_decoder, grad_skip, grad_mat, grad_vec, grad_table = pullback(cotangent.astype(jnp.float32))
    squares = jnp.sum(grad_mat * grad_mat) + jnp.sum(grad_vec * grad_vec) + jnp.sum(grad_table * grad_table)
    global_norm = jnp.sqrt(squares)
    factor = CLIP / jnp.maximum(global_norm, CLIP)
    mat_outs = adamw_update(mat_master, mat_first, mat_second, mat_average, grad_mat, factor, MATRIX_DECAY)
    vec_outs = adamw_update(vec_master, vec_first, vec_second, vec_average, grad_vec, factor, 0.0)
    table_outs = adamw_update(table_master, table_first, table_second, table_average, grad_table, factor, 0.0)
    return (layer_float.astype(jnp.bfloat16), grad_decoder, grad_skip, global_norm, mat_outs[0], mat_outs[1], mat_outs[2], mat_outs[3], mat_outs[4], mat_outs[5], vec_outs[0], vec_outs[1], vec_outs[2], vec_outs[3], vec_outs[4], vec_outs[5], table_outs[0], table_outs[1], table_outs[2], table_outs[3], table_outs[4], table_outs[5])
```

```python
import functools
import math
import jax
import jax.numpy as jnp
from jax import lax
from jax.experimental import pallas as pl
from jax.experimental.pallas import tpu as pltpu
from jax.sharding import PartitionSpec as P

C = 192
HEADS = 6
HEAD_DIM = 32
HIDDEN_SIZE = 768
WS = 4
DEPTH = 16
STEP = 10
WTOK = 64
REL = 343

EPS = 1e-05
MASK_FILL = -1000000000.0
CLIP = 1.0
BETA_ONE = 0.9
BETA_TWO = 0.999
RATE = 0.3
MATRIX_DECAY = 0.05
ADAM_EPS = 1e-08
EMA_RATE = 0.9

BF = jnp.bfloat16
F32 = jnp.float32
GROUP = 256
GWIN = GROUP // WTOK
T = 1024
GROUPS = T // GROUP
WIN = T // WTOK
QSCALE = HEAD_DIM ** (-0.5)
SHAPES = ((C, C), (C, 2 * C), (C, C), (C, HIDDEN_SIZE), (HIDDEN_SIZE, C))
VLEN = (C, C, C, C, C, C, C, HIDDEN_SIZE, C)
VOFF = tuple(sum(VLEN[:n]) for n in range(len(VLEN)))
VEC = sum(VLEN)
MAT = sum(r * c for r, c in SHAPES)
ROWS = 32
OUTER = 4
INNER = ROWS // OUTER
BLOCK = (16, 896)
BLOCK_TILES = BLOCK[1] // 128
VEC_TILE = MAT // ROWS // 128
SIDE_TILE = VEC_TILE + 1
TABLE_LANES = 8 * 384 // ROWS


def mm(a, b):
    return jnp.dot(a, b, preferred_element_type=F32)


def mm_nt(a, b):
    return lax.dot_general(a, b, (((1,), (1,)), ((), ())), preferred_element_type=F32)


def iota(shape, dim):
    return lax.broadcasted_iota(jnp.int32, shape, dim)


def kept(value):
    return pltpu.with_memory_space_constraint(value, pltpu.HBM)


def both(column):
    return jnp.concatenate([column, column], axis=1)


def place(slot):
    span = 2 * WS - 1
    return ((slot >> 4) * span + ((slot >> 2) & 3)) * span + (slot & 3)


def splits(value):
    high = value.astype(BF)
    rest = value - high.astype(F32)
    middle = rest.astype(BF)
    return high, middle, (rest - middle.astype(F32)).astype(BF)


def normed(value):
    center = value - jnp.sum(value, axis=0, keepdims=True) * (1.0 / C)
    scale = lax.rsqrt(jnp.sum(center * center, axis=0, keepdims=True) * (1.0 / C) + EPS)
    return center * scale, scale


def normed_back(grad_hat, hat, scale):
    mean_grad = jnp.sum(grad_hat, axis=0, keepdims=True) * (1.0 / C)
    mean_both = jnp.sum(grad_hat * hat, axis=0, keepdims=True) * (1.0 / C)
    return scale * (grad_hat - mean_grad - hat * mean_both)


def fold(value):
    return sum(value[:, n : n + 128] for n in range(0, value.shape[1], 128))


def gelu_parts(u):
    t = pl.reciprocal(1.0 + (0.3275911 * 0.5**0.5) * jnp.abs(u), approx=True)
    bell = jnp.exp2((-0.5 * math.log2(math.e)) * (u * u))
    series = 0.5 * 1.061405429
    for factor in (-1.453152027, 1.421413741, -0.284496736, 0.254829592):
        series = series * t + 0.5 * factor
    tail = series * t * bell
    cdf = jnp.where(u >= 0.0, 1.0 - tail, tail)
    return u * cdf, cdf + ((0.5 / math.pi) ** 0.5 * u) * bell


def early_kernel(skip_count, windows, chosen, table, after, bias_s, ranks, tab_s, big, count_s):
    del after
    tab_s[...] = jnp.zeros_like(tab_s)
    tab_s[0:HEADS, 0:REL] = table[...]
    hot = (iota((256, 128), 0) == place(iota((256, 128), 1) & 63)).astype(BF)
    total = None
    for part in splits(tab_s[...]):
        part = part.astype(F32)
        for j in range(WTOK):
            turn = (place(j) - place(WTOK - 1)) % 384
            rolled = pltpu.roll(part, turn, 1) if turn else part
            big[0, 8 * j : 8 * j + 8, :] = rolled[:, 0:128]
            big[1, 8 * j : 8 * j + 8, :] = rolled[:, 128:256]
        product = mm(big[0].astype(BF), hot[0:128]) + mm(big[1].astype(BF), hot[128:256])
        total = product if total is None else total + product
    big[0] = total
    for h in range(HEADS):
        bias_s[h] = big[0, pl.ds(h, WTOK, stride=8), :]
    for e in range(skip_count):
        count_s[e] = 0

    def note(w, rank_row):
        owner = lax.div(chosen[w], windows)
        rank = count_s[owner]
        count_s[owner] = rank + 1
        return jnp.where(iota((1, 128), 1) == w, rank, rank_row)

    ranks[...] = lax.fori_loop(0, windows, note, jnp.zeros((1, 128), jnp.int32))


def layer_kernel(
    skip_count,
    windows,
    piece_count,
    chosen,
    extents,
    here,
    ranks,
    dec_all,
    cot_all,
    bias_s,
    *refs,
):
    step = pl.program_id(0)
    packs, refs = refs[:OUTER], refs[OUTER:]
    pieces, refs = refs[:piece_count], refs[piece_count:]
    layer_out, grad_dec, everyone, *refs = refs
    grad_picks, refs = refs[:skip_count], refs[skip_count:]
    grad_packs, refs = refs[:OUTER], refs[OUTER:]
    (
        pick_s,
        big,
        vcol,
        wq,
        wqt,
        wkv,
        wkvt,
        wo,
        wot,
        w1,
        w1t,
        w2,
        w2t,
        xn_s,
        sn_s,
        hn_s,
        o_s,
        gl_s,
        du_s,
        q_s,
        qbd_s,
        kst_s,
        vst_s,
        kcat_s,
        vcat_s,
        pf_s,
        pb_s,
        ds_s,
        da_s,
        do_s,
        dm_s,
        u_s,
        ga_s,
        gh_s,
        gs_s,
        dq_s,
        dkv_s,
        n1_s,
        n2_s,
        n3_s,
        x1_s,
        gds_s,
        aq,
        akv,
        ao,
        a1,
        a2,
        ln_s,
        slab,
        slab_sem,
        dec_s,
        cot_s,
        token_sem,
        pack_s,
        pack_sem,
    ) = refs
    dec, cot = dec_s.at[step], cot_s.at[step]
    stage, block_s = u_s, ga_s
    my_skip, mix = here[0], here[1]
    lane = iota((1, 128), 1)
    left = lane < WTOK

    def tile_of(number):
        j, n = divmod(number, BLOCK_TILES)
        return n, pl.ds(j, ROWS, stride=BLOCK[0]), slice(None)


    def token_copies(n):
        lanes = slice(T * n, T * n + T)
        return [
            pltpu.make_async_copy(dec_all.at[:, lanes], dec_s.at[n], token_sem.at[2 * n]),
            pltpu.make_async_copy(cot_all.at[:, lanes], cot_s.at[n], token_sem.at[2 * n + 1]),
        ]

    for n in range(1, windows // WIN):

        @pl.when(step == n)
        def _(n=n):
            for copy in token_copies(n):
                copy.wait()

    @pl.when(step == 0)
    def _():
        copies = token_copies(0) + [
            pltpu.make_async_copy(
                piece, slab.at[:, n * piece.shape[1] : (n + 1) * piece.shape[1]], slab_sem.at[n]
            )
            for n, piece in enumerate(pieces)
        ]
        pack_copies = [
            pltpu.make_async_copy(packs[n], pack_s.at[n], pack_sem.at[n]) for n in range(OUTER)
        ]
        for copy in pack_copies + copies + [copy for n in range(1, windows // WIN) for copy in token_copies(n)]:
            copy.start()
        for ref in (gds_s, aq, akv, ao, a1, a2, ln_s):
            ref[...] = jnp.zeros_like(ref)
        for ref, rows in ((xn_s, C), (sn_s, C), (hn_s, C), (o_s, C), (gl_s, HIDDEN_SIZE)):
            ref[rows : rows + 16, :] = jnp.ones((16, T), BF)
        for copy in pack_copies:
            copy.wait()
        for outer in range(OUTER):
            for inner in range(INNER):
                k = inner * OUTER + lax.bitwise_xor(my_skip, outer)
                rows = pl.ds(pl.multiple_of(k * BLOCK[0], BLOCK[0]), BLOCK[0])
                for n in range(BLOCK_TILES):
                    block_s[n, rows, :] = pack_s[outer, inner, :, 128 * n : 128 * n + 128].astype(
                        F32
                    )
        offset = 0
        for (rows, cols), plain, turned in zip(
            SHAPES, (wq, wkv, wo, w1, w2), (wqt, wkvt, wot, w1t, w2t)
        ):
            per = rows // ROWS
            tiles = -(-cols // 128)
            for a in range(per):
                first, shift = divmod(offset + a * cols, 128)
                for n in range(tiles):
                    piece = block_s[tile_of(first + n)]
                    if shift and n + 1 < tiles:
                        after = block_s[tile_of(first + n + 1)]
                        piece = jnp.concatenate([piece[:, shift:], after[:, :shift]], axis=1)
                    elif shift:
                        piece = pltpu.roll(piece, 128 - shift, 1)
                    stage[n, pl.ds(a, ROWS, stride=per), :] = piece
            for n in range(tiles):
                width = min(128, cols - 128 * n)
                value = stage[n, 0:rows, :].astype(BF)
                plain[:, 128 * n : 128 * n + width] = value[:, 0:width]
                turned[128 * n : 128 * n + width, :] = jnp.transpose(value)[0:width]
            offset += per * cols
        side = block_s[tile_of(VEC_TILE)]
        per = VEC // ROWS
        vec = jnp.concatenate([side[k : k + 1, 0:per] for k in range(ROWS)], axis=1)
        vcol[...] = jnp.transpose(jnp.broadcast_to(vec, (128, VEC)))
        side = block_s[tile_of(SIDE_TILE)]
        everyone[...] = side.astype(jnp.int32)
        for copy in copies:
            copy.wait()

    def column(number, first=0, last=None):
        start = VOFF[number]
        return vcol[start + first : start + (VLEN[number] if last is None else last), :]

    chunks = [slice(128 * c, 128 * c + 128) for c in range(T // 128)]
    tiles = [slice(GROUP * g, GROUP * g + GROUP) for g in range(GROUPS)]
    layers, valid = [], []
    for c in range(len(chunks)):
        deep = [
            jnp.clip(extents[0] - WS * (chosen[step * WIN + 2 * c + w] & 3), 0, WS) for w in (0, 1)
        ]
        layers.append(jnp.where(left, deep[0], deep[1]))
        valid.append(jnp.where((lane & 63) >> 4 < layers[c], 1.0, 0.0))

    scale_one, scale_two, scale_three = {}, {}, {}

    def stacks(rows, g, stack_ref, cat_ref):
        turned = pltpu.roll(rows, WTOK, 1)
        first, second = rows[:, 0:128], rows[:, 128:256]
        mixed, middle = turned[:, 0:128], turned[:, 128:256]
        at_left = (first, middle, second, mixed)
        at_right = (mixed, first, middle, second)
        for h in range(0, HEADS, 2):
            n = g * HEADS + h
            at = slice(HEAD_DIM * h, HEAD_DIM * h + HEAD_DIM)
            after = slice(HEAD_DIM * h + HEAD_DIM, HEAD_DIM * h + 2 * HEAD_DIM)
            pieces = []
            for w in range(GWIN):
                to = slice(HEAD_DIM * w, HEAD_DIM * w + HEAD_DIM)
                stack_ref[n, to, :] = at_left[w][at, 0:WTOK]
                stack_ref[n + 1, to, :] = at_left[w][after, 0:WTOK]
                pieces.append(jnp.where(left, at_left[w][at], at_right[w][after]))
            pair = jnp.transpose(jnp.concatenate(pieces, axis=0))
            cat_ref[n] = pair[0:WTOK]
            cat_ref[n + 1] = pair[WTOK:]

    window_mask = [
        (iota((HEAD_DIM, GROUP), 1) >> 6 == w).astype(F32).astype(BF) for w in range(GWIN)
    ]

    def spread(rows):
        return jnp.concatenate([rows * mask for mask in window_mask], axis=0)

    def own(stacked, probs):
        parts = []
        for n in range(GWIN // 2):
            cut = mm(
                stacked[2 * HEAD_DIM * n : 2 * HEAD_DIM * (n + 1)],
                probs[:, 128 * n : 128 * n + 128],
            )
            parts.append(jnp.where(left, cut[0:HEAD_DIM], cut[HEAD_DIM:]))
        return jnp.concatenate(parts, axis=1)

    def unstack(product):
        parts = []
        for n in range(GWIN // 2):
            cut = product[2 * HEAD_DIM * n : 2 * HEAD_DIM * (n + 1)]
            parts.append(jnp.where(left, cut[0:HEAD_DIM], cut[HEAD_DIM:]))
        return jnp.concatenate(parts, axis=1)

    def filled(g):
        return jnp.concatenate(
            [
                jnp.concatenate(
                    [
                        jnp.broadcast_to(jnp.where(layers[c] > d, 0.0, MASK_FILL), (WS * WS, 128))
                        for d in range(WS)
                    ],
                    axis=0,
                )
                for c in (2 * g, 2 * g + 1)
            ],
            axis=1,
        )

    def place_of(n):
        g, h = divmod(n, HEADS)
        return slice(HEAD_DIM * h, HEAD_DIM * h + HEAD_DIM), tiles[g]

    def softmax(n, scores, fill):
        scores = scores + both(bias_s[n % HEADS]) + fill
        powers = jnp.exp(scores - jnp.max(scores, axis=0, keepdims=True))
        probs = powers * pl.reciprocal(jnp.sum(powers, axis=0, keepdims=True), approx=True)
        pf_s[n] = probs
        pb_s[n] = probs.astype(BF)

    def softmax_back(n, grad_probs):
        probs = pf_s[n]
        grad_scores = (
            probs * (grad_probs - jnp.sum(probs * grad_probs, axis=0, keepdims=True))
        ).astype(BF)
        gds_s[n % HEADS] += fold(grad_scores.astype(F32))
        ds_s[n] = grad_scores

    def forward(g):
        lanes = tiles[g]
        for c in (2 * g, 2 * g + 1):
            cut = chunks[c]
            hat, scale_one[c] = normed(dec[:, cut].astype(F32))
            n1_s[:, cut] = hat
            xn_s[0:C, cut] = (hat * column(0) + column(1)).astype(BF)
            yield 130
            halves = []
            for w in (0, 1):
                a = chosen[step * WIN + 2 * c + w]
                at = lax.bitwise_xor(a, mix * windows) >> 1
                part = slab[:, pl.ds(pl.multiple_of(at * 128, 128), 128)]
                halves.append(pltpu.roll(part, ((a + w) & 1) * WTOK, 1))
            hat, scale_two[c] = normed(jnp.where(left, halves[0], halves[1]).astype(F32))
            n2_s[:, cut] = hat
            sn_s[0:C, cut] = (hat * column(0) + column(1)).astype(BF)
            yield 160
        query = mm(wqt[...], xn_s[0:C, lanes])
        pair = mm(wkvt[...], sn_s[0:C, lanes])
        q_s[:, lanes] = ((query + both(column(2))) * QSCALE).astype(BF)
        for c in (2 * g, 2 * g + 1):
            dm_s[:, chunks[c]] = (cot[:, chunks[c]].astype(F32) * valid[c]).astype(BF)
        yield 250
        first = g * HEADS
        for n in range(first, first + HEADS):
            qbd_s[n] = spread(q_s[place_of(n)])
        stacks(pair[0:C].astype(BF), g, kst_s, kcat_s)
        yield 250
        stacks((pair[C:] + both(column(3))).astype(BF), g, vst_s, vcat_s)
        yield 250
        fill = filled(g)
        scores = {}
        for n in range(first, first + HEADS + 2):
            if n < first + HEADS:
                scores[n] = mm(kcat_s[n], qbd_s[n])
            if n >= first + 2:
                o_s[place_of(n - 2)] = own(vst_s[n - 2], pb_s[n - 2]).astype(BF)
            if first + 1 <= n <= first + HEADS:
                softmax(n - 1, scores.pop(n - 1), fill)
            yield 180
        product = mm(w2[...], dm_s[:, lanes])
        ga_s[2 * g] = product[:, 0:128]
        ga_s[2 * g + 1] = product[:, 128:256]
        yield 300
        x1_s[:, lanes] = mm(wot[...], o_s[0:C, lanes])
        yield 150
        for c in (2 * g, 2 * g + 1):
            cut = chunks[c]
            middle = dec[:, cut].astype(F32) + x1_s[:, cut] + column(4)
            x1_s[:, cut] = middle
            hat, scale_three[c] = normed(middle)
            n3_s[:, cut] = hat
            hn_s[0:C, cut] = (hat * column(5) + column(6)).astype(BF)
            yield 150

    def feed(g):
        lanes = tiles[g]
        product = mm(w1t[...], hn_s[0:C, lanes])
        u_s[2 * g] = product[:, 0:128]
        u_s[2 * g + 1] = product[:, 128:256]
        yield 300
        piece = 32
        for start in range(0, HIDDEN_SIZE, piece):
            rows = slice(start, start + piece)
            for c in (2 * g, 2 * g + 1):
                active, slope = gelu_parts(u_s[c, rows, :] + column(7, start, start + piece))
                gl_s[rows, chunks[c]] = active.astype(BF)
                du_s[rows, chunks[c]] = (ga_s[c, rows, :] * slope).astype(BF)
            yield 35 * piece // 16
        gh_s[:, lanes] = mm(w1[...], du_s[:, lanes])
        yield 450
        mlp = mm(w2t[...], gl_s[0:HIDDEN_SIZE, lanes]) + both(column(8))
        layer_out[:, lanes] = (
            jnp.concatenate([valid[2 * g], valid[2 * g + 1]], axis=1) * (x1_s[:, lanes] + mlp)
        ).astype(BF)
        yield 500
        for c in (2 * g, 2 * g + 1):
            cut = chunks[c]
            grad, hat = gh_s[:, cut], n3_s[:, cut]
            ln_s[2] += grad * hat
            ln_s[3] += grad
            back = normed_back(grad * column(5), hat, scale_three[c])
            grad_middle = cot[:, cut].astype(F32) * valid[c] + back
            x1_s[:, cut] = grad_middle
            da_s[:, cut] = grad_middle.astype(BF)
            yield 170
        do_s[:, lanes] = mm(wo[...], da_s[:, lanes]).astype(BF)
        yield 150

    def backward(g):
        lanes = tiles[g]
        first = g * HEADS
        spreads, grads = {}, {}
        for n in range(first, first + HEADS + 2):
            if n < first + HEADS:
                at, _ = place_of(n)
                spreads[n] = spread(do_s[at, lanes])
                grads[n] = mm(vcat_s[n], spreads[n])
                twice = jnp.concatenate([pb_s[n], pb_s[n]], axis=0)
                dkv_s[at.start + C : at.stop + C, lanes] = unstack(
                    mm_nt(spreads.pop(n), twice)
                ).astype(BF)
            if n >= first + 2:
                at, _ = place_of(n - 2)
                dq_s[at, lanes] = own(kst_s[n - 2], ds_s[n - 2]).astype(BF)
                twice = jnp.concatenate([ds_s[n - 2], ds_s[n - 2]], axis=0)
                dkv_s[at, lanes] = unstack(mm_nt(qbd_s[n - 2], twice)).astype(BF)
            if first + 1 <= n <= first + HEADS:
                softmax_back(n - 1, grads.pop(n - 1))
            yield 340
        gh_s[:, lanes] = mm(wq[...], dq_s[:, lanes])
        yield 150
        gs_s[:, lanes] = mm(wkv[...], dkv_s[:, lanes])
        yield 300
        for c in (2 * g, 2 * g + 1):
            cut = chunks[c]
            grad, hat = gh_s[:, cut] * QSCALE, n1_s[:, cut]
            ln_s[0] += grad * hat
            ln_s[1] += grad
            grad_dec[:, cut] = x1_s[:, cut] + normed_back(grad * column(0), hat, scale_one[c])
            yield 170
            grad, hat = gs_s[:, cut], n2_s[:, cut]
            ln_s[0] += grad * hat
            ln_s[1] += grad
            back = normed_back(grad * column(0), hat, scale_two[c]).astype(BF)
            for w in (0, 1):
                a = chosen[step * WIN + 2 * c + w]
                rank = ranks[0, step * WIN + 2 * c + w]
                owner = lax.bitwise_xor(lax.div(a, windows), mix)
                half = pltpu.roll(back, ((rank + w) & 1) * WTOK, 1)
                at = pl.ds(pl.multiple_of((rank >> 1) * 128, 128), 128)
                pick_s[owner, :, at] = jnp.where(
                    lane >> 6 == (rank & 1), half, pick_s[owner, :, at]
                )
            yield 250

    def add(ref, product):
        ref[0] += product[:, 0:128]
        ref[1, :, 0 : C - 128] += product[:, 128:]

    def early_sums():
        add(a2, mm_nt(gl_s[...], dm_s[...]))
        yield 1200
        a1[...] += mm_nt(du_s[...], hn_s[...])
        yield 1200
        add(ao, mm_nt(o_s[...], da_s[...]))
        yield 400

    costs = {forward: 3500, feed: 3450, backward: 4000, early_sums: 2800}

    def interleaved(parts):
        running = [[part(*args), 0, costs[part]] for part, *args in parts]
        while running:
            now = min(running, key=lambda entry: entry[1] / entry[2])
            try:
                now[1] += next(now[0])
            except StopIteration:
                running.remove(now)

    for slot in range(GROUPS + 2):
        parts = [
            (part, slot - lag)
            for lag, part in enumerate((forward, feed, backward))
            if 0 <= slot - lag < GROUPS
        ]
        if slot == GROUPS + 1:
            parts.append((early_sums,))
        interleaved(parts)
    add(aq, mm_nt(xn_s[...], dq_s[...]))
    akv[...] += mm_nt(dkv_s[...], sn_s[...])

    @pl.when(step == pl.num_programs(0) - 1)
    def _():
        offset = 0
        sums = {1: [], 3: []}
        for number, ((rows, cols), ref) in enumerate(zip(SHAPES, (aq, akv, ao, a1, a2))):
            per = rows // ROWS
            tiles = -(-cols // 128)
            source = ref
            if number in sums:
                source = stage
                for n in range(tiles):
                    turned = jnp.transpose(ref[128 * n : 128 * n + 128, :])
                    sums[number].append(turned[rows : rows + 1])
                    stage[n, 0:rows, :] = turned[0:rows]
            joined = 2 if cols % 128 else 1
            for a in range(0, per, joined):
                value = jnp.concatenate(
                    [
                        jnp.concatenate(
                            [source[n, pl.ds(b, ROWS, stride=per), :] for n in range(tiles)], axis=1
                        )[:, 0:cols]
                        for b in range(a, a + joined)
                    ],
                    axis=1,
                )
                if number == 0:
                    value = value * QSCALE
                for n in range(joined * cols // 128):
                    block_s[tile_of((offset + a * cols) // 128 + n)] = value[
                        :, 128 * n : 128 * n + 128
                    ]
            offset += per * cols
        rows = [jnp.sum(jnp.transpose(ln_s[n]), axis=0, keepdims=True) for n in range(4)]
        def last_row(ref, at):
            return jnp.concatenate(
                [ref[0, at : at + 1, :], ref[1, at : at + 1, 0 : C - 128]], axis=1
            )

        flat = jnp.concatenate(
            [
                rows[0],
                rows[1],
                last_row(aq, C) * QSCALE,
                jnp.concatenate(sums[1], axis=1)[:, C:],
                last_row(ao, C),
                rows[2],
                rows[3],
                *sums[3],
                last_row(a2, HIDDEN_SIZE),
            ],
            axis=1,
        )
        big[0] = jnp.zeros((8 * WTOK, 128), F32)
        for h in range(HEADS):
            big[0, pl.ds(h, WTOK, stride=8), :] = gds_s[h]
        hot = (iota((128, 256), 1) == place(iota((128, 256), 0) & 63)).astype(BF)
        total = sum(mm(part, hot) for part in splits(big[0]))
        big[0] = total[:, 0:128]
        big[1] = total[:, 128:256]
        result = jnp.zeros((8, 384), F32)
        for j in range(WTOK):
            row = jnp.concatenate(
                [
                    big[0, 8 * j : 8 * j + 8, :],
                    big[1, 8 * j : 8 * j + 8, :],
                    jnp.zeros((8, 128), F32),
                ],
                axis=1,
            )
            turn = (place(WTOK - 1) - place(j)) % 384
            result = result + (pltpu.roll(row, turn, 1) if turn else row)
        per = VEC // ROWS
        block_s[tile_of(VEC_TILE)] = jnp.concatenate(
            [
                jnp.concatenate([flat[:, per * k : per * k + per] for k in range(ROWS)], axis=0),
                jnp.zeros((ROWS, 128 - per), F32),
            ],
            axis=1,
        )
        count = TABLE_LANES
        block_s[tile_of(SIDE_TILE)] = jnp.concatenate(
            [
                jnp.concatenate([result[:, count * n : count * n + count] for n in range(4)], axis=0),
                jnp.zeros((ROWS, 128 - count), F32),
            ],
            axis=1,
        )
        for number in range(SIDE_TILE + 1, BLOCK[0] * BLOCK_TILES):
            block_s[tile_of(number)] = jnp.zeros((ROWS, 128), F32)
        for outer in range(OUTER):
            for inner in range(INNER):
                k = inner * OUTER + lax.bitwise_xor(my_skip, outer)
                rows = pl.ds(pl.multiple_of(k * BLOCK[0], BLOCK[0]), BLOCK[0])
                for n in range(BLOCK_TILES):
                    grad_packs[outer][inner, :, 128 * n : 128 * n + 128] = block_s[
                        n, rows, :
                    ].astype(BF)
        for n in range(skip_count):
            grad_picks[n][...] = pick_s[n]


def layer_call(skip_count, chosen, extents, here, ranks, dec, cot, bias, packs, pieces):
    tokens = dec.shape[1]
    windows = tokens // WTOK
    steps = tokens // T
    share = tokens // skip_count
    block = pl.BlockSpec((C, T), lambda i: (0, i))
    smem = pl.BlockSpec(memory_space=pltpu.SMEM)
    hbm = pl.BlockSpec(memory_space=pltpu.HBM)

    def whole(shape):
        return pl.BlockSpec(shape, lambda i: (0,) * len(shape))

    scratch = [
        ((skip_count, C, share), BF),
        ((2, 8 * WTOK, 128), F32),
        ((VEC, 128), F32),
        ((C, C), BF),
        ((C, C), BF),
        ((C, 2 * C), BF),
        ((2 * C, C), BF),
        ((C, C), BF),
        ((C, C), BF),
        ((C, HIDDEN_SIZE), BF),
        ((HIDDEN_SIZE, C), BF),
        ((HIDDEN_SIZE, C), BF),
        ((C, HIDDEN_SIZE), BF),
        ((C + 16, T), BF),
        ((C + 16, T), BF),
        ((C + 16, T), BF),
        ((C + 16, T), BF),
        ((HIDDEN_SIZE + 16, T), BF),
        ((HIDDEN_SIZE, T), BF),
        ((C, T), BF),
        ((GROUPS * HEADS, GWIN * HEAD_DIM, GROUP), BF),
        ((GROUPS * HEADS, GWIN * HEAD_DIM, WTOK), BF),
        ((GROUPS * HEADS, GWIN * HEAD_DIM, WTOK), BF),
        ((GROUPS * HEADS, WTOK, GWIN * HEAD_DIM), BF),
        ((GROUPS * HEADS, WTOK, GWIN * HEAD_DIM), BF),
        ((GROUPS * HEADS, WTOK, GROUP), F32),
        ((GROUPS * HEADS, WTOK, GROUP), BF),
        ((GROUPS * HEADS, WTOK, GROUP), BF),
        ((C, T), BF),
        ((C, T), BF),
        ((C, T), BF),
        ((T // 128, HIDDEN_SIZE, 128), F32),
        ((T // 128, HIDDEN_SIZE, 128), F32),
        ((C, T), F32),
        ((C, T), F32),
        ((C, T), BF),
        ((2 * C, T), BF),
        ((C, T), F32),
        ((C, T), F32),
        ((C, T), F32),
        ((C, T), F32),
        ((HEADS, WTOK, 128), F32),
        ((2, C + 16, 128), F32),
        ((2 * C, C + 16), F32),
        ((2, C + 16, 128), F32),
        ((HIDDEN_SIZE, C + 16), F32),
        ((2, HIDDEN_SIZE + 16, 128), F32),
        ((4, C, 128), F32),
    ]
    flops = 2 * tokens * (3 * 442368 + 12 * WTOK * C)
    return pl.pallas_call(
        functools.partial(layer_kernel, skip_count, windows, len(pieces)),
        grid=(steps,),
        in_specs=[smem, smem, smem, smem, hbm, hbm, whole(bias.shape)]
        + [pl.BlockSpec(memory_space=pl.ANY)] * (OUTER + len(pieces)),
        out_specs=[block, block, whole((ROWS, 128))]
        + [whole((C, share))] * skip_count
        + [whole((INNER, *BLOCK))] * OUTER,
        out_shape=[
            jax.ShapeDtypeStruct((C, tokens), BF),
            jax.ShapeDtypeStruct((C, tokens), F32),
            jax.ShapeDtypeStruct((ROWS, 128), jnp.int32),
        ]
        + [jax.ShapeDtypeStruct((C, share), BF)] * skip_count
        + [jax.ShapeDtypeStruct((INNER, *BLOCK), BF)] * OUTER,
        scratch_shapes=[pltpu.VMEM(shape, kind) for shape, kind in scratch]
        + [
            pltpu.VMEM((C, skip_count * tokens), BF),
            pltpu.SemaphoreType.DMA((len(pieces),)),
            pltpu.VMEM((steps, C, T), BF),
            pltpu.VMEM((steps, C, T), BF),
            pltpu.SemaphoreType.DMA((2 * steps,)),
            pltpu.VMEM((OUTER, INNER, *BLOCK), BF),
            pltpu.SemaphoreType.DMA((OUTER,)),
        ],
        compiler_params=pltpu.CompilerParams(
            dimension_semantics=("arbitrary",), vmem_limit_bytes=42 * 1024 * 1024
        ),
        cost_estimate=pl.CostEstimate(
            flops=flops, bytes_accessed=8_000_000, transcendentals=tokens * 1200
        ),
        name="layer",
    )(
        kept(chosen),
        extents,
        here,
        ranks,
        kept(dec),
        kept(cot),
        bias,
        *packs,
        kept(pieces[0]),
        *[pltpu.with_memory_space_constraint(piece, pltpu.VMEM) for piece in pieces[1:]],
    )


def pack_kernel(mat, vec, chosen, out):
    flat = jnp.concatenate(
        [
            mat[...],
            vec[...],
            jnp.zeros((1, 128 - vec.shape[1]), F32),
            chosen[...].astype(F32),
            jnp.zeros((1, BLOCK[0] * BLOCK[1] - 128 * SIDE_TILE - chosen.shape[1]), F32),
        ],
        axis=1,
    )
    block = jnp.concatenate(
        [flat[:, BLOCK[1] * j : BLOCK[1] * (j + 1)] for j in range(BLOCK[0])], axis=0
    ).astype(BF)
    for n in range(INNER):
        out[n] = block


def skip_sum_kernel(*refs):
    blocks, out = refs[:-1], refs[-1]
    for n in range(INNER):
        out[n] = sum(block[n].astype(F32) for block in blocks).astype(BF)


def split_kernel(here, *refs):
    blocks, (keep, send) = refs[:-2], refs[-2:]
    for n in range(INNER // 2):
        for odd, out in enumerate((keep, send)):
            at = lax.bitwise_xor(here[3], 2 * n + odd)
            out[n] = sum(block[at].astype(F32) for block in blocks).astype(out.dtype)


def halve_kernel(kept, came, keep, send):
    for n in range(kept.shape[0] // 2):
        keep[n] = kept[2 * n] + came[2 * n].astype(F32)
        send[n] = (kept[2 * n + 1] + came[2 * n + 1].astype(F32)).astype(BF)


def slab_sum_kernel(kept, came, mat, vec, tail):
    total = kept[0] + came[0].astype(F32)
    squares = jnp.sum(jnp.sum(total * total, axis=1, keepdims=True), axis=0, keepdims=True)
    flat = jnp.concatenate([total[j : j + 1, :] for j in range(BLOCK[0])], axis=1)
    mat[...] = flat[:, 0 : mat.shape[1]]
    vec[...] = flat[:, 128 * VEC_TILE : 128 * VEC_TILE + vec.shape[1]]
    side = flat[:, 128 * SIDE_TILE : 128 * SIDE_TILE + 128]
    side = jnp.where(iota((1, 128), 1) == TABLE_LANES, squares, side)
    tail[...] = jnp.broadcast_to(side, tail.shape)


def return_kernel(windows, row, here, everyone, after, *refs):
    del after
    received, (out, gathered, source) = refs[:-3], refs[-3:]
    skip_count = len(received)
    per = windows // skip_count
    mix = here[1]
    for d in range(skip_count):
        gathered[d] = received[d][...]
        s = lax.bitwise_xor(mix, d)

        def note(w, rank):
            a = everyone[here[3] * row + s, w]
            mine = lax.div(a, windows) == here[2]

            @pl.when(mine)
            def _():
                source[lax.rem(a, windows)] = d * per + rank

            return rank + mine.astype(jnp.int32)

        lax.fori_loop(0, windows, note, 0)
    left = iota((1, 128), 1) < WTOK
    for n in range(windows // 2):
        halves = []
        for w in (0, 1):
            place_in = source[2 * n + w]
            d, rank = lax.div(place_in, per), lax.rem(place_in, per)
            lanes = pl.ds(pl.multiple_of((rank >> 1) * 128, 128), 128)
            block = gathered[d, :, lanes].astype(F32)
            halves.append(pltpu.roll(block, ((rank + w) & 1) * WTOK, 1))
        out[:, 128 * n : 128 * n + 128] = jnp.where(left, halves[0], halves[1])


VMEM = pl.BlockSpec(memory_space=pltpu.VMEM)
SMEM = pl.BlockSpec(memory_space=pltpu.SMEM)


def small_call(kernel, name, in_specs, outs, operands, scratch=(), moved=1_000_000):
    return pl.pallas_call(
        kernel,
        in_specs=in_specs,
        out_specs=[VMEM] * len(outs),
        out_shape=outs,
        scratch_shapes=scratch,
        compiler_params=pltpu.CompilerParams(vmem_limit_bytes=16 * 1024 * 1024),
        cost_estimate=pl.CostEstimate(flops=moved, bytes_accessed=moved, transcendentals=0),
        name=name,
    )(*operands)


def repack(packed, count):
    pieces, offset = [], 0
    for rows, cols in SHAPES:
        width = rows * cols // packed.shape[0]
        pieces.append(packed[:, offset : offset + width].reshape(count, -1))
        offset += width
    return jnp.concatenate(pieces, axis=1)


def padded(value, width):
    return jnp.pad(value, ((0, 0), (0, width - value.shape[1])))


def adamw_update(master, first, second, average, grad, factor, decay):
    clipped = grad * factor
    first_new = BETA_ONE * first + (1.0 - BETA_ONE) * clipped
    second_new = BETA_TWO * second + (1.0 - BETA_TWO) * clipped * clipped
    first_hat = first_new / (1.0 - BETA_ONE**STEP)
    second_hat = second_new / (1.0 - BETA_TWO**STEP)
    master_new = master - RATE * (first_hat / (jnp.sqrt(second_hat) + ADAM_EPS) + decay * master)
    average_new = EMA_RATE * average + (1.0 - EMA_RATE) * master_new
    return (clipped, master_new, first_new, second_new, average_new, master_new.astype(BF))


def update_kernel(mat_share, vec_share, tail, *refs):
    mats, vecs, tables = refs[0:4], refs[4:8], refs[8:12]
    norm_out, outs = refs[12], refs[13:]
    squares = jnp.sum(tail[:, TABLE_LANES : TABLE_LANES + 1], axis=0, keepdims=True)
    norm = jnp.sqrt(squares)
    norm_out[...] = norm
    factor = CLIP / jnp.maximum(norm, CLIP)
    table = jnp.concatenate([tail[8 * q : 8 * q + 8, 0:TABLE_LANES] for q in range(4)], axis=1)
    work = (
        (mats, mat_share[...], MATRIX_DECAY),
        (vecs, vec_share[...], 0.0),
        (tables, table[0:HEADS, 0:REL], 0.0),
    )
    for n, (group, grad, decay) in enumerate(work):
        results = adamw_update(*[ref[...] for ref in group], grad, factor, decay)
        for ref, value in zip(outs[6 * n : 6 * n + 6], results):
            ref[...] = value


def on_device(
    decoder_tokens,
    skip_tokens,
    cotangent,
    extents,
    assignment,
    mat_master,
    mat_first,
    mat_second,
    mat_average,
    vec_master,
    vec_first,
    vec_second,
    vec_average,
    table_master,
    table_first,
    table_second,
    table_average,
):
    skip_count = lax.axis_size("skip")
    slab_count = lax.axis_size("slab")
    device_count = skip_count * slab_count
    windows = assignment.shape[1]
    mat_width, vec_width = mat_master.shape[1], vec_master.shape[1]
    me = lax.axis_index("skip")
    plain = (skip_count, slab_count) == (OUTER, INNER)

    def swap(value, axis, distance):
        count = lax.axis_size(axis)
        return lax.ppermute(value, axis, [(n, n ^ distance) for n in range(count)])

    if plain:
        here = jnp.stack([me, me, me, lax.axis_index("slab")])
        (block,) = small_call(
            pack_kernel,
            "pack",
            [VMEM] * 3,
            [jax.ShapeDtypeStruct((INNER, *BLOCK), BF)],
            (kept(mat_master), kept(vec_master), kept(assignment)),
            moved=100_000,
        )
        own = lax.all_to_all(block, "slab", split_axis=0, concat_axis=0)
        across = swap(skip_tokens, "skip", 2)
        near = swap(skip_tokens, "skip", 1)
        packs_across = swap(own, "skip", 2)
        packs_across, across = lax.optimization_barrier((packs_across, across))
        packs = [own, swap(own, "skip", 1), packs_across, swap(packs_across, "skip", 1)]
        pieces = [skip_tokens, near, across, swap(across, "skip", 1)]
    else:
        zero = jnp.zeros_like(me)
        here = jnp.stack([zero, zero, me, zero])
        low = jnp.concatenate([mat_master, vec_master], axis=1).astype(BF)
        low = lax.all_gather(low, ("slab", "skip"), axis=0, tiled=True)
        vec = padded(low[:, mat_width:].reshape(ROWS, -1), 128)
        low = padded(
            jnp.concatenate([repack(low, ROWS), vec], axis=1), BLOCK[0] * BLOCK[1]
        ).reshape(INNER, OUTER, *BLOCK)
        packs = [low[:, n] for n in range(OUTER)]
        pieces = [lax.all_gather(skip_tokens, "skip", axis=0, tiled=True)]

    bias, ranks = pl.pallas_call(
        functools.partial(early_kernel, skip_count, windows),
        in_specs=[SMEM, VMEM, pl.BlockSpec(memory_space=pl.ANY)],
        out_specs=[VMEM, VMEM],
        out_shape=[
            jax.ShapeDtypeStruct((HEADS, WTOK, 128), F32),
            jax.ShapeDtypeStruct((1, 128), jnp.int32),
        ],
        scratch_shapes=[
            pltpu.VMEM((8, 384), F32),
            pltpu.VMEM((2, 8 * WTOK, 128), F32),
            pltpu.SMEM((skip_count,), jnp.int32),
        ],
        compiler_params=pltpu.CompilerParams(vmem_limit_bytes=16 * 1024 * 1024),
        cost_estimate=pl.CostEstimate(flops=100_000_000, bytes_accessed=1_000_000, transcendentals=0),
        name="early",
    )(kept(assignment[0]), kept(table_master.T), packs[0])
    layer_out, grad_decoder, everyone, *grads = layer_call(
        skip_count,
        assignment[0],
        extents,
        here,
        ranks,
        decoder_tokens.T,
        cotangent.T,
        bias,
        packs,
        [piece.T for piece in pieces],
    )
    grad_picks, grad_packs = grads[:skip_count], grads[skip_count:]

    def returned_call(here, everyone, after, received):
        (grad_skip,) = small_call(
            functools.partial(return_kernel, windows, OUTER),
            "returned",
            [SMEM, SMEM] + [VMEM] * (1 + skip_count),
            [jax.ShapeDtypeStruct((C, windows * WTOK), F32)],
            (here, everyone, after, *received),
            [
                pltpu.VMEM((skip_count, *received[0].shape), BF),
                pltpu.SMEM((windows,), jnp.int32),
            ],
            3_000_000,
        )
        return grad_skip

    shares = [
        jax.ShapeDtypeStruct((1, mat_width), F32),
        jax.ShapeDtypeStruct((1, vec_width), F32),
    ]
    if plain:
        far = swap(grad_packs[3], "skip", 1)
        near = swap(grad_packs[1], "skip", 1)
        (far,) = small_call(
            skip_sum_kernel,
            "core_sum",
            [VMEM] * 2,
            [jax.ShapeDtypeStruct((INNER, *BLOCK), BF)],
            (grad_packs[2], far),
        )
        keep, send = small_call(
            split_kernel,
            "skip_sum",
            [SMEM] + [VMEM] * 3,
            [
                jax.ShapeDtypeStruct((INNER // 2, *BLOCK), F32),
                jax.ShapeDtypeStruct((INNER // 2, *BLOCK), BF),
            ],
            (here, grad_packs[0], near, swap(far, "skip", 2)),
        )
        send, grad_picks = lax.optimization_barrier((send, grad_picks))
        received = [grad_picks[0]] + [swap(grad_picks[d], "skip", d) for d in range(1, OUTER)]
        for distance in (1, 2):
            half = keep.shape[0] // 2
            keep, send = small_call(
                halve_kernel,
                "slab_half",
                [VMEM] * 2,
                [
                    jax.ShapeDtypeStruct((half, *BLOCK), F32),
                    jax.ShapeDtypeStruct((half, *BLOCK), BF),
                ],
                (keep, swap(send, "slab", distance)),
                moved=300_000,
            )
        came, received = lax.optimization_barrier((swap(send, "slab", 4), received))
        mat_share, vec_share, tail = small_call(
            slab_sum_kernel,
            "slab_sum",
            [VMEM] * 2,
            shares + [jax.ShapeDtypeStruct((ROWS, 128), F32)],
            (keep, came),
            moved=300_000,
        )
        grad_skip = returned_call(here, everyone, vec_share, received)
        tail = lax.all_to_all(tail, ("slab", "skip"), split_axis=0, concat_axis=0, tiled=True)
        tail, grad_skip = lax.optimization_barrier((tail, grad_skip))
    else:
        received = list(
            lax.all_to_all(jnp.stack(grad_picks), "skip", split_axis=0, concat_axis=0)
        )
        everyone = lax.all_gather(assignment, "skip", axis=0, tiled=True)
        rows = jnp.stack(grad_packs, axis=1).reshape(ROWS, -1)
        start, side = 128 * VEC_TILE, 128 * SIDE_TILE
        rows = jnp.concatenate(
            [
                repack(rows, device_count),
                rows[:, start : start + VEC // ROWS].reshape(device_count, -1),
                rows[:, side : side + TABLE_LANES].reshape(device_count, -1),
            ],
            axis=1,
        )
        share = lax.psum_scatter(
            rows.astype(F32), ("slab", "skip"), scatter_dimension=0, tiled=True
        )
        mat_share = share[:, :mat_width]
        vec_share = share[:, mat_width : mat_width + vec_width]
        table = lax.all_gather(
            share[:, mat_width + vec_width :], ("slab", "skip"), axis=0, tiled=True
        )
        squares = lax.psum(jnp.sum(share * share), ("slab", "skip")) * (1.0 / ROWS)
        tail = jnp.concatenate(
            [table.reshape(ROWS, TABLE_LANES), jnp.full((ROWS, 128 - TABLE_LANES), squares)],
            axis=1,
        )

    if not plain:
        grad_skip = returned_call(here, everyone, vec_share, received)
    groups = (
        (mat_master, mat_first, mat_second, mat_average),
        (vec_master, vec_first, vec_second, vec_average),
        (table_master.T, table_first.T, table_second.T, table_average.T),
    )
    kinds = [jax.ShapeDtypeStruct((1, 1), F32)]
    for group in groups:
        kinds += [jax.ShapeDtypeStruct(group[0].shape, F32)] * 5
        kinds += [jax.ShapeDtypeStruct(group[0].shape, BF)]
    outs = small_call(
        update_kernel,
        "update",
        [VMEM] * 15,
        kinds,
        (mat_share, vec_share, tail, *groups[0], *groups[1], *groups[2]),
    )
    return (
        layer_out.T,
        grad_decoder.T,
        grad_skip.T,
        outs[0].reshape(()),
        *outs[1:13],
        *[value.T for value in outs[13:]],
    )


def solution(mesh):
    split = P(("slab", "skip"), None)
    return jax.shard_map(
        on_device,
        mesh=mesh,
        in_specs=(split, split, split, P("slab"), P("slab", "skip"))
        + (split,) * 8
        + (P(),) * 4,
        out_specs=(split, split, split, P()) + (split,) * 12 + (P(),) * 6,
        check_vma=False,
    )
```

```python
import functools
import math
import jax
import jax.numpy as jnp
from jax import lax
from jax.experimental import pallas as pl
from jax.experimental.pallas import tpu as pltpu
from jax.sharding import PartitionSpec as P

C = 192
HEADS = 6
HEAD_DIM = 32
HIDDEN_SIZE = 768
WS = 4
DEPTH = 16
STEP = 10
WTOK = 64
REL = 343

EPS = 1e-05
MASK_FILL = -1000000000.0
CLIP = 1.0
BETA_ONE = 0.9
BETA_TWO = 0.999
RATE = 0.3
MATRIX_DECAY = 0.05
ADAM_EPS = 1e-08
EMA_RATE = 0.9

BF = jnp.bfloat16
F32 = jnp.float32
GROUP = 256
GWIN = GROUP // WTOK
T = 1024
GROUPS = T // GROUP
WIN = T // WTOK
QSCALE = HEAD_DIM ** (-0.5)
SHAPES = ((C, C), (C, 2 * C), (C, C), (C, HIDDEN_SIZE), (HIDDEN_SIZE, C))
VLEN = (C, C, C, C, C, C, C, HIDDEN_SIZE, C)
VOFF = tuple(sum(VLEN[:n]) for n in range(len(VLEN)))
VEC = sum(VLEN)
MAT = sum(r * c for r, c in SHAPES)
ROWS = 32
OUTER = 4
INNER = ROWS // OUTER
BLOCK = (16, 896)
BLOCK_TILES = BLOCK[1] // 128
VEC_TILE = MAT // ROWS // 128
SIDE_TILE = VEC_TILE + 1
TABLE_LANES = 8 * 384 // ROWS


def mm(a, b):
    return jnp.dot(a, b, preferred_element_type=F32)


def mm_nt(a, b):
    return lax.dot_general(a, b, (((1,), (1,)), ((), ())), preferred_element_type=F32)


def iota(shape, dim):
    return lax.broadcasted_iota(jnp.int32, shape, dim)


def kept(value):
    return pltpu.with_memory_space_constraint(value, pltpu.HBM)


def both(column):
    return jnp.concatenate([column, column], axis=1)


def place(slot):
    span = 2 * WS - 1
    return ((slot >> 4) * span + ((slot >> 2) & 3)) * span + (slot & 3)


def splits(value):
    high = value.astype(BF)
    rest = value - high.astype(F32)
    middle = rest.astype(BF)
    return high, middle, (rest - middle.astype(F32)).astype(BF)


def normed(value):
    center = value - jnp.sum(value, axis=0, keepdims=True) * (1.0 / C)
    scale = lax.rsqrt(jnp.sum(center * center, axis=0, keepdims=True) * (1.0 / C) + EPS)
    return center * scale, scale


def normed_back(grad_hat, hat, scale):
    mean_grad = jnp.sum(grad_hat, axis=0, keepdims=True) * (1.0 / C)
    mean_both = jnp.sum(grad_hat * hat, axis=0, keepdims=True) * (1.0 / C)
    return scale * (grad_hat - mean_grad - hat * mean_both)


def fold(value):
    return sum(value[:, n : n + 128] for n in range(0, value.shape[1], 128))


def gelu_parts(u):
    t = pl.reciprocal(1.0 + (0.3275911 * 0.5**0.5) * jnp.abs(u), approx=True)
    bell = jnp.exp2((-0.5 * math.log2(math.e)) * (u * u))
    series = 0.5 * 1.061405429
    for factor in (-1.453152027, 1.421413741, -0.284496736, 0.254829592):
        series = series * t + 0.5 * factor
    tail = series * t * bell
    cdf = jnp.where(u >= 0.0, 1.0 - tail, tail)
    return u * cdf, cdf + ((0.5 / math.pi) ** 0.5 * u) * bell


def early_kernel(skip_count, windows, chosen, table, after, bias_s, ranks, tab_s, big, count_s):
    del after
    tab_s[...] = jnp.zeros_like(tab_s)
    tab_s[0:HEADS, 0:REL] = table[...]
    hot = (iota((256, 128), 0) == place(iota((256, 128), 1) & 63)).astype(BF)
    total = None
    for part in splits(tab_s[...]):
        part = part.astype(F32)
        for j in range(WTOK):
            turn = (place(j) - place(WTOK - 1)) % 384
            rolled = pltpu.roll(part, turn, 1) if turn else part
            big[0, 8 * j : 8 * j + 8, :] = rolled[:, 0:128]
            big[1, 8 * j : 8 * j + 8, :] = rolled[:, 128:256]
        product = mm(big[0].astype(BF), hot[0:128]) + mm(big[1].astype(BF), hot[128:256])
        total = product if total is None else total + product
    big[0] = total
    for h in range(HEADS):
        bias_s[h] = big[0, pl.ds(h, WTOK, stride=8), :]
    for e in range(skip_count):
        count_s[e] = 0

    def note(w, rank_row):
        owner = lax.div(chosen[w], windows)
        rank = count_s[owner]
        count_s[owner] = rank + 1
        return jnp.where(iota((1, 128), 1) == w, rank, rank_row)

    ranks[...] = lax.fori_loop(0, windows, note, jnp.zeros((1, 128), jnp.int32))


def layer_kernel(
    skip_count,
    windows,
    piece_count,
    chosen,
    extents,
    here,
    ranks,
    dec_all,
    cot_all,
    bias_s,
    *refs,
):
    step = pl.program_id(0)
    packs, refs = refs[:OUTER], refs[OUTER:]
    pieces, refs = refs[:piece_count], refs[piece_count:]
    layer_out, grad_dec, everyone, *refs = refs
    grad_picks, refs = refs[:skip_count], refs[skip_count:]
    grad_packs, refs = refs[:OUTER], refs[OUTER:]
    (
        pick_s,
        big,
        vcol,
        wq,
        wqt,
        wkv,
        wkvt,
        wo,
        wot,
        w1,
        w1t,
        w2,
        w2t,
        xn_s,
        sn_s,
        hn_s,
        o_s,
        gl_s,
        du_s,
        q_s,
        qbd_s,
        kst_s,
        vst_s,
        kcat_s,
        vcat_s,
        pf_s,
        pb_s,
        ds_s,
        da_s,
        do_s,
        dm_s,
        u_s,
        ga_s,
        gh_s,
        gs_s,
        dq_s,
        dkv_s,
        n1_s,
        n2_s,
        n3_s,
        x1_s,
        gds_s,
        aq,
        akv,
        ao,
        a1,
        a2,
        ln_s,
        slab,
        slab_sem,
        dec_s,
        cot_s,
        token_sem,
        pack_s,
        pack_sem,
    ) = refs
    dec, cot = dec_s.at[step], cot_s.at[step]
    stage, block_s = u_s, ga_s
    my_skip, mix = here[0], here[1]
    lane = iota((1, 128), 1)
    left = lane < WTOK

    def tile_of(number):
        j, n = divmod(number, BLOCK_TILES)
        return n, pl.ds(j, ROWS, stride=BLOCK[0]), slice(None)


    def token_copies(n):
        lanes = slice(T * n, T * n + T)
        return [
            pltpu.make_async_copy(dec_all.at[:, lanes], dec_s.at[n], token_sem.at[2 * n]),
            pltpu.make_async_copy(cot_all.at[:, lanes], cot_s.at[n], token_sem.at[2 * n + 1]),
        ]

    for n in range(1, windows // WIN):

        @pl.when(step == n)
        def _(n=n):
            for copy in token_copies(n):
                copy.wait()

    @pl.when(step == 0)
    def _():
        copies = token_copies(0) + [
            pltpu.make_async_copy(
                piece, slab.at[:, n * piece.shape[1] : (n + 1) * piece.shape[1]], slab_sem.at[n]
            )
            for n, piece in enumerate(pieces)
        ]
        pack_copies = [
            pltpu.make_async_copy(packs[n], pack_s.at[n], pack_sem.at[n]) for n in range(OUTER)
        ]
        for copy in pack_copies + copies + [copy for n in range(1, windows // WIN) for copy in token_copies(n)]:
            copy.start()
        for ref in (gds_s, aq, akv, ao, a1, a2, ln_s):
            ref[...] = jnp.zeros_like(ref)
        for ref, rows in ((xn_s, C), (sn_s, C), (hn_s, C), (o_s, C), (gl_s, HIDDEN_SIZE)):
            ref[rows : rows + 16, :] = jnp.ones((16, T), BF)
        for copy in pack_copies:
            copy.wait()
        for outer in range(OUTER):
            for inner in range(INNER):
                k = inner * OUTER + lax.bitwise_xor(my_skip, outer)
                rows = pl.ds(pl.multiple_of(k * BLOCK[0], BLOCK[0]), BLOCK[0])
                for n in range(BLOCK_TILES):
                    block_s[n, rows, :] = pack_s[outer, inner, :, 128 * n : 128 * n + 128].astype(
                        F32
                    )
        offset = 0
        for (rows, cols), plain, turned in zip(
            SHAPES, (wq, wkv, wo, w1, w2), (wqt, wkvt, wot, w1t, w2t)
        ):
            per = rows // ROWS
            tiles = -(-cols // 128)
            for a in range(per):
                first, shift = divmod(offset + a * cols, 128)
                for n in range(tiles):
                    piece = block_s[tile_of(first + n)]
                    if shift and n + 1 < tiles:
                        after = block_s[tile_of(first + n + 1)]
                        piece = jnp.concatenate([piece[:, shift:], after[:, :shift]], axis=1)
                    elif shift:
                        piece = pltpu.roll(piece, 128 - shift, 1)
                    stage[n, pl.ds(a, ROWS, stride=per), :] = piece
            for n in range(tiles):
                width = min(128, cols - 128 * n)
                value = stage[n, 0:rows, :].astype(BF)
                plain[:, 128 * n : 128 * n + width] = value[:, 0:width]
                turned[128 * n : 128 * n + width, :] = jnp.transpose(value)[0:width]
            offset += per * cols
        side = block_s[tile_of(VEC_TILE)]
        per = VEC // ROWS
        vec = jnp.concatenate([side[k : k + 1, 0:per] for k in range(ROWS)], axis=1)
        vcol[...] = jnp.transpose(jnp.broadcast_to(vec, (128, VEC)))
        side = block_s[tile_of(SIDE_TILE)]
        everyone[...] = side.astype(jnp.int32)
        for copy in copies:
            copy.wait()

    def column(number, first=0, last=None):
        start = VOFF[number]
        return vcol[start + first : start + (VLEN[number] if last is None else last), :]

    chunks = [slice(128 * c, 128 * c + 128) for c in range(T // 128)]
    tiles = [slice(GROUP * g, GROUP * g + GROUP) for g in range(GROUPS)]
    layers, valid = [], []
    for c in range(len(chunks)):
        deep = [
            jnp.clip(extents[0] - WS * (chosen[step * WIN + 2 * c + w] & 3), 0, WS) for w in (0, 1)
        ]
        layers.append(jnp.where(left, deep[0], deep[1]))
        valid.append(jnp.where((lane & 63) >> 4 < layers[c], 1.0, 0.0))

    scale_one, scale_two, scale_three = {}, {}, {}

    def stacks(rows, g, stack_ref, cat_ref):
        turned = pltpu.roll(rows, WTOK, 1)
        first, second = rows[:, 0:128], rows[:, 128:256]
        mixed, middle = turned[:, 0:128], turned[:, 128:256]
        at_left = (first, middle, second, mixed)
        at_right = (mixed, first, middle, second)
        for h in range(0, HEADS, 2):
            n = g * HEADS + h
            at = slice(HEAD_DIM * h, HEAD_DIM * h + HEAD_DIM)
            after = slice(HEAD_DIM * h + HEAD_DIM, HEAD_DIM * h + 2 * HEAD_DIM)
            pieces = []
            for w in range(GWIN):
                to = slice(HEAD_DIM * w, HEAD_DIM * w + HEAD_DIM)
                stack_ref[n, to, :] = at_left[w][at, 0:WTOK]
                stack_ref[n + 1, to, :] = at_left[w][after, 0:WTOK]
                pieces.append(jnp.where(left, at_left[w][at], at_right[w][after]))
            pair = jnp.transpose(jnp.concatenate(pieces, axis=0))
            cat_ref[n] = pair[0:WTOK]
            cat_ref[n + 1] = pair[WTOK:]

    window_mask = [
        (iota((HEAD_DIM, GROUP), 1) >> 6 == w).astype(F32).astype(BF) for w in range(GWIN)
    ]

    def spread(rows):
        return jnp.concatenate([rows * mask for mask in window_mask], axis=0)

    def own(stacked, probs):
        parts = []
        for n in range(GWIN // 2):
            cut = mm(
                stacked[2 * HEAD_DIM * n : 2 * HEAD_DIM * (n + 1)],
                probs[:, 128 * n : 128 * n + 128],
            )
            parts.append(jnp.where(left, cut[0:HEAD_DIM], cut[HEAD_DIM:]))
        return jnp.concatenate(parts, axis=1)

    def unstack(product):
        parts = []
        for n in range(GWIN // 2):
            cut = product[2 * HEAD_DIM * n : 2 * HEAD_DIM * (n + 1)]
            parts.append(jnp.where(left, cut[0:HEAD_DIM], cut[HEAD_DIM:]))
        return jnp.concatenate(parts, axis=1)

    def filled(g):
        return jnp.concatenate(
            [
                jnp.concatenate(
                    [
                        jnp.broadcast_to(jnp.where(layers[c] > d, 0.0, MASK_FILL), (WS * WS, 128))
                        for d in range(WS)
                    ],
                    axis=0,
                )
                for c in (2 * g, 2 * g + 1)
            ],
            axis=1,
        )

    def place_of(n):
        g, h = divmod(n, HEADS)
        return slice(HEAD_DIM * h, HEAD_DIM * h + HEAD_DIM), tiles[g]

    def softmax(n, scores, fill):
        scores = scores + both(bias_s[n % HEADS]) + fill
        powers = jnp.exp(scores - jnp.max(scores, axis=0, keepdims=True))
        probs = powers * pl.reciprocal(jnp.sum(powers, axis=0, keepdims=True), approx=True)
        pf_s[n] = probs
        pb_s[n] = probs.astype(BF)

    def softmax_back(n, grad_probs):
        probs = pf_s[n]
        grad_scores = (
            probs * (grad_probs - jnp.sum(probs * grad_probs, axis=0, keepdims=True))
        ).astype(BF)
        gds_s[n % HEADS] += fold(grad_scores.astype(F32))
        ds_s[n] = grad_scores

    def forward(g):
        lanes = tiles[g]
        for c in (2 * g, 2 * g + 1):
            cut = chunks[c]
            hat, scale_one[c] = normed(dec[:, cut].astype(F32))
            n1_s[:, cut] = hat
            xn_s[0:C, cut] = (hat * column(0) + column(1)).astype(BF)
            yield 130
            halves = []
            for w in (0, 1):
                a = chosen[step * WIN + 2 * c + w]
                at = lax.bitwise_xor(a, mix * windows) >> 1
                part = slab[:, pl.ds(pl.multiple_of(at * 128, 128), 128)]
                halves.append(pltpu.roll(part, ((a + w) & 1) * WTOK, 1))
            hat, scale_two[c] = normed(jnp.where(left, halves[0], halves[1]).astype(F32))
            n2_s[:, cut] = hat
            sn_s[0:C, cut] = (hat * column(0) + column(1)).astype(BF)
            yield 160
        query = mm(wqt[...], xn_s[0:C, lanes])
        pair = mm(wkvt[...], sn_s[0:C, lanes])
        q_s[:, lanes] = ((query + both(column(2))) * QSCALE).astype(BF)
        for c in (2 * g, 2 * g + 1):
            dm_s[:, chunks[c]] = (cot[:, chunks[c]].astype(F32) * valid[c]).astype(BF)
        yield 250
        first = g * HEADS
        for n in range(first, first + HEADS):
            qbd_s[n] = spread(q_s[place_of(n)])
        stacks(pair[0:C].astype(BF), g, kst_s, kcat_s)
        yield 250
        stacks((pair[C:] + both(column(3))).astype(BF), g, vst_s, vcat_s)
        yield 250
        fill = filled(g)
        scores = {}
        for n in range(first, first + HEADS + 2):
            if n < first + HEADS:
                scores[n] = mm(kcat_s[n], qbd_s[n])
            if n >= first + 2:
                o_s[place_of(n - 2)] = own(vst_s[n - 2], pb_s[n - 2]).astype(BF)
            if first + 1 <= n <= first + HEADS:
                softmax(n - 1, scores.pop(n - 1), fill)
            yield 180
        product = mm(w2[...], dm_s[:, lanes])
        ga_s[2 * g] = product[:, 0:128]
        ga_s[2 * g + 1] = product[:, 128:256]
        yield 300
        x1_s[:, lanes] = mm(wot[...], o_s[0:C, lanes])
        yield 150
        for c in (2 * g, 2 * g + 1):
            cut = chunks[c]
            middle = dec[:, cut].astype(F32) + x1_s[:, cut] + column(4)
            x1_s[:, cut] = middle
            hat, scale_three[c] = normed(middle)
            n3_s[:, cut] = hat
            hn_s[0:C, cut] = (hat * column(5) + column(6)).astype(BF)
            yield 150

    def feed(g):
        lanes = tiles[g]
        product = mm(w1t[...], hn_s[0:C, lanes])
        u_s[2 * g] = product[:, 0:128]
        u_s[2 * g + 1] = product[:, 128:256]
        yield 300
        piece = 32
        for start in range(0, HIDDEN_SIZE, piece):
            rows = slice(start, start + piece)
            for c in (2 * g, 2 * g + 1):
                active, slope = gelu_parts(u_s[c, rows, :] + column(7, start, start + piece))
                gl_s[rows, chunks[c]] = active.astype(BF)
                du_s[rows, chunks[c]] = (ga_s[c, rows, :] * slope).astype(BF)
            yield 35 * piece // 16
        gh_s[:, lanes] = mm(w1[...], du_s[:, lanes])
        yield 450
        mlp = mm(w2t[...], gl_s[0:HIDDEN_SIZE, lanes]) + both(column(8))
        layer_out[:, lanes] = (
            jnp.concatenate([valid[2 * g], valid[2 * g + 1]], axis=1) * (x1_s[:, lanes] + mlp)
        ).astype(BF)
        yield 500
        for c in (2 * g, 2 * g + 1):
            cut = chunks[c]
            grad, hat = gh_s[:, cut], n3_s[:, cut]
            ln_s[2] += grad * hat
            ln_s[3] += grad
            back = normed_back(grad * column(5), hat, scale_three[c])
            grad_middle = cot[:, cut].astype(F32) * valid[c] + back
            x1_s[:, cut] = grad_middle
            da_s[:, cut] = grad_middle.astype(BF)
            yield 170
        do_s[:, lanes] = mm(wo[...], da_s[:, lanes]).astype(BF)
        yield 150

    def backward(g):
        lanes = tiles[g]
        first = g * HEADS
        spreads, grads = {}, {}
        for n in range(first, first + HEADS + 2):
            if n < first + HEADS:
                at, _ = place_of(n)
                spreads[n] = spread(do_s[at, lanes])
                grads[n] = mm(vcat_s[n], spreads[n])
                twice = jnp.concatenate([pb_s[n], pb_s[n]], axis=0)
                dkv_s[at.start + C : at.stop + C, lanes] = unstack(
                    mm_nt(spreads.pop(n), twice)
                ).astype(BF)
            if n >= first + 2:
                at, _ = place_of(n - 2)
                dq_s[at, lanes] = own(kst_s[n - 2], ds_s[n - 2]).astype(BF)
                twice = jnp.concatenate([ds_s[n - 2], ds_s[n - 2]], axis=0)
                dkv_s[at, lanes] = unstack(mm_nt(qbd_s[n - 2], twice)).astype(BF)
            if first + 1 <= n <= first + HEADS:
                softmax_back(n - 1, grads.pop(n - 1))
            yield 340
        gh_s[:, lanes] = mm(wq[...], dq_s[:, lanes])
        yield 150
        gs_s[:, lanes] = mm(wkv[...], dkv_s[:, lanes])
        yield 300
        for c in (2 * g, 2 * g + 1):
            cut = chunks[c]
            grad, hat = gh_s[:, cut] * QSCALE, n1_s[:, cut]
            ln_s[0] += grad * hat
            ln_s[1] += grad
            grad_dec[:, cut] = x1_s[:, cut] + normed_back(grad * column(0), hat, scale_one[c])
            yield 170
            grad, hat = gs_s[:, cut], n2_s[:, cut]
            ln_s[0] += grad * hat
            ln_s[1] += grad
            back = normed_back(grad * column(0), hat, scale_two[c]).astype(BF)
            for w in (0, 1):
                a = chosen[step * WIN + 2 * c + w]
                rank = ranks[0, step * WIN + 2 * c + w]
                owner = lax.bitwise_xor(lax.div(a, windows), mix)
                half = pltpu.roll(back, ((rank + w) & 1) * WTOK, 1)
                at = pl.ds(pl.multiple_of((rank >> 1) * 128, 128), 128)
                pick_s[owner, :, at] = jnp.where(
                    lane >> 6 == (rank & 1), half, pick_s[owner, :, at]
                )
            yield 250

    def add(ref, product):
        ref[0] += product[:, 0:128]
        ref[1, :, 0 : C - 128] += product[:, 128:]

    def early_sums():
        add(a2, mm_nt(gl_s[...], dm_s[...]))
        yield 1200
        a1[...] += mm_nt(du_s[...], hn_s[...])
        yield 1200
        add(ao, mm_nt(o_s[...], da_s[...]))
        yield 400

    costs = {forward: 3500, feed: 3450, backward: 4000, early_sums: 2800}

    def interleaved(parts):
        running = [[part(*args), 0, costs[part]] for part, *args in parts]
        while running:
            now = min(running, key=lambda entry: entry[1] / entry[2])
            try:
                now[1] += next(now[0])
            except StopIteration:
                running.remove(now)

    for slot in range(GROUPS + 2):
        parts = [
            (part, slot - lag)
            for lag, part in enumerate((forward, feed, backward))
            if 0 <= slot - lag < GROUPS
        ]
        if slot == GROUPS + 1:
            parts.append((early_sums,))
        interleaved(parts)
    add(aq, mm_nt(xn_s[...], dq_s[...]))
    akv[...] += mm_nt(dkv_s[...], sn_s[...])

    @pl.when(step == pl.num_programs(0) - 1)
    def _():
        offset = 0
        sums = {1: [], 3: []}
        for number, ((rows, cols), ref) in enumerate(zip(SHAPES, (aq, akv, ao, a1, a2))):
            per = rows // ROWS
            tiles = -(-cols // 128)
            source = ref
            if number in sums:
                source = stage
                for n in range(tiles):
                    turned = jnp.transpose(ref[128 * n : 128 * n + 128, :])
                    sums[number].append(turned[rows : rows + 1])
                    stage[n, 0:rows, :] = turned[0:rows]
            joined = 2 if cols % 128 else 1
            for a in range(0, per, joined):
                value = jnp.concatenate(
                    [
                        jnp.concatenate(
                            [source[n, pl.ds(b, ROWS, stride=per), :] for n in range(tiles)], axis=1
                        )[:, 0:cols]
                        for b in range(a, a + joined)
                    ],
                    axis=1,
                )
                if number == 0:
                    value = value * QSCALE
                for n in range(joined * cols // 128):
                    block_s[tile_of((offset + a * cols) // 128 + n)] = value[
                        :, 128 * n : 128 * n + 128
                    ]
            offset += per * cols
        rows = [jnp.sum(jnp.transpose(ln_s[n]), axis=0, keepdims=True) for n in range(4)]
        def last_row(ref, at):
            return jnp.concatenate(
                [ref[0, at : at + 1, :], ref[1, at : at + 1, 0 : C - 128]], axis=1
            )

        flat = jnp.concatenate(
            [
                rows[0],
                rows[1],
                last_row(aq, C) * QSCALE,
                jnp.concatenate(sums[1], axis=1)[:, C:],
                last_row(ao, C),
                rows[2],
                rows[3],
                *sums[3],
                last_row(a2, HIDDEN_SIZE),
            ],
            axis=1,
        )
        big[0] = jnp.zeros((8 * WTOK, 128), F32)
        for h in range(HEADS):
            big[0, pl.ds(h, WTOK, stride=8), :] = gds_s[h]
        hot = (iota((128, 256), 1) == place(iota((128, 256), 0) & 63)).astype(BF)
        total = sum(mm(part, hot) for part in splits(big[0]))
        big[0] = total[:, 0:128]
        big[1] = total[:, 128:256]
        result = jnp.zeros((8, 384), F32)
        for j in range(WTOK):
            row = jnp.concatenate(
                [
                    big[0, 8 * j : 8 * j + 8, :],
                    big[1, 8 * j : 8 * j + 8, :],
                    jnp.zeros((8, 128), F32),
                ],
                axis=1,
            )
            turn = (place(WTOK - 1) - place(j)) % 384
            result = result + (pltpu.roll(row, turn, 1) if turn else row)
        per = VEC // ROWS
        block_s[tile_of(VEC_TILE)] = jnp.concatenate(
            [
                jnp.concatenate([flat[:, per * k : per * k + per] for k in range(ROWS)], axis=0),
                jnp.zeros((ROWS, 128 - per), F32),
            ],
            axis=1,
        )
        count = TABLE_LANES
        block_s[tile_of(SIDE_TILE)] = jnp.concatenate(
            [
                jnp.concatenate([result[:, count * n : count * n + count] for n in range(4)], axis=0),
                jnp.zeros((ROWS, 128 - count), F32),
            ],
            axis=1,
        )
        for number in range(SIDE_TILE + 1, BLOCK[0] * BLOCK_TILES):
            block_s[tile_of(number)] = jnp.zeros((ROWS, 128), F32)
        for outer in range(OUTER):
            for inner in range(INNER):
                k = inner * OUTER + lax.bitwise_xor(my_skip, outer)
                rows = pl.ds(pl.multiple_of(k * BLOCK[0], BLOCK[0]), BLOCK[0])
                for n in range(BLOCK_TILES):
                    grad_packs[outer][inner, :, 128 * n : 128 * n + 128] = block_s[
                        n, rows, :
                    ].astype(BF)
        for n in range(skip_count):
            grad_picks[n][...] = pick_s[n]


def layer_call(skip_count, chosen, extents, here, ranks, dec, cot, bias, packs, pieces):
    tokens = dec.shape[1]
    windows = tokens // WTOK
    steps = tokens // T
    share = tokens // skip_count
    block = pl.BlockSpec((C, T), lambda i: (0, i))
    smem = pl.BlockSpec(memory_space=pltpu.SMEM)
    hbm = pl.BlockSpec(memory_space=pltpu.HBM)

    def whole(shape):
        return pl.BlockSpec(shape, lambda i: (0,) * len(shape))

    scratch = [
        ((skip_count, C, share), BF),
        ((2, 8 * WTOK, 128), F32),
        ((VEC, 128), F32),
        ((C, C), BF),
        ((C, C), BF),
        ((C, 2 * C), BF),
        ((2 * C, C), BF),
        ((C, C), BF),
        ((C, C), BF),
        ((C, HIDDEN_SIZE), BF),
        ((HIDDEN_SIZE, C), BF),
        ((HIDDEN_SIZE, C), BF),
        ((C, HIDDEN_SIZE), BF),
        ((C + 16, T), BF),
        ((C + 16, T), BF),
        ((C + 16, T), BF),
        ((C + 16, T), BF),
        ((HIDDEN_SIZE + 16, T), BF),
        ((HIDDEN_SIZE, T), BF),
        ((C, T), BF),
        ((GROUPS * HEADS, GWIN * HEAD_DIM, GROUP), BF),
        ((GROUPS * HEADS, GWIN * HEAD_DIM, WTOK), BF),
        ((GROUPS * HEADS, GWIN * HEAD_DIM, WTOK), BF),
        ((GROUPS * HEADS, WTOK, GWIN * HEAD_DIM), BF),
        ((GROUPS * HEADS, WTOK, GWIN * HEAD_DIM), BF),
        ((GROUPS * HEADS, WTOK, GROUP), F32),
        ((GROUPS * HEADS, WTOK, GROUP), BF),
        ((GROUPS * HEADS, WTOK, GROUP), BF),
        ((C, T), BF),
        ((C, T), BF),
        ((C, T), BF),
        ((T // 128, HIDDEN_SIZE, 128), F32),
        ((T // 128, HIDDEN_SIZE, 128), F32),
        ((C, T), F32),
        ((C, T), F32),
        ((C, T), BF),
        ((2 * C, T), BF),
        ((C, T), F32),
        ((C, T), F32),
        ((C, T), F32),
        ((C, T), F32),
        ((HEADS, WTOK, 128), F32),
        ((2, C + 16, 128), F32),
        ((2 * C, C + 16), F32),
        ((2, C + 16, 128), F32),
        ((HIDDEN_SIZE, C + 16), F32),
        ((2, HIDDEN_SIZE + 16, 128), F32),
        ((4, C, 128), F32),
    ]
    flops = 2 * tokens * (3 * 442368 + 12 * WTOK * C)
    return pl.pallas_call(
        functools.partial(layer_kernel, skip_count, windows, len(pieces)),
        grid=(steps,),
        in_specs=[smem, smem, smem, smem, hbm, hbm, whole(bias.shape)]
        + [pl.BlockSpec(memory_space=pl.ANY)] * (OUTER + len(pieces)),
        out_specs=[block, block, whole((ROWS, 128))]
        + [whole((C, share))] * skip_count
        + [whole((INNER, *BLOCK))] * OUTER,
        out_shape=[
            jax.ShapeDtypeStruct((C, tokens), BF),
            jax.ShapeDtypeStruct((C, tokens), F32),
            jax.ShapeDtypeStruct((ROWS, 128), jnp.int32),
        ]
        + [jax.ShapeDtypeStruct((C, share), BF)] * skip_count
        + [jax.ShapeDtypeStruct((INNER, *BLOCK), BF)] * OUTER,
        scratch_shapes=[pltpu.VMEM(shape, kind) for shape, kind in scratch]
        + [
            pltpu.VMEM((C, skip_count * tokens), BF),
            pltpu.SemaphoreType.DMA((len(pieces),)),
            pltpu.VMEM((steps, C, T), BF),
            pltpu.VMEM((steps, C, T), BF),
            pltpu.SemaphoreType.DMA((2 * steps,)),
            pltpu.VMEM((OUTER, INNER, *BLOCK), BF),
            pltpu.SemaphoreType.DMA((OUTER,)),
        ],
        compiler_params=pltpu.CompilerParams(
            dimension_semantics=("arbitrary",), vmem_limit_bytes=42 * 1024 * 1024
        ),
        cost_estimate=pl.CostEstimate(
            flops=flops, bytes_accessed=8_000_000, transcendentals=tokens * 1200
        ),
        name="layer",
    )(
        kept(chosen),
        extents,
        here,
        ranks,
        kept(dec),
        kept(cot),
        bias,
        *packs,
        kept(pieces[0]),
        *pieces[1:3],
        *[kept(piece) for piece in pieces[3:]],
    )


def pack_kernel(mat, vec, chosen, out):
    flat = jnp.concatenate(
        [
            mat[...],
            vec[...],
            jnp.zeros((1, 128 - vec.shape[1]), F32),
            chosen[...].astype(F32),
            jnp.zeros((1, BLOCK[0] * BLOCK[1] - 128 * SIDE_TILE - chosen.shape[1]), F32),
        ],
        axis=1,
    )
    block = jnp.concatenate(
        [flat[:, BLOCK[1] * j : BLOCK[1] * (j + 1)] for j in range(BLOCK[0])], axis=0
    ).astype(BF)
    for n in range(INNER):
        out[n] = block


def skip_sum_kernel(*refs):
    blocks, out = refs[:-1], refs[-1]
    for n in range(INNER):
        out[n] = sum(block[n].astype(F32) for block in blocks).astype(BF)


def split_kernel(here, *refs):
    blocks, (keep, send) = refs[:-2], refs[-2:]
    for n in range(INNER // 2):
        for odd, out in enumerate((keep, send)):
            at = lax.bitwise_xor(here[3], 2 * n + odd)
            out[n] = sum(block[at].astype(F32) for block in blocks).astype(out.dtype)


def halve_kernel(kept, came, keep, send):
    for n in range(kept.shape[0] // 2):
        keep[n] = kept[2 * n] + came[2 * n].astype(F32)
        send[n] = (kept[2 * n + 1] + came[2 * n + 1].astype(F32)).astype(BF)


def slab_sum_kernel(kept, came, mat, vec, tail):
    total = kept[0] + came[0].astype(F32)
    squares = jnp.sum(jnp.sum(total * total, axis=1, keepdims=True), axis=0, keepdims=True)
    flat = jnp.concatenate([total[j : j + 1, :] for j in range(BLOCK[0])], axis=1)
    mat[...] = flat[:, 0 : mat.shape[1]]
    vec[...] = flat[:, 128 * VEC_TILE : 128 * VEC_TILE + vec.shape[1]]
    side = flat[:, 128 * SIDE_TILE : 128 * SIDE_TILE + 128]
    side = jnp.where(iota((1, 128), 1) == TABLE_LANES, squares, side)
    tail[...] = jnp.broadcast_to(side, tail.shape)


def return_kernel(windows, row, here, everyone, after, *refs):
    del after
    received, (out, gathered, source) = refs[:-3], refs[-3:]
    skip_count = len(received)
    per = windows // skip_count
    mix = here[1]
    for d in range(skip_count):
        gathered[d] = received[d][...]
        s = lax.bitwise_xor(mix, d)

        def note(w, rank):
            a = everyone[here[3] * row + s, w]
            mine = lax.div(a, windows) == here[2]

            @pl.when(mine)
            def _():
                source[lax.rem(a, windows)] = d * per + rank

            return rank + mine.astype(jnp.int32)

        lax.fori_loop(0, windows, note, 0)
    left = iota((1, 128), 1) < WTOK
    for n in range(windows // 2):
        halves = []
        for w in (0, 1):
            place_in = source[2 * n + w]
            d, rank = lax.div(place_in, per), lax.rem(place_in, per)
            lanes = pl.ds(pl.multiple_of((rank >> 1) * 128, 128), 128)
            block = gathered[d, :, lanes].astype(F32)
            halves.append(pltpu.roll(block, ((rank + w) & 1) * WTOK, 1))
        out[:, 128 * n : 128 * n + 128] = jnp.where(left, halves[0], halves[1])


VMEM = pl.BlockSpec(memory_space=pltpu.VMEM)
SMEM = pl.BlockSpec(memory_space=pltpu.SMEM)


def small_call(kernel, name, in_specs, outs, operands, scratch=(), moved=1_000_000):
    return pl.pallas_call(
        kernel,
        in_specs=in_specs,
        out_specs=[VMEM] * len(outs),
        out_shape=outs,
        scratch_shapes=scratch,
        compiler_params=pltpu.CompilerParams(vmem_limit_bytes=16 * 1024 * 1024),
        cost_estimate=pl.CostEstimate(flops=moved, bytes_accessed=moved, transcendentals=0),
        name=name,
    )(*operands)


def repack(packed, count):
    pieces, offset = [], 0
    for rows, cols in SHAPES:
        width = rows * cols // packed.shape[0]
        pieces.append(packed[:, offset : offset + width].reshape(count, -1))
        offset += width
    return jnp.concatenate(pieces, axis=1)


def padded(value, width):
    return jnp.pad(value, ((0, 0), (0, width - value.shape[1])))


def adamw_update(master, first, second, average, grad, factor, decay):
    clipped = grad * factor
    first_new = BETA_ONE * first + (1.0 - BETA_ONE) * clipped
    second_new = BETA_TWO * second + (1.0 - BETA_TWO) * clipped * clipped
    first_hat = first_new / (1.0 - BETA_ONE**STEP)
    second_hat = second_new / (1.0 - BETA_TWO**STEP)
    master_new = master - RATE * (first_hat / (jnp.sqrt(second_hat) + ADAM_EPS) + decay * master)
    average_new = EMA_RATE * average + (1.0 - EMA_RATE) * master_new
    return (clipped, master_new, first_new, second_new, average_new, master_new.astype(BF))


def update_kernel(mat_share, vec_share, tail, *refs):
    mats, vecs, tables = refs[0:4], refs[4:8], refs[8:12]
    norm_out, outs = refs[12], refs[13:]
    squares = jnp.sum(tail[:, TABLE_LANES : TABLE_LANES + 1], axis=0, keepdims=True)
    norm = jnp.sqrt(squares)
    norm_out[...] = norm
    factor = CLIP / jnp.maximum(norm, CLIP)
    table = jnp.concatenate([tail[8 * q : 8 * q + 8, 0:TABLE_LANES] for q in range(4)], axis=1)
    work = (
        (mats, mat_share[...], MATRIX_DECAY),
        (vecs, vec_share[...], 0.0),
        (tables, table[0:HEADS, 0:REL], 0.0),
    )
    for n, (group, grad, decay) in enumerate(work):
        results = adamw_update(*[ref[...] for ref in group], grad, factor, decay)
        for ref, value in zip(outs[6 * n : 6 * n + 6], results):
            ref[...] = value


def on_device(
    decoder_tokens,
    skip_tokens,
    cotangent,
    extents,
    assignment,
    mat_master,
    mat_first,
    mat_second,
    mat_average,
    vec_master,
    vec_first,
    vec_second,
    vec_average,
    table_master,
    table_first,
    table_second,
    table_average,
):
    skip_count = lax.axis_size("skip")
    slab_count = lax.axis_size("slab")
    device_count = skip_count * slab_count
    windows = assignment.shape[1]
    mat_width, vec_width = mat_master.shape[1], vec_master.shape[1]
    me = lax.axis_index("skip")
    plain = (skip_count, slab_count) == (OUTER, INNER)

    def swap(value, axis, distance):
        count = lax.axis_size(axis)
        return lax.ppermute(value, axis, [(n, n ^ distance) for n in range(count)])

    if plain:
        here = jnp.stack([me, me, me, lax.axis_index("slab")])
        (block,) = small_call(
            pack_kernel,
            "pack",
            [VMEM] * 3,
            [jax.ShapeDtypeStruct((INNER, *BLOCK), BF)],
            (kept(mat_master), kept(vec_master), kept(assignment)),
            moved=100_000,
        )
        own = lax.all_to_all(block, "slab", split_axis=0, concat_axis=0)
        across = swap(skip_tokens, "skip", 2)
        near = swap(skip_tokens, "skip", 1)
        packs_across = swap(own, "skip", 2)
        packs_across, across = lax.optimization_barrier((packs_across, across))
        packs = [own, swap(own, "skip", 1), packs_across, swap(packs_across, "skip", 1)]
        pieces = [skip_tokens, near, across, swap(across, "skip", 1)]
    else:
        zero = jnp.zeros_like(me)
        here = jnp.stack([zero, zero, me, zero])
        low = jnp.concatenate([mat_master, vec_master], axis=1).astype(BF)
        low = lax.all_gather(low, ("slab", "skip"), axis=0, tiled=True)
        vec = padded(low[:, mat_width:].reshape(ROWS, -1), 128)
        low = padded(
            jnp.concatenate([repack(low, ROWS), vec], axis=1), BLOCK[0] * BLOCK[1]
        ).reshape(INNER, OUTER, *BLOCK)
        packs = [low[:, n] for n in range(OUTER)]
        pieces = [lax.all_gather(skip_tokens, "skip", axis=0, tiled=True)]

    bias, ranks = pl.pallas_call(
        functools.partial(early_kernel, skip_count, windows),
        in_specs=[SMEM, VMEM, pl.BlockSpec(memory_space=pl.ANY)],
        out_specs=[VMEM, VMEM],
        out_shape=[
            jax.ShapeDtypeStruct((HEADS, WTOK, 128), F32),
            jax.ShapeDtypeStruct((1, 128), jnp.int32),
        ],
        scratch_shapes=[
            pltpu.VMEM((8, 384), F32),
            pltpu.VMEM((2, 8 * WTOK, 128), F32),
            pltpu.SMEM((skip_count,), jnp.int32),
        ],
        compiler_params=pltpu.CompilerParams(vmem_limit_bytes=16 * 1024 * 1024),
        cost_estimate=pl.CostEstimate(flops=100_000_000, bytes_accessed=1_000_000, transcendentals=0),
        name="early",
    )(kept(assignment[0]), kept(table_master.T), packs[0])
    layer_out, grad_decoder, everyone, *grads = layer_call(
        skip_count,
        assignment[0],
        extents,
        here,
        ranks,
        decoder_tokens.T,
        cotangent.T,
        bias,
        packs,
        [piece.T for piece in pieces],
    )
    grad_picks, grad_packs = grads[:skip_count], grads[skip_count:]

    def returned_call(here, everyone, after, received):
        (grad_skip,) = small_call(
            functools.partial(return_kernel, windows, OUTER),
            "returned",
            [SMEM, SMEM] + [VMEM] * (1 + skip_count),
            [jax.ShapeDtypeStruct((C, windows * WTOK), F32)],
            (here, everyone, after, *received),
            [
                pltpu.VMEM((skip_count, *received[0].shape), BF),
                pltpu.SMEM((windows,), jnp.int32),
            ],
            3_000_000,
        )
        return grad_skip

    shares = [
        jax.ShapeDtypeStruct((1, mat_width), F32),
        jax.ShapeDtypeStruct((1, vec_width), F32),
    ]
    if plain:
        far = swap(grad_packs[3], "skip", 1)
        near = swap(grad_packs[1], "skip", 1)
        (far,) = small_call(
            skip_sum_kernel,
            "core_sum",
            [VMEM] * 2,
            [jax.ShapeDtypeStruct((INNER, *BLOCK), BF)],
            (grad_packs[2], far),
        )
        keep, send = small_call(
            split_kernel,
            "skip_sum",
            [SMEM] + [VMEM] * 3,
            [
                jax.ShapeDtypeStruct((INNER // 2, *BLOCK), F32),
                jax.ShapeDtypeStruct((INNER // 2, *BLOCK), BF),
            ],
            (here, grad_packs[0], near, swap(far, "skip", 2)),
        )
        send, grad_picks = lax.optimization_barrier((send, grad_picks))
        received = [grad_picks[0]] + [swap(grad_picks[d], "skip", d) for d in range(1, OUTER)]
        for distance in (1, 2):
            half = keep.shape[0] // 2
            keep, send = small_call(
                halve_kernel,
                "slab_half",
                [VMEM] * 2,
                [
                    jax.ShapeDtypeStruct((half, *BLOCK), F32),
                    jax.ShapeDtypeStruct((half, *BLOCK), BF),
                ],
                (keep, swap(send, "slab", distance)),
                moved=300_000,
            )
        came, received = lax.optimization_barrier((swap(send, "slab", 4), received))
        mat_share, vec_share, tail = small_call(
            slab_sum_kernel,
            "slab_sum",
            [VMEM] * 2,
            shares + [jax.ShapeDtypeStruct((ROWS, 128), F32)],
            (keep, came),
            moved=300_000,
        )
        grad_skip = returned_call(here, everyone, vec_share, received)
        tail = lax.all_to_all(tail, ("slab", "skip"), split_axis=0, concat_axis=0, tiled=True)
        tail, grad_skip = lax.optimization_barrier((tail, grad_skip))
    else:
        received = list(
            lax.all_to_all(jnp.stack(grad_picks), "skip", split_axis=0, concat_axis=0)
        )
        everyone = lax.all_gather(assignment, "skip", axis=0, tiled=True)
        rows = jnp.stack(grad_packs, axis=1).reshape(ROWS, -1)
        start, side = 128 * VEC_TILE, 128 * SIDE_TILE
        rows = jnp.concatenate(
            [
                repack(rows, device_count),
                rows[:, start : start + VEC // ROWS].reshape(device_count, -1),
                rows[:, side : side + TABLE_LANES].reshape(device_count, -1),
            ],
            axis=1,
        )
        share = lax.psum_scatter(
            rows.astype(F32), ("slab", "skip"), scatter_dimension=0, tiled=True
        )
        mat_share = share[:, :mat_width]
        vec_share = share[:, mat_width : mat_width + vec_width]
        table = lax.all_gather(
            share[:, mat_width + vec_width :], ("slab", "skip"), axis=0, tiled=True
        )
        squares = lax.psum(jnp.sum(share * share), ("slab", "skip")) * (1.0 / ROWS)
        tail = jnp.concatenate(
            [table.reshape(ROWS, TABLE_LANES), jnp.full((ROWS, 128 - TABLE_LANES), squares)],
            axis=1,
        )

    if not plain:
        grad_skip = returned_call(here, everyone, vec_share, received)
    groups = (
        (mat_master, mat_first, mat_second, mat_average),
        (vec_master, vec_first, vec_second, vec_average),
        (table_master.T, table_first.T, table_second.T, table_average.T),
    )
    kinds = [jax.ShapeDtypeStruct((1, 1), F32)]
    for group in groups:
        kinds += [jax.ShapeDtypeStruct(group[0].shape, F32)] * 5
        kinds += [jax.ShapeDtypeStruct(group[0].shape, BF)]
    outs = small_call(
        update_kernel,
        "update",
        [VMEM] * 15,
        kinds,
        (mat_share, vec_share, tail, *groups[0], *groups[1], *groups[2]),
    )
    return (
        layer_out.T,
        grad_decoder.T,
        grad_skip.T,
        outs[0].reshape(()),
        *outs[1:13],
        *[value.T for value in outs[13:]],
    )


def solution(mesh):
    split = P(("slab", "skip"), None)
    return jax.shard_map(
        on_device,
        mesh=mesh,
        in_specs=(split, split, split, P("slab"), P("slab", "skip"))
        + (split,) * 8
        + (P(),) * 4,
        out_specs=(split, split, split, P()) + (split,) * 12 + (P(),) * 6,
        check_vma=False,
    )
```

```python
import functools
import math
import jax
import jax.numpy as jnp
from jax import lax
from jax.experimental import pallas as pl
from jax.experimental.pallas import tpu as pltpu
from jax.sharding import PartitionSpec as P

C = 192
HEADS = 6
HEAD_DIM = 32
HIDDEN_SIZE = 768
WS = 4
DEPTH = 16
STEP = 10
WTOK = 64
REL = 343

EPS = 1e-05
MASK_FILL = -1000000000.0
CLIP = 1.0
BETA_ONE = 0.9
BETA_TWO = 0.999
RATE = 0.3
MATRIX_DECAY = 0.05
ADAM_EPS = 1e-08
EMA_RATE = 0.9

BF = jnp.bfloat16
F32 = jnp.float32
GROUP = 256
GWIN = GROUP // WTOK
T = 1024
GROUPS = T // GROUP
WIDE = 512
PARTS = T // WIDE
WIN = T // WTOK
QSCALE = HEAD_DIM ** (-0.5)
SHAPES = ((C, C), (C, 2 * C), (C, C), (C, HIDDEN_SIZE), (HIDDEN_SIZE, C))
VLEN = (C, C, C, C, C, C, C, HIDDEN_SIZE, C)
VOFF = tuple(sum(VLEN[:n]) for n in range(len(VLEN)))
VEC = sum(VLEN)
MAT = sum(r * c for r, c in SHAPES)
ROWS = 32
OUTER = 4
INNER = ROWS // OUTER
BLOCK = (16, 896)
BLOCK_TILES = BLOCK[1] // 128
VEC_TILE = MAT // ROWS // 128
SIDE_TILE = VEC_TILE + 1
TABLE_LANES = 8 * 384 // ROWS


def mm(a, b):
    return jnp.dot(a, b, preferred_element_type=F32)


def mm_nt(a, b):
    return lax.dot_general(a, b, (((1,), (1,)), ((), ())), preferred_element_type=F32)


def iota(shape, dim):
    return lax.broadcasted_iota(jnp.int32, shape, dim)


def kept(value):
    return pltpu.with_memory_space_constraint(value, pltpu.HBM)


def both(column, width=256):
    return jnp.concatenate([column] * (width // 128), axis=1)


def place(slot):
    span = 2 * WS - 1
    return ((slot >> 4) * span + ((slot >> 2) & 3)) * span + (slot & 3)


def splits(value):
    high = value.astype(BF)
    rest = value - high.astype(F32)
    middle = rest.astype(BF)
    return high, middle, (rest - middle.astype(F32)).astype(BF)


def normed(value):
    center = value - jnp.sum(value, axis=0, keepdims=True) * (1.0 / C)
    scale = lax.rsqrt(jnp.sum(center * center, axis=0, keepdims=True) * (1.0 / C) + EPS)
    return center * scale, scale


def normed_back(grad_hat, hat, scale):
    mean_grad = jnp.sum(grad_hat, axis=0, keepdims=True) * (1.0 / C)
    mean_both = jnp.sum(grad_hat * hat, axis=0, keepdims=True) * (1.0 / C)
    return scale * (grad_hat - mean_grad - hat * mean_both)


def fold(value):
    return sum(value[:, n : n + 128] for n in range(0, value.shape[1], 128))


def gelu_parts(u):
    t = pl.reciprocal(1.0 + (0.3275911 * 0.5**0.5) * jnp.abs(u), approx=True)
    bell = jnp.exp2((-0.5 * math.log2(math.e)) * (u * u))
    series = 0.5 * 1.061405429
    for factor in (-1.453152027, 1.421413741, -0.284496736, 0.254829592):
        series = series * t + 0.5 * factor
    tail = series * t * bell
    cdf = jnp.where(u >= 0.0, 1.0 - tail, tail)
    return u * cdf, cdf + ((0.5 / math.pi) ** 0.5 * u) * bell


def early_kernel(skip_count, windows, chosen, table, after, bias_s, ranks, tab_s, big, count_s):
    del after
    tab_s[...] = jnp.zeros_like(tab_s)
    tab_s[0:HEADS, 0:REL] = table[...]
    hot = (iota((256, 128), 0) == place(iota((256, 128), 1) & 63)).astype(BF)
    total = None
    for part in splits(tab_s[...]):
        part = part.astype(F32)
        for j in range(WTOK):
            turn = (place(j) - place(WTOK - 1)) % 384
            rolled = pltpu.roll(part, turn, 1) if turn else part
            big[0, 8 * j : 8 * j + 8, :] = rolled[:, 0:128]
            big[1, 8 * j : 8 * j + 8, :] = rolled[:, 128:256]
        product = mm(big[0].astype(BF), hot[0:128]) + mm(big[1].astype(BF), hot[128:256])
        total = product if total is None else total + product
    big[0] = total
    for h in range(HEADS):
        bias_s[h] = big[0, pl.ds(h, WTOK, stride=8), :]
    for e in range(skip_count):
        count_s[e] = 0

    def note(w, rank_row):
        owner = lax.div(chosen[w], windows)
        rank = count_s[owner]
        count_s[owner] = rank + 1
        return jnp.where(iota((1, 128), 1) == w, rank, rank_row)

    ranks[...] = lax.fori_loop(0, windows, note, jnp.zeros((1, 128), jnp.int32))


def layer_kernel(
    skip_count,
    windows,
    piece_count,
    chosen,
    extents,
    here,
    ranks,
    dec_all,
    cot_all,
    bias_s,
    *refs,
):
    step = pl.program_id(0)
    packs, refs = refs[:OUTER], refs[OUTER:]
    pieces, refs = refs[:piece_count], refs[piece_count:]
    layer_out, grad_dec, everyone, *refs = refs
    grad_picks, refs = refs[:skip_count], refs[skip_count:]
    grad_packs, refs = refs[:OUTER], refs[OUTER:]
    (
        pick_s,
        big,
        vcol,
        wq,
        wqt,
        wkv,
        wkvt,
        wo,
        wot,
        w1,
        w1t,
        w2,
        w2t,
        xn_s,
        sn_s,
        hn_s,
        o_s,
        gl_s,
        du_s,
        q_s,
        qbd_s,
        kst_s,
        vst_s,
        kcat_s,
        vcat_s,
        pf_s,
        pb_s,
        ds_s,
        da_s,
        do_s,
        dm_s,
        u_s,
        ga_s,
        gh_s,
        gs_s,
        dq_s,
        dkv_s,
        n1_s,
        n2_s,
        n3_s,
        x1_s,
        gds_s,
        aq,
        akv,
        ao,
        a1,
        a2,
        ln_s,
        slab,
        slab_sem,
        dec_s,
        cot_s,
        token_sem,
        pack_s,
        pack_sem,
    ) = refs
    dec, cot = dec_s.at[step], cot_s.at[step]
    stage, block_s = u_s, ga_s
    my_skip, mix = here[0], here[1]
    lane = iota((1, 128), 1)
    left = lane < WTOK

    def tile_of(number):
        j, n = divmod(number, BLOCK_TILES)
        return n, pl.ds(j, ROWS, stride=BLOCK[0]), slice(None)


    def token_copies(n):
        lanes = slice(T * n, T * n + T)
        return [
            pltpu.make_async_copy(dec_all.at[:, lanes], dec_s.at[n], token_sem.at[2 * n]),
            pltpu.make_async_copy(cot_all.at[:, lanes], cot_s.at[n], token_sem.at[2 * n + 1]),
        ]

    for n in range(1, windows // WIN):

        @pl.when(step == n)
        def _(n=n):
            for copy in token_copies(n):
                copy.wait()

    @pl.when(step == 0)
    def _():
        copies = token_copies(0) + [
            pltpu.make_async_copy(
                piece, slab.at[:, n * piece.shape[1] : (n + 1) * piece.shape[1]], slab_sem.at[n]
            )
            for n, piece in enumerate(pieces)
        ]
        pack_copies = [
            pltpu.make_async_copy(packs[n], pack_s.at[n], pack_sem.at[n]) for n in range(OUTER)
        ]
        for copy in pack_copies + copies + [copy for n in range(1, windows // WIN) for copy in token_copies(n)]:
            copy.start()
        for ref in (gds_s, aq, akv, ao, a1, a2, ln_s):
            ref[...] = jnp.zeros_like(ref)
        for ref, rows in ((xn_s, C), (sn_s, C), (hn_s, C), (o_s, C), (gl_s, HIDDEN_SIZE)):
            ref[rows : rows + 16, :] = jnp.ones((16, T), BF)
        for copy in pack_copies:
            copy.wait()
        for outer in range(OUTER):
            for inner in range(INNER):
                k = inner * OUTER + lax.bitwise_xor(my_skip, outer)
                rows = pl.ds(pl.multiple_of(k * BLOCK[0], BLOCK[0]), BLOCK[0])
                for n in range(BLOCK_TILES):
                    block_s[n, rows, :] = pack_s[outer, inner, :, 128 * n : 128 * n + 128].astype(
                        F32
                    )
        offset = 0
        for (rows, cols), plain, turned in zip(
            SHAPES, (wq, wkv, wo, w1, w2), (wqt, wkvt, wot, w1t, w2t)
        ):
            per = rows // ROWS
            tiles = -(-cols // 128)
            for a in range(per):
                first, shift = divmod(offset + a * cols, 128)
                for n in range(tiles):
                    piece = block_s[tile_of(first + n)]
                    if shift and n + 1 < tiles:
                        after = block_s[tile_of(first + n + 1)]
                        piece = jnp.concatenate([piece[:, shift:], after[:, :shift]], axis=1)
                    elif shift:
                        piece = pltpu.roll(piece, 128 - shift, 1)
                    stage[n, pl.ds(a, ROWS, stride=per), :] = piece
            for n in range(tiles):
                width = min(128, cols - 128 * n)
                value = stage[n, 0:rows, :].astype(BF)
                plain[:, 128 * n : 128 * n + width] = value[:, 0:width]
                turned[128 * n : 128 * n + width, :] = jnp.transpose(value)[0:width]
            offset += per * cols
        side = block_s[tile_of(VEC_TILE)]
        per = VEC // ROWS
        vec = jnp.concatenate([side[k : k + 1, 0:per] for k in range(ROWS)], axis=1)
        vcol[...] = jnp.transpose(jnp.broadcast_to(vec, (128, VEC)))
        side = block_s[tile_of(SIDE_TILE)]
        everyone[...] = side.astype(jnp.int32)
        for copy in copies:
            copy.wait()

    def column(number, first=0, last=None):
        start = VOFF[number]
        return vcol[start + first : start + (VLEN[number] if last is None else last), :]

    chunks = [slice(128 * c, 128 * c + 128) for c in range(T // 128)]
    tiles = [slice(GROUP * g, GROUP * g + GROUP) for g in range(GROUPS)]
    wides = [slice(WIDE * g, WIDE * g + WIDE) for g in range(PARTS)]
    per_wide = WIDE // 128
    groups_wide = WIDE // GROUP
    layers, valid = [], []
    for c in range(len(chunks)):
        deep = [
            jnp.clip(extents[0] - WS * (chosen[step * WIN + 2 * c + w] & 3), 0, WS) for w in (0, 1)
        ]
        layers.append(jnp.where(left, deep[0], deep[1]))
        valid.append(jnp.where((lane & 63) >> 4 < layers[c], 1.0, 0.0))

    scale_one, scale_two, scale_three = {}, {}, {}

    def stacks(rows, g, stack_ref, cat_ref):
        turned = pltpu.roll(rows, WTOK, 1)
        first, second = rows[:, 0:128], rows[:, 128:256]
        mixed, middle = turned[:, 0:128], turned[:, 128:256]
        at_left = (first, middle, second, mixed)
        at_right = (mixed, first, middle, second)
        for h in range(0, HEADS, 2):
            n = g * HEADS + h
            at = slice(HEAD_DIM * h, HEAD_DIM * h + HEAD_DIM)
            after = slice(HEAD_DIM * h + HEAD_DIM, HEAD_DIM * h + 2 * HEAD_DIM)
            pieces = []
            for w in range(GWIN):
                to = slice(HEAD_DIM * w, HEAD_DIM * w + HEAD_DIM)
                stack_ref[n, to, :] = at_left[w][at, 0:WTOK]
                stack_ref[n + 1, to, :] = at_left[w][after, 0:WTOK]
                pieces.append(jnp.where(left, at_left[w][at], at_right[w][after]))
            pair = jnp.transpose(jnp.concatenate(pieces, axis=0))
            cat_ref[n] = pair[0:WTOK]
            cat_ref[n + 1] = pair[WTOK:]

    window_mask = [
        (iota((HEAD_DIM, GROUP), 1) >> 6 == w).astype(F32).astype(BF) for w in range(GWIN)
    ]

    def spread(rows):
        return jnp.concatenate([rows * mask for mask in window_mask], axis=0)

    def own(stacked, probs):
        parts = []
        for n in range(GWIN // 2):
            cut = mm(
                stacked[2 * HEAD_DIM * n : 2 * HEAD_DIM * (n + 1)],
                probs[:, 128 * n : 128 * n + 128],
            )
            parts.append(jnp.where(left, cut[0:HEAD_DIM], cut[HEAD_DIM:]))
        return jnp.concatenate(parts, axis=1)

    def unstack(product):
        parts = []
        for n in range(GWIN // 2):
            cut = product[2 * HEAD_DIM * n : 2 * HEAD_DIM * (n + 1)]
            parts.append(jnp.where(left, cut[0:HEAD_DIM], cut[HEAD_DIM:]))
        return jnp.concatenate(parts, axis=1)

    def filled(g):
        return jnp.concatenate(
            [
                jnp.concatenate(
                    [
                        jnp.broadcast_to(jnp.where(layers[c] > d, 0.0, MASK_FILL), (WS * WS, 128))
                        for d in range(WS)
                    ],
                    axis=0,
                )
                for c in (2 * g, 2 * g + 1)
            ],
            axis=1,
        )

    def place_of(n):
        g, h = divmod(n, HEADS)
        return slice(HEAD_DIM * h, HEAD_DIM * h + HEAD_DIM), tiles[g]

    def softmax(n, scores, fill):
        scores = scores + both(bias_s[n % HEADS]) + fill
        powers = jnp.exp(scores - jnp.max(scores, axis=0, keepdims=True))
        probs = powers * pl.reciprocal(jnp.sum(powers, axis=0, keepdims=True), approx=True)
        pf_s[n] = probs
        pb_s[n] = probs.astype(BF)

    def softmax_back(n, grad_probs):
        probs = pf_s[n]
        grad_scores = (
            probs * (grad_probs - jnp.sum(probs * grad_probs, axis=0, keepdims=True))
        ).astype(BF)
        gds_s[n % HEADS] += fold(grad_scores.astype(F32))
        ds_s[n] = grad_scores

    def forward(g):
        lanes = wides[g]
        for c in range(per_wide * g, per_wide * (g + 1)):
            cut = chunks[c]
            hat, scale_one[c] = normed(dec[:, cut].astype(F32))
            n1_s[:, cut] = hat
            xn_s[0:C, cut] = (hat * column(0) + column(1)).astype(BF)
            yield 130
            halves = []
            for w in (0, 1):
                a = chosen[step * WIN + 2 * c + w]
                at = lax.bitwise_xor(a, mix * windows) >> 1
                part = slab[:, pl.ds(pl.multiple_of(at * 128, 128), 128)]
                halves.append(pltpu.roll(part, ((a + w) & 1) * WTOK, 1))
            hat, scale_two[c] = normed(jnp.where(left, halves[0], halves[1]).astype(F32))
            n2_s[:, cut] = hat
            sn_s[0:C, cut] = (hat * column(0) + column(1)).astype(BF)
            yield 160
        query = mm(wqt[...], xn_s[0:C, lanes])
        pair = mm(wkvt[...], sn_s[0:C, lanes])
        q_s[:, lanes] = ((query + both(column(2), WIDE)) * QSCALE).astype(BF)
        for c in range(per_wide * g, per_wide * (g + 1)):
            dm_s[:, chunks[c]] = (cot[:, chunks[c]].astype(F32) * valid[c]).astype(BF)
        yield 250
        first, units = g * groups_wide * HEADS, groups_wide * HEADS
        for n in range(first, first + units):
            qbd_s[n] = spread(q_s[place_of(n)])
        keys = pair[0:C].astype(BF)
        values = (pair[C:] + both(column(3), WIDE)).astype(BF)
        for k in range(groups_wide):
            cut = slice(GROUP * k, GROUP * k + GROUP)
            stacks(keys[:, cut], groups_wide * g + k, kst_s, kcat_s)
            yield 250
            stacks(values[:, cut], groups_wide * g + k, vst_s, vcat_s)
            yield 250
        scores = {}
        for n in range(first, first + units + 2):
            if n < first + units:
                scores[n] = mm(kcat_s[n], qbd_s[n])
            if n >= first + 2:
                o_s[place_of(n - 2)] = own(vst_s[n - 2], pb_s[n - 2]).astype(BF)
            if first + 1 <= n <= first + units:
                if (n - 1) % HEADS == 0:
                    fill = filled((n - 1) // HEADS)
                softmax(n - 1, scores.pop(n - 1), fill)
            yield 180
        product = mm(w2[...], dm_s[:, lanes])
        for c in range(per_wide):
            ga_s[per_wide * g + c] = product[:, 128 * c : 128 * c + 128]
        yield 300
        x1_s[:, lanes] = mm(wot[...], o_s[0:C, lanes])
        yield 150
        for c in range(per_wide * g, per_wide * (g + 1)):
            cut = chunks[c]
            middle = dec[:, cut].astype(F32) + x1_s[:, cut] + column(4)
            x1_s[:, cut] = middle
            hat, scale_three[c] = normed(middle)
            n3_s[:, cut] = hat
            hn_s[0:C, cut] = (hat * column(5) + column(6)).astype(BF)
            yield 150

    def feed(g):
        lanes = wides[g]
        product = mm(w1t[...], hn_s[0:C, lanes])
        for c in range(per_wide):
            u_s[per_wide * g + c] = product[:, 128 * c : 128 * c + 128]
        yield 300
        piece = 32
        for start in range(0, HIDDEN_SIZE, piece):
            rows = slice(start, start + piece)
            for c in range(per_wide * g, per_wide * (g + 1)):
                active, slope = gelu_parts(u_s[c, rows, :] + column(7, start, start + piece))
                gl_s[rows, chunks[c]] = active.astype(BF)
                du_s[rows, chunks[c]] = (ga_s[c, rows, :] * slope).astype(BF)
            yield 35 * piece // 16
        gh_s[:, lanes] = mm(w1[...], du_s[:, lanes])
        yield 450
        mlp = mm(w2t[...], gl_s[0:HIDDEN_SIZE, lanes]) + both(column(8), WIDE)
        layer_out[:, lanes] = (
            jnp.concatenate(valid[per_wide * g : per_wide * (g + 1)], axis=1) * (x1_s[:, lanes] + mlp)
        ).astype(BF)
        yield 500
        for c in range(per_wide * g, per_wide * (g + 1)):
            cut = chunks[c]
            grad, hat = gh_s[:, cut], n3_s[:, cut]
            ln_s[2] += grad * hat
            ln_s[3] += grad
            back = normed_back(grad * column(5), hat, scale_three[c])
            grad_middle = cot[:, cut].astype(F32) * valid[c] + back
            x1_s[:, cut] = grad_middle
            da_s[:, cut] = grad_middle.astype(BF)
            yield 170
        do_s[:, lanes] = mm(wo[...], da_s[:, lanes]).astype(BF)
        yield 150

    def backward(g):
        lanes = wides[g]
        first, units = g * groups_wide * HEADS, groups_wide * HEADS
        spreads, grads = {}, {}
        for n in range(first, first + units + 2):
            if n < first + units:
                lanes = place_of(n)[1]
                at, _ = place_of(n)
                spreads[n] = spread(do_s[at, lanes])
                grads[n] = mm(vcat_s[n], spreads[n])
                twice = jnp.concatenate([pb_s[n], pb_s[n]], axis=0)
                dkv_s[at.start + C : at.stop + C, lanes] = unstack(
                    mm_nt(spreads.pop(n), twice)
                ).astype(BF)
            if n >= first + 2:
                at, lanes = place_of(n - 2)
                dq_s[at, lanes] = own(kst_s[n - 2], ds_s[n - 2]).astype(BF)
                twice = jnp.concatenate([ds_s[n - 2], ds_s[n - 2]], axis=0)
                dkv_s[at, lanes] = unstack(mm_nt(qbd_s[n - 2], twice)).astype(BF)
            if first + 1 <= n <= first + units:
                softmax_back(n - 1, grads.pop(n - 1))
            yield 340
        lanes = wides[g]
        gh_s[:, lanes] = mm(wq[...], dq_s[:, lanes])
        yield 150
        gs_s[:, lanes] = mm(wkv[...], dkv_s[:, lanes])
        yield 300
        for c in range(per_wide * g, per_wide * (g + 1)):
            cut = chunks[c]
            grad, hat = gh_s[:, cut] * QSCALE, n1_s[:, cut]
            ln_s[0] += grad * hat
            ln_s[1] += grad
            grad_dec[:, cut] = x1_s[:, cut] + normed_back(grad * column(0), hat, scale_one[c])
            yield 170
            grad, hat = gs_s[:, cut], n2_s[:, cut]
            ln_s[0] += grad * hat
            ln_s[1] += grad
            back = normed_back(grad * column(0), hat, scale_two[c]).astype(BF)
            for w in (0, 1):
                a = chosen[step * WIN + 2 * c + w]
                rank = ranks[0, step * WIN + 2 * c + w]
                owner = lax.bitwise_xor(lax.div(a, windows), mix)
                half = pltpu.roll(back, ((rank + w) & 1) * WTOK, 1)
                at = pl.ds(pl.multiple_of((rank >> 1) * 128, 128), 128)
                pick_s[owner, :, at] = jnp.where(
                    lane >> 6 == (rank & 1), half, pick_s[owner, :, at]
                )
            yield 250

    def add(ref, product):
        for n in range(ref.shape[0]):
            width = min(128, product.shape[1] - 128 * n)
            ref[n, :, 0:width] += product[:, 128 * n : 128 * n + width]

    def early_sums():
        add(a2, mm_nt(gl_s[...], dm_s[...]))
        yield 1200
        add(a1, mm_nt(hn_s[...], du_s[...]))
        yield 1200
        add(ao, mm_nt(o_s[...], da_s[...]))
        yield 400

    costs = {forward: 3500, feed: 3450, backward: 4000, early_sums: 2800}

    def interleaved(parts):
        running = [[part(*args), 0, costs[part]] for part, *args in parts]
        while running:
            now = min(running, key=lambda entry: entry[1] / entry[2])
            try:
                now[1] += next(now[0])
            except StopIteration:
                running.remove(now)

    for slot in range(PARTS + 2):
        parts = [
            (part, slot - lag)
            for lag, part in enumerate((forward, feed, backward))
            if 0 <= slot - lag < PARTS
        ]
        if slot == PARTS + 1:
            parts.append((early_sums,))
        interleaved(parts)
    add(aq, mm_nt(xn_s[...], dq_s[...]))
    add(akv, mm_nt(sn_s[...], dkv_s[...]))

    @pl.when(step == pl.num_programs(0) - 1)
    def _():
        offset = 0
        for number, ((rows, cols), ref) in enumerate(zip(SHAPES, (aq, akv, ao, a1, a2))):
            per = rows // ROWS
            tiles = -(-cols // 128)
            joined = 2 if cols % 128 else 1
            for a in range(0, per, joined):
                value = jnp.concatenate(
                    [
                        jnp.concatenate(
                            [ref[n, pl.ds(b, ROWS, stride=per), :] for n in range(tiles)], axis=1
                        )[:, 0:cols]
                        for b in range(a, a + joined)
                    ],
                    axis=1,
                )
                if number == 0:
                    value = value * QSCALE
                for n in range(joined * cols // 128):
                    block_s[tile_of((offset + a * cols) // 128 + n)] = value[
                        :, 128 * n : 128 * n + 128
                    ]
            offset += per * cols
        rows = [jnp.sum(jnp.transpose(ln_s[n]), axis=0, keepdims=True) for n in range(4)]
        def last_row(ref, at):
            row = [ref[n, at : at + 1, :] for n in range(ref.shape[0])]
            return jnp.concatenate(row, axis=1)

        flat = jnp.concatenate(
            [
                rows[0],
                rows[1],
                last_row(aq, C)[:, 0:C] * QSCALE,
                last_row(akv, C)[:, C:],
                last_row(ao, C)[:, 0:C],
                rows[2],
                rows[3],
                last_row(a1, C),
                last_row(a2, HIDDEN_SIZE)[:, 0:C],
            ],
            axis=1,
        )
        big[0] = jnp.zeros((8 * WTOK, 128), F32)
        for h in range(HEADS):
            big[0, pl.ds(h, WTOK, stride=8), :] = gds_s[h]
        hot = (iota((128, 256), 1) == place(iota((128, 256), 0) & 63)).astype(BF)
        total = sum(mm(part, hot) for part in splits(big[0]))
        big[0] = total[:, 0:128]
        big[1] = total[:, 128:256]
        result = jnp.zeros((8, 384), F32)
        for j in range(WTOK):
            row = jnp.concatenate(
                [
                    big[0, 8 * j : 8 * j + 8, :],
                    big[1, 8 * j : 8 * j + 8, :],
                    jnp.zeros((8, 128), F32),
                ],
                axis=1,
            )
            turn = (place(WTOK - 1) - place(j)) % 384
            result = result + (pltpu.roll(row, turn, 1) if turn else row)
        per = VEC // ROWS
        block_s[tile_of(VEC_TILE)] = jnp.concatenate(
            [
                jnp.concatenate([flat[:, per * k : per * k + per] for k in range(ROWS)], axis=0),
                jnp.zeros((ROWS, 128 - per), F32),
            ],
            axis=1,
        )
        count = TABLE_LANES
        block_s[tile_of(SIDE_TILE)] = jnp.concatenate(
            [
                jnp.concatenate([result[:, count * n : count * n + count] for n in range(4)], axis=0),
                jnp.zeros((ROWS, 128 - count), F32),
            ],
            axis=1,
        )
        for number in range(SIDE_TILE + 1, BLOCK[0] * BLOCK_TILES):
            block_s[tile_of(number)] = jnp.zeros((ROWS, 128), F32)
        for outer in range(OUTER):
            for inner in range(INNER):
                k = inner * OUTER + lax.bitwise_xor(my_skip, outer)
                rows = pl.ds(pl.multiple_of(k * BLOCK[0], BLOCK[0]), BLOCK[0])
                for n in range(BLOCK_TILES):
                    grad_packs[outer][inner, :, 128 * n : 128 * n + 128] = block_s[
                        n, rows, :
                    ].astype(BF)
        for n in range(skip_count):
            grad_picks[n][...] = pick_s[n]


def layer_call(skip_count, chosen, extents, here, ranks, dec, cot, bias, packs, pieces):
    tokens = dec.shape[1]
    windows = tokens // WTOK
    steps = tokens // T
    share = tokens // skip_count
    block = pl.BlockSpec((C, T), lambda i: (0, i))
    smem = pl.BlockSpec(memory_space=pltpu.SMEM)
    hbm = pl.BlockSpec(memory_space=pltpu.HBM)

    def whole(shape):
        return pl.BlockSpec(shape, lambda i: (0,) * len(shape))

    scratch = [
        ((skip_count, C, share), BF),
        ((2, 8 * WTOK, 128), F32),
        ((VEC, 128), F32),
        ((C, C), BF),
        ((C, C), BF),
        ((C, 2 * C), BF),
        ((2 * C, C), BF),
        ((C, C), BF),
        ((C, C), BF),
        ((C, HIDDEN_SIZE), BF),
        ((HIDDEN_SIZE, C), BF),
        ((HIDDEN_SIZE, C), BF),
        ((C, HIDDEN_SIZE), BF),
        ((C + 16, T), BF),
        ((C + 16, T), BF),
        ((C + 16, T), BF),
        ((C + 16, T), BF),
        ((HIDDEN_SIZE + 16, T), BF),
        ((HIDDEN_SIZE, T), BF),
        ((C, T), BF),
        ((GROUPS * HEADS, GWIN * HEAD_DIM, GROUP), BF),
        ((GROUPS * HEADS, GWIN * HEAD_DIM, WTOK), BF),
        ((GROUPS * HEADS, GWIN * HEAD_DIM, WTOK), BF),
        ((GROUPS * HEADS, WTOK, GWIN * HEAD_DIM), BF),
        ((GROUPS * HEADS, WTOK, GWIN * HEAD_DIM), BF),
        ((GROUPS * HEADS, WTOK, GROUP), F32),
        ((GROUPS * HEADS, WTOK, GROUP), BF),
        ((GROUPS * HEADS, WTOK, GROUP), BF),
        ((C, T), BF),
        ((C, T), BF),
        ((C, T), BF),
        ((T // 128, HIDDEN_SIZE, 128), F32),
        ((T // 128, HIDDEN_SIZE, 128), F32),
        ((C, T), F32),
        ((C, T), F32),
        ((C, T), BF),
        ((2 * C, T), BF),
        ((C, T), F32),
        ((C, T), F32),
        ((C, T), F32),
        ((C, T), F32),
        ((HEADS, WTOK, 128), F32),
        ((2, C + 16, 128), F32),
        ((3, C + 16, 128), F32),
        ((2, C + 16, 128), F32),
        ((6, C + 16, 128), F32),
        ((2, HIDDEN_SIZE + 16, 128), F32),
        ((4, C, 128), F32),
    ]
    flops = 2 * tokens * (3 * 442368 + 12 * WTOK * C)
    return pl.pallas_call(
        functools.partial(layer_kernel, skip_count, windows, len(pieces)),
        grid=(steps,),
        in_specs=[smem, smem, smem, smem, hbm, hbm, whole(bias.shape)]
        + [pl.BlockSpec(memory_space=pl.ANY)] * (OUTER + len(pieces)),
        out_specs=[block, block, whole((ROWS, 128))]
        + [whole((C, share))] * skip_count
        + [whole((INNER, *BLOCK))] * OUTER,
        out_shape=[
            jax.ShapeDtypeStruct((C, tokens), BF),
            jax.ShapeDtypeStruct((C, tokens), F32),
            jax.ShapeDtypeStruct((ROWS, 128), jnp.int32),
        ]
        + [jax.ShapeDtypeStruct((C, share), BF)] * skip_count
        + [jax.ShapeDtypeStruct((INNER, *BLOCK), BF)] * OUTER,
        scratch_shapes=[pltpu.VMEM(shape, kind) for shape, kind in scratch]
        + [
            pltpu.VMEM((C, skip_count * tokens), BF),
            pltpu.SemaphoreType.DMA((len(pieces),)),
            pltpu.VMEM((steps, C, T), BF),
            pltpu.VMEM((steps, C, T), BF),
            pltpu.SemaphoreType.DMA((2 * steps,)),
            pltpu.VMEM((OUTER, INNER, *BLOCK), BF),
            pltpu.SemaphoreType.DMA((OUTER,)),
        ],
        compiler_params=pltpu.CompilerParams(
            dimension_semantics=("arbitrary",), vmem_limit_bytes=42 * 1024 * 1024
        ),
        cost_estimate=pl.CostEstimate(
            flops=flops, bytes_accessed=8_000_000, transcendentals=tokens * 1200
        ),
        name="layer",
    )(
        kept(chosen),
        extents,
        here,
        ranks,
        kept(dec),
        kept(cot),
        bias,
        *packs,
        kept(pieces[0]),
        *pieces[1:3],
        *[kept(piece) for piece in pieces[3:]],
    )


def pack_kernel(mat, vec, chosen, out):
    flat = jnp.concatenate(
        [
            mat[...],
            vec[...],
            jnp.zeros((1, 128 - vec.shape[1]), F32),
            chosen[...].astype(F32),
            jnp.zeros((1, BLOCK[0] * BLOCK[1] - 128 * SIDE_TILE - chosen.shape[1]), F32),
        ],
        axis=1,
    )
    block = jnp.concatenate(
        [flat[:, BLOCK[1] * j : BLOCK[1] * (j + 1)] for j in range(BLOCK[0])], axis=0
    ).astype(BF)
    for n in range(INNER):
        out[n] = block


def skip_sum_kernel(*refs):
    blocks, out = refs[:-1], refs[-1]
    for n in range(INNER):
        out[n] = sum(block[n].astype(F32) for block in blocks).astype(BF)


def split_kernel(here, *refs):
    blocks, (keep, send) = refs[:-2], refs[-2:]
    for n in range(INNER // 2):
        for odd, out in enumerate((keep, send)):
            at = lax.bitwise_xor(here[3], 2 * n + odd)
            out[n] = sum(block[at].astype(F32) for block in blocks).astype(out.dtype)


def halve_kernel(kept, came, keep, send):
    for n in range(kept.shape[0] // 2):
        keep[n] = kept[2 * n] + came[2 * n].astype(F32)
        send[n] = (kept[2 * n + 1] + came[2 * n + 1].astype(F32)).astype(BF)


def slab_sum_kernel(kept, came, mat, vec, tail):
    total = kept[0] + came[0].astype(F32)
    squares = jnp.sum(jnp.sum(total * total, axis=1, keepdims=True), axis=0, keepdims=True)
    flat = jnp.concatenate([total[j : j + 1, :] for j in range(BLOCK[0])], axis=1)
    mat[...] = flat[:, 0 : mat.shape[1]]
    vec[...] = flat[:, 128 * VEC_TILE : 128 * VEC_TILE + vec.shape[1]]
    side = flat[:, 128 * SIDE_TILE : 128 * SIDE_TILE + 128]
    side = jnp.where(iota((1, 128), 1) == TABLE_LANES, squares, side)
    tail[...] = jnp.broadcast_to(side, tail.shape)


def return_kernel(windows, row, here, everyone, after, *refs):
    del after
    received, (out, gathered, source) = refs[:-3], refs[-3:]
    skip_count = len(received)
    per = windows // skip_count
    mix = here[1]
    for d in range(skip_count):
        gathered[d] = received[d][...]
        s = lax.bitwise_xor(mix, d)

        def note(w, rank):
            a = everyone[here[3] * row + s, w]
            mine = lax.div(a, windows) == here[2]

            @pl.when(mine)
            def _():
                source[lax.rem(a, windows)] = d * per + rank

            return rank + mine.astype(jnp.int32)

        lax.fori_loop(0, windows, note, 0)
    left = iota((1, 128), 1) < WTOK
    for n in range(windows // 2):
        halves = []
        for w in (0, 1):
            place_in = source[2 * n + w]
            d, rank = lax.div(place_in, per), lax.rem(place_in, per)
            lanes = pl.ds(pl.multiple_of((rank >> 1) * 128, 128), 128)
            block = gathered[d, :, lanes].astype(F32)
            halves.append(pltpu.roll(block, ((rank + w) & 1) * WTOK, 1))
        out[:, 128 * n : 128 * n + 128] = jnp.where(left, halves[0], halves[1])


VMEM = pl.BlockSpec(memory_space=pltpu.VMEM)
SMEM = pl.BlockSpec(memory_space=pltpu.SMEM)


def small_call(kernel, name, in_specs, outs, operands, scratch=(), moved=1_000_000):
    return pl.pallas_call(
        kernel,
        in_specs=in_specs,
        out_specs=[VMEM] * len(outs),
        out_shape=outs,
        scratch_shapes=scratch,
        compiler_params=pltpu.CompilerParams(vmem_limit_bytes=16 * 1024 * 1024),
        cost_estimate=pl.CostEstimate(flops=moved, bytes_accessed=moved, transcendentals=0),
        name=name,
    )(*operands)


def repack(packed, count):
    pieces, offset = [], 0
    for rows, cols in SHAPES:
        width = rows * cols // packed.shape[0]
        pieces.append(packed[:, offset : offset + width].reshape(count, -1))
        offset += width
    return jnp.concatenate(pieces, axis=1)


def padded(value, width):
    return jnp.pad(value, ((0, 0), (0, width - value.shape[1])))


def adamw_update(master, first, second, average, grad, factor, decay):
    clipped = grad * factor
    first_new = BETA_ONE * first + (1.0 - BETA_ONE) * clipped
    second_new = BETA_TWO * second + (1.0 - BETA_TWO) * clipped * clipped
    first_hat = first_new / (1.0 - BETA_ONE**STEP)
    second_hat = second_new / (1.0 - BETA_TWO**STEP)
    master_new = master - RATE * (first_hat / (jnp.sqrt(second_hat) + ADAM_EPS) + decay * master)
    average_new = EMA_RATE * average + (1.0 - EMA_RATE) * master_new
    return (clipped, master_new, first_new, second_new, average_new, master_new.astype(BF))


def update_kernel(mat_share, vec_share, tail, *refs):
    mats, vecs, tables = refs[0:4], refs[4:8], refs[8:12]
    norm_out, outs = refs[12], refs[13:]
    squares = jnp.sum(tail[:, TABLE_LANES : TABLE_LANES + 1], axis=0, keepdims=True)
    norm = jnp.sqrt(squares)
    norm_out[...] = norm
    factor = CLIP / jnp.maximum(norm, CLIP)
    table = jnp.concatenate([tail[8 * q : 8 * q + 8, 0:TABLE_LANES] for q in range(4)], axis=1)
    work = (
        (mats, mat_share[...], MATRIX_DECAY),
        (vecs, vec_share[...], 0.0),
        (tables, table[0:HEADS, 0:REL], 0.0),
    )
    for n, (group, grad, decay) in enumerate(work):
        results = adamw_update(*[ref[...] for ref in group], grad, factor, decay)
        for ref, value in zip(outs[6 * n : 6 * n + 6], results):
            ref[...] = value


def on_device(
    decoder_tokens,
    skip_tokens,
    cotangent,
    extents,
    assignment,
    mat_master,
    mat_first,
    mat_second,
    mat_average,
    vec_master,
    vec_first,
    vec_second,
    vec_average,
    table_master,
    table_first,
    table_second,
    table_average,
):
    skip_count = lax.axis_size("skip")
    slab_count = lax.axis_size("slab")
    device_count = skip_count * slab_count
    windows = assignment.shape[1]
    mat_width, vec_width = mat_master.shape[1], vec_master.shape[1]
    me = lax.axis_index("skip")
    plain = (skip_count, slab_count) == (OUTER, INNER)

    def swap(value, axis, distance):
        count = lax.axis_size(axis)
        return lax.ppermute(value, axis, [(n, n ^ distance) for n in range(count)])

    def early_call(after):
        return pl.pallas_call(
            functools.partial(early_kernel, skip_count, windows),
            in_specs=[SMEM, VMEM, pl.BlockSpec(memory_space=pl.ANY)],
            out_specs=[VMEM, VMEM],
            out_shape=[
                jax.ShapeDtypeStruct((HEADS, WTOK, 128), F32),
                jax.ShapeDtypeStruct((1, 128), jnp.int32),
            ],
            scratch_shapes=[
                pltpu.VMEM((8, 384), F32),
                pltpu.VMEM((2, 8 * WTOK, 128), F32),
                pltpu.SMEM((skip_count,), jnp.int32),
            ],
            compiler_params=pltpu.CompilerParams(vmem_limit_bytes=16 * 1024 * 1024),
            cost_estimate=pl.CostEstimate(flops=100_000_000, bytes_accessed=1_000_000, transcendentals=0),
            name="early",
        )(kept(assignment[0]), kept(table_master.T), after)

    if plain:
        here = jnp.stack([me, me, me, lax.axis_index("slab")])
        (block,) = small_call(
            pack_kernel,
            "pack",
            [VMEM] * 3,
            [jax.ShapeDtypeStruct((INNER, *BLOCK), BF)],
            (kept(mat_master), kept(vec_master), kept(assignment)),
            moved=100_000,
        )
        own = lax.all_to_all(block, "slab", split_axis=0, concat_axis=0)
        across = swap(skip_tokens, "skip", 2)
        near = swap(skip_tokens, "skip", 1)
        packs_across = swap(own, "skip", 2)
        bias, ranks = early_call(own)
        packs_across, across, bias, ranks = lax.optimization_barrier(
            (packs_across, across, bias, ranks)
        )
        packs = [own, swap(own, "skip", 1), packs_across, swap(packs_across, "skip", 1)]
        pieces = [skip_tokens, near, across, swap(across, "skip", 1)]
    else:
        zero = jnp.zeros_like(me)
        here = jnp.stack([zero, zero, me, zero])
        low = jnp.concatenate([mat_master, vec_master], axis=1).astype(BF)
        low = lax.all_gather(low, ("slab", "skip"), axis=0, tiled=True)
        vec = padded(low[:, mat_width:].reshape(ROWS, -1), 128)
        low = padded(
            jnp.concatenate([repack(low, ROWS), vec], axis=1), BLOCK[0] * BLOCK[1]
        ).reshape(INNER, OUTER, *BLOCK)
        packs = [low[:, n] for n in range(OUTER)]
        pieces = [lax.all_gather(skip_tokens, "skip", axis=0, tiled=True)]
        bias, ranks = early_call(packs[0])

    layer_out, grad_decoder, everyone, *grads = layer_call(
        skip_count,
        assignment[0],
        extents,
        here,
        ranks,
        decoder_tokens.T,
        cotangent.T,
        bias,
        packs,
        [piece.T for piece in pieces],
    )
    grad_picks, grad_packs = grads[:skip_count], grads[skip_count:]

    def returned_call(here, everyone, after, received):
        (grad_skip,) = small_call(
            functools.partial(return_kernel, windows, OUTER),
            "returned",
            [SMEM, SMEM] + [VMEM] * (1 + skip_count),
            [jax.ShapeDtypeStruct((C, windows * WTOK), F32)],
            (here, everyone, after, *received),
            [
                pltpu.VMEM((skip_count, *received[0].shape), BF),
                pltpu.SMEM((windows,), jnp.int32),
            ],
            3_000_000,
        )
        return grad_skip

    shares = [
        jax.ShapeDtypeStruct((1, mat_width), F32),
        jax.ShapeDtypeStruct((1, vec_width), F32),
    ]
    if plain:
        far = swap(grad_packs[3], "skip", 1)
        near = swap(grad_packs[1], "skip", 1)
        (far,) = small_call(
            skip_sum_kernel,
            "core_sum",
            [VMEM] * 2,
            [jax.ShapeDtypeStruct((INNER, *BLOCK), BF)],
            (grad_packs[2], far),
        )
        keep, send = small_call(
            split_kernel,
            "skip_sum",
            [SMEM] + [VMEM] * 3,
            [
                jax.ShapeDtypeStruct((INNER // 2, *BLOCK), F32),
                jax.ShapeDtypeStruct((INNER // 2, *BLOCK), BF),
            ],
            (here, grad_packs[0], near, swap(far, "skip", 2)),
        )
        send, grad_picks = lax.optimization_barrier((send, grad_picks))
        received = [grad_picks[0]] + [swap(grad_picks[d], "skip", d) for d in range(1, OUTER)]
        for distance in (1, 2):
            half = keep.shape[0] // 2
            keep, send = small_call(
                halve_kernel,
                "slab_half",
                [VMEM] * 2,
                [
                    jax.ShapeDtypeStruct((half, *BLOCK), F32),
                    jax.ShapeDtypeStruct((half, *BLOCK), BF),
                ],
                (keep, swap(send, "slab", distance)),
                moved=300_000,
            )
        came, received = lax.optimization_barrier((swap(send, "slab", 4), received))
        mat_share, vec_share, tail = small_call(
            slab_sum_kernel,
            "slab_sum",
            [VMEM] * 2,
            shares + [jax.ShapeDtypeStruct((ROWS, 128), F32)],
            (keep, came),
            moved=300_000,
        )
        grad_skip = returned_call(here, everyone, vec_share, received)
        tail = lax.all_to_all(tail, ("slab", "skip"), split_axis=0, concat_axis=0, tiled=True)
        tail, grad_skip = lax.optimization_barrier((tail, grad_skip))
    else:
        received = list(
            lax.all_to_all(jnp.stack(grad_picks), "skip", split_axis=0, concat_axis=0)
        )
        everyone = lax.all_gather(assignment, "skip", axis=0, tiled=True)
        rows = jnp.stack(grad_packs, axis=1).reshape(ROWS, -1)
        start, side = 128 * VEC_TILE, 128 * SIDE_TILE
        rows = jnp.concatenate(
            [
                repack(rows, device_count),
                rows[:, start : start + VEC // ROWS].reshape(device_count, -1),
                rows[:, side : side + TABLE_LANES].reshape(device_count, -1),
            ],
            axis=1,
        )
        share = lax.psum_scatter(
            rows.astype(F32), ("slab", "skip"), scatter_dimension=0, tiled=True
        )
        mat_share = share[:, :mat_width]
        vec_share = share[:, mat_width : mat_width + vec_width]
        table = lax.all_gather(
            share[:, mat_width + vec_width :], ("slab", "skip"), axis=0, tiled=True
        )
        squares = lax.psum(jnp.sum(share * share), ("slab", "skip")) * (1.0 / ROWS)
        tail = jnp.concatenate(
            [table.reshape(ROWS, TABLE_LANES), jnp.full((ROWS, 128 - TABLE_LANES), squares)],
            axis=1,
        )

    if not plain:
        grad_skip = returned_call(here, everyone, vec_share, received)
    groups = (
        (mat_master, mat_first, mat_second, mat_average),
        (vec_master, vec_first, vec_second, vec_average),
        (table_master.T, table_first.T, table_second.T, table_average.T),
    )
    kinds = [jax.ShapeDtypeStruct((1, 1), F32)]
    for group in groups:
        kinds += [jax.ShapeDtypeStruct(group[0].shape, F32)] * 5
        kinds += [jax.ShapeDtypeStruct(group[0].shape, BF)]
    outs = small_call(
        update_kernel,
        "update",
        [VMEM] * 15,
        kinds,
        (mat_share, vec_share, tail, *groups[0], *groups[1], *groups[2]),
    )
    return (
        layer_out.T,
        grad_decoder.T,
        grad_skip.T,
        outs[0].reshape(()),
        *outs[1:13],
        *[value.T for value in outs[13:]],
    )


def solution(mesh):
    split = P(("slab", "skip"), None)
    return jax.shard_map(
        on_device,
        mesh=mesh,
        in_specs=(split, split, split, P("slab"), P("slab", "skip"))
        + (split,) * 8
        + (P(),) * 4,
        out_specs=(split, split, split, P()) + (split,) * 12 + (P(),) * 6,
        check_vma=False,
    )
```

```python
import functools
import math
import jax
import jax.numpy as jnp
from jax import lax
from jax.experimental import pallas as pl
from jax.experimental.pallas import tpu as pltpu
from jax.sharding import PartitionSpec as P

C = 192
HEADS = 6
HEAD_DIM = 32
HIDDEN_SIZE = 768
WS = 4
DEPTH = 16
STEP = 10
WTOK = 64
REL = 343

EPS = 1e-05
MASK_FILL = -1000000000.0
CLIP = 1.0
BETA_ONE = 0.9
BETA_TWO = 0.999
RATE = 0.3
MATRIX_DECAY = 0.05
ADAM_EPS = 1e-08
EMA_RATE = 0.9

BF = jnp.bfloat16
F32 = jnp.float32
GROUP = 256
GWIN = GROUP // WTOK
T = 1024
GROUPS = T // GROUP
WIDE = 1024
PARTS = T // WIDE
WIN = T // WTOK
QSCALE = HEAD_DIM ** (-0.5)
SHAPES = ((C, C), (C, 2 * C), (C, C), (C, HIDDEN_SIZE), (HIDDEN_SIZE, C))
VLEN = (C, C, C, C, C, C, C, HIDDEN_SIZE, C)
VOFF = tuple(sum(VLEN[:n]) for n in range(len(VLEN)))
VEC = sum(VLEN)
MAT = sum(r * c for r, c in SHAPES)
ROWS = 32
OUTER = 4
INNER = ROWS // OUTER
BLOCK = (16, 896)
BLOCK_TILES = BLOCK[1] // 128
VEC_TILE = MAT // ROWS // 128
SIDE_TILE = VEC_TILE + 1
TABLE_LANES = 8 * 384 // ROWS


def mm(a, b):
    return jnp.dot(a, b, preferred_element_type=F32)


def mm_nt(a, b):
    return lax.dot_general(a, b, (((1,), (1,)), ((), ())), preferred_element_type=F32)


def iota(shape, dim):
    return lax.broadcasted_iota(jnp.int32, shape, dim)


def kept(value):
    return pltpu.with_memory_space_constraint(value, pltpu.HBM)


def both(column, width=256):
    return jnp.concatenate([column] * (width // 128), axis=1)


def place(slot):
    span = 2 * WS - 1
    return ((slot >> 4) * span + ((slot >> 2) & 3)) * span + (slot & 3)


def splits(value):
    high = value.astype(BF)
    rest = value - high.astype(F32)
    middle = rest.astype(BF)
    return high, middle, (rest - middle.astype(F32)).astype(BF)


def normed(value):
    center = value - jnp.sum(value, axis=0, keepdims=True) * (1.0 / C)
    scale = lax.rsqrt(jnp.sum(center * center, axis=0, keepdims=True) * (1.0 / C) + EPS)
    return center * scale, scale


def normed_back(grad_hat, hat, scale):
    mean_grad = jnp.sum(grad_hat, axis=0, keepdims=True) * (1.0 / C)
    mean_both = jnp.sum(grad_hat * hat, axis=0, keepdims=True) * (1.0 / C)
    return scale * (grad_hat - mean_grad - hat * mean_both)


def fold(value):
    return sum(value[:, n : n + 128] for n in range(0, value.shape[1], 128))


def gelu_parts(u):
    t = pl.reciprocal(1.0 + (0.3275911 * 0.5**0.5) * jnp.abs(u), approx=True)
    bell = jnp.exp2((-0.5 * math.log2(math.e)) * (u * u))
    series = 0.5 * 1.061405429
    for factor in (-1.453152027, 1.421413741, -0.284496736, 0.254829592):
        series = series * t + 0.5 * factor
    tail = series * t * bell
    cdf = jnp.where(u >= 0.0, 1.0 - tail, tail)
    return u * cdf, cdf + ((0.5 / math.pi) ** 0.5 * u) * bell


def early_kernel(skip_count, windows, chosen, table, after, bias_s, ranks, tab_s, big, count_s):
    del after
    tab_s[...] = jnp.zeros_like(tab_s)
    tab_s[0:HEADS, 0:REL] = table[...]
    hot = (iota((256, 128), 0) == place(iota((256, 128), 1) & 63)).astype(BF)
    total = None
    for part in splits(tab_s[...]):
        part = part.astype(F32)
        for j in range(WTOK):
            turn = (place(j) - place(WTOK - 1)) % 384
            rolled = pltpu.roll(part, turn, 1) if turn else part
            big[0, 8 * j : 8 * j + 8, :] = rolled[:, 0:128]
            big[1, 8 * j : 8 * j + 8, :] = rolled[:, 128:256]
        product = mm(big[0].astype(BF), hot[0:128]) + mm(big[1].astype(BF), hot[128:256])
        total = product if total is None else total + product
    big[0] = total
    for h in range(HEADS):
        bias_s[h] = big[0, pl.ds(h, WTOK, stride=8), :]
    for e in range(skip_count):
        count_s[e] = 0

    def note(w, rank_row):
        owner = lax.div(chosen[w], windows)
        rank = count_s[owner]
        count_s[owner] = rank + 1
        return jnp.where(iota((1, 128), 1) == w, rank, rank_row)

    ranks[...] = lax.fori_loop(0, windows, note, jnp.zeros((1, 128), jnp.int32))


def layer_kernel(
    skip_count,
    windows,
    piece_count,
    chosen,
    extents,
    here,
    ranks,
    dec_all,
    cot_all,
    bias_s,
    *refs,
):
    step = pl.program_id(0)
    packs, refs = refs[:OUTER], refs[OUTER:]
    pieces, refs = refs[:piece_count], refs[piece_count:]
    layer_out, grad_dec, everyone, *refs = refs
    grad_picks, refs = refs[:skip_count], refs[skip_count:]
    grad_packs, refs = refs[:OUTER], refs[OUTER:]
    (
        pick_s,
        big,
        vcol,
        wq,
        wqt,
        wkv,
        wkvt,
        wo,
        wot,
        w1,
        w1t,
        w2,
        w2t,
        xn_s,
        sn_s,
        hn_s,
        o_s,
        gl_s,
        du_s,
        q_s,
        qbd_s,
        kst_s,
        vst_s,
        kcat_s,
        vcat_s,
        pf_s,
        pb_s,
        ds_s,
        da_s,
        do_s,
        dm_s,
        u_s,
        ga_s,
        gh_s,
        gs_s,
        dq_s,
        dkv_s,
        n1_s,
        n2_s,
        n3_s,
        x1_s,
        gds_s,
        aq,
        akv,
        ao,
        a1,
        a2,
        ln_s,
        slab,
        slab_sem,
        dec_s,
        cot_s,
        token_sem,
        pack_s,
        pack_sem,
    ) = refs
    dec, cot = dec_s.at[step], cot_s.at[step]
    stage, block_s = u_s, ga_s
    my_skip, mix = here[0], here[1]
    lane = iota((1, 128), 1)
    left = lane < WTOK

    def tile_of(number):
        j, n = divmod(number, BLOCK_TILES)
        return n, pl.ds(j, ROWS, stride=BLOCK[0]), slice(None)


    def token_copies(n):
        lanes = slice(T * n, T * n + T)
        return [
            pltpu.make_async_copy(dec_all.at[:, lanes], dec_s.at[n], token_sem.at[2 * n]),
            pltpu.make_async_copy(cot_all.at[:, lanes], cot_s.at[n], token_sem.at[2 * n + 1]),
        ]

    for n in range(1, windows // WIN):

        @pl.when(step == n)
        def _(n=n):
            for copy in token_copies(n):
                copy.wait()

    @pl.when(step == 0)
    def _():
        copies = token_copies(0) + [
            pltpu.make_async_copy(
                piece, slab.at[:, n * piece.shape[1] : (n + 1) * piece.shape[1]], slab_sem.at[n]
            )
            for n, piece in enumerate(pieces)
        ]
        pack_copies = [
            pltpu.make_async_copy(packs[n], pack_s.at[n], pack_sem.at[n]) for n in range(OUTER)
        ]
        for copy in pack_copies + copies + [copy for n in range(1, windows // WIN) for copy in token_copies(n)]:
            copy.start()
        for ref in (gds_s, aq, akv, ao, a1, a2, ln_s):
            ref[...] = jnp.zeros_like(ref)
        for ref, rows in ((xn_s, C), (sn_s, C), (hn_s, C), (o_s, C), (gl_s, HIDDEN_SIZE)):
            ref[rows : rows + 16, :] = jnp.ones((16, T), BF)
        for copy in pack_copies:
            copy.wait()
        for outer in range(OUTER):
            for inner in range(INNER):
                k = inner * OUTER + lax.bitwise_xor(my_skip, outer)
                rows = pl.ds(pl.multiple_of(k * BLOCK[0], BLOCK[0]), BLOCK[0])
                for n in range(BLOCK_TILES):
                    block_s[n, rows, :] = pack_s[outer, inner, :, 128 * n : 128 * n + 128].astype(
                        F32
                    )
        offset = 0
        for (rows, cols), plain, turned in zip(
            SHAPES, (wq, wkv, wo, w1, w2), (wqt, wkvt, wot, w1t, w2t)
        ):
            per = rows // ROWS
            tiles = -(-cols // 128)
            for a in range(per):
                first, shift = divmod(offset + a * cols, 128)
                for n in range(tiles):
                    piece = block_s[tile_of(first + n)]
                    if shift and n + 1 < tiles:
                        after = block_s[tile_of(first + n + 1)]
                        piece = jnp.concatenate([piece[:, shift:], after[:, :shift]], axis=1)
                    elif shift:
                        piece = pltpu.roll(piece, 128 - shift, 1)
                    stage[n, pl.ds(a, ROWS, stride=per), :] = piece
            for n in range(tiles):
                width = min(128, cols - 128 * n)
                value = stage[n, 0:rows, :].astype(BF)
                plain[:, 128 * n : 128 * n + width] = value[:, 0:width]
                turned[128 * n : 128 * n + width, :] = jnp.transpose(value)[0:width]
            offset += per * cols
        side = block_s[tile_of(VEC_TILE)]
        per = VEC // ROWS
        vec = jnp.concatenate([side[k : k + 1, 0:per] for k in range(ROWS)], axis=1)
        vcol[...] = jnp.transpose(jnp.broadcast_to(vec, (128, VEC)))
        side = block_s[tile_of(SIDE_TILE)]
        everyone[...] = side.astype(jnp.int32)
        for copy in copies:
            copy.wait()

    def column(number, first=0, last=None):
        start = VOFF[number]
        return vcol[start + first : start + (VLEN[number] if last is None else last), :]

    chunks = [slice(128 * c, 128 * c + 128) for c in range(T // 128)]
    tiles = [slice(GROUP * g, GROUP * g + GROUP) for g in range(GROUPS)]
    wides = [slice(WIDE * g, WIDE * g + WIDE) for g in range(PARTS)]
    per_wide = WIDE // 128
    groups_wide = WIDE // GROUP
    layers, valid = [], []
    for c in range(len(chunks)):
        deep = [
            jnp.clip(extents[0] - WS * (chosen[step * WIN + 2 * c + w] & 3), 0, WS) for w in (0, 1)
        ]
        layers.append(jnp.where(left, deep[0], deep[1]))
        valid.append(jnp.where((lane & 63) >> 4 < layers[c], 1.0, 0.0))

    scale_one, scale_two, scale_three = {}, {}, {}

    def stacks(rows, g, stack_ref, cat_ref):
        turned = pltpu.roll(rows, WTOK, 1)
        first, second = rows[:, 0:128], rows[:, 128:256]
        mixed, middle = turned[:, 0:128], turned[:, 128:256]
        at_left = (first, middle, second, mixed)
        at_right = (mixed, first, middle, second)
        for h in range(0, HEADS, 2):
            n = g * HEADS + h
            at = slice(HEAD_DIM * h, HEAD_DIM * h + HEAD_DIM)
            after = slice(HEAD_DIM * h + HEAD_DIM, HEAD_DIM * h + 2 * HEAD_DIM)
            pieces = []
            for w in range(GWIN):
                to = slice(HEAD_DIM * w, HEAD_DIM * w + HEAD_DIM)
                stack_ref[n, to, :] = at_left[w][at, 0:WTOK]
                stack_ref[n + 1, to, :] = at_left[w][after, 0:WTOK]
                pieces.append(jnp.where(left, at_left[w][at], at_right[w][after]))
            pair = jnp.transpose(jnp.concatenate(pieces, axis=0))
            cat_ref[n] = pair[0:WTOK]
            cat_ref[n + 1] = pair[WTOK:]

    window_mask = [
        (iota((HEAD_DIM, GROUP), 1) >> 6 == w).astype(F32).astype(BF) for w in range(GWIN)
    ]

    def spread(rows):
        return jnp.concatenate([rows * mask for mask in window_mask], axis=0)

    def own(stacked, probs):
        parts = []
        for n in range(GWIN // 2):
            cut = mm(
                stacked[2 * HEAD_DIM * n : 2 * HEAD_DIM * (n + 1)],
                probs[:, 128 * n : 128 * n + 128],
            )
            parts.append(jnp.where(left, cut[0:HEAD_DIM], cut[HEAD_DIM:]))
        return jnp.concatenate(parts, axis=1)

    def unstack(product):
        low = product.astype(BF)
        return jnp.concatenate(
            [low[HEAD_DIM * w : HEAD_DIM * w + HEAD_DIM] for w in range(GWIN)], axis=1
        )

    def filled(g):
        return jnp.concatenate(
            [
                jnp.concatenate(
                    [
                        jnp.broadcast_to(jnp.where(layers[c] > d, 0.0, MASK_FILL), (WS * WS, 128))
                        for d in range(WS)
                    ],
                    axis=0,
                )
                for c in (2 * g, 2 * g + 1)
            ],
            axis=1,
        )

    def place_of(n):
        g, h = divmod(n, HEADS)
        return slice(HEAD_DIM * h, HEAD_DIM * h + HEAD_DIM), tiles[g]

    def softmax(n, scores, fill):
        scores = scores + both(bias_s[n % HEADS]) + fill
        powers = jnp.exp(scores - jnp.max(scores, axis=0, keepdims=True))
        probs = powers * pl.reciprocal(jnp.sum(powers, axis=0, keepdims=True), approx=True)
        pf_s[n] = probs
        pb_s[n] = probs.astype(BF)

    def softmax_back(n, grad_probs):
        probs = pf_s[n]
        grad_scores = (
            probs * (grad_probs - jnp.sum(probs * grad_probs, axis=0, keepdims=True))
        ).astype(BF)
        gds_s[n % HEADS] += fold(grad_scores.astype(F32))
        ds_s[n] = grad_scores

    def forward(g):
        lanes = wides[g]
        for c in range(per_wide * g, per_wide * (g + 1)):
            cut = chunks[c]
            hat, scale_one[c] = normed(dec[:, cut].astype(F32))
            n1_s[:, cut] = hat
            xn_s[0:C, cut] = (hat * column(0) + column(1)).astype(BF)
            yield 130
            halves = []
            for w in (0, 1):
                a = chosen[step * WIN + 2 * c + w]
                at = lax.bitwise_xor(a, mix * windows) >> 1
                part = slab[:, pl.ds(pl.multiple_of(at * 128, 128), 128)]
                halves.append(pltpu.roll(part, ((a + w) & 1) * WTOK, 1))
            hat, scale_two[c] = normed(jnp.where(left, halves[0], halves[1]).astype(F32))
            n2_s[:, cut] = hat
            sn_s[0:C, cut] = (hat * column(0) + column(1)).astype(BF)
            yield 160
        query = mm(wqt[...], xn_s[0:C, lanes])
        pair = mm(wkvt[...], sn_s[0:C, lanes])
        q_s[:, lanes] = ((query + both(column(2), WIDE)) * QSCALE).astype(BF)
        for c in range(per_wide * g, per_wide * (g + 1)):
            dm_s[:, chunks[c]] = (cot[:, chunks[c]].astype(F32) * valid[c]).astype(BF)
        yield 250
        first, units = g * groups_wide * HEADS, groups_wide * HEADS
        for n in range(first, first + units):
            qbd_s[n] = spread(q_s[place_of(n)])
        keys = pair[0:C].astype(BF)
        values = (pair[C:] + both(column(3), WIDE)).astype(BF)
        for k in range(groups_wide):
            cut = slice(GROUP * k, GROUP * k + GROUP)
            stacks(keys[:, cut], groups_wide * g + k, kst_s, kcat_s)
            yield 250
            stacks(values[:, cut], groups_wide * g + k, vst_s, vcat_s)
            yield 250
        scores = {}
        for n in range(first, first + units + 2):
            if n < first + units:
                scores[n] = mm(kcat_s[n], qbd_s[n])
            if n >= first + 2:
                o_s[place_of(n - 2)] = own(vst_s[n - 2], pb_s[n - 2]).astype(BF)
            if first + 1 <= n <= first + units:
                if (n - 1) % HEADS == 0:
                    fill = filled((n - 1) // HEADS)
                softmax(n - 1, scores.pop(n - 1), fill)
            yield 180
        product = mm(w2[...], dm_s[:, lanes])
        for c in range(per_wide):
            ga_s[per_wide * g + c] = product[:, 128 * c : 128 * c + 128]
        yield 300
        x1_s[:, lanes] = mm(wot[...], o_s[0:C, lanes])
        yield 150
        for c in range(per_wide * g, per_wide * (g + 1)):
            cut = chunks[c]
            middle = dec[:, cut].astype(F32) + x1_s[:, cut] + column(4)
            x1_s[:, cut] = middle
            hat, scale_three[c] = normed(middle)
            n3_s[:, cut] = hat
            hn_s[0:C, cut] = (hat * column(5) + column(6)).astype(BF)
            yield 150

    def feed(g):
        lanes = wides[g]
        product = mm(w1t[...], hn_s[0:C, lanes])
        for c in range(per_wide):
            u_s[per_wide * g + c] = product[:, 128 * c : 128 * c + 128]
        yield 300
        piece = 32
        for start in range(0, HIDDEN_SIZE, piece):
            rows = slice(start, start + piece)
            for c in range(per_wide * g, per_wide * (g + 1)):
                active, slope = gelu_parts(u_s[c, rows, :] + column(7, start, start + piece))
                gl_s[rows, chunks[c]] = active.astype(BF)
                du_s[rows, chunks[c]] = (ga_s[c, rows, :] * slope).astype(BF)
            yield 35 * piece // 16
        gh_s[:, lanes] = mm(w1[...], du_s[:, lanes])
        yield 450
        mlp = mm(w2t[...], gl_s[0:HIDDEN_SIZE, lanes]) + both(column(8), WIDE)
        layer_out[:, lanes] = (
            jnp.concatenate(valid[per_wide * g : per_wide * (g + 1)], axis=1) * (x1_s[:, lanes] + mlp)
        ).astype(BF)
        yield 500
        for c in range(per_wide * g, per_wide * (g + 1)):
            cut = chunks[c]
            grad, hat = gh_s[:, cut], n3_s[:, cut]
            ln_s[1] += grad * hat
            back = normed_back(grad * column(5), hat, scale_three[c])
            grad_middle = cot[:, cut].astype(F32) * valid[c] + back
            x1_s[:, cut] = grad_middle
            da_s[:, cut] = grad_middle.astype(BF)
            yield 170
        do_s[:, lanes] = mm(wo[...], da_s[:, lanes]).astype(BF)
        yield 150

    def backward(g):
        lanes = wides[g]
        first, units = g * groups_wide * HEADS, groups_wide * HEADS
        spreads, grads = {}, {}
        for n in range(first, first + units + 2):
            if n < first + units:
                lanes = place_of(n)[1]
                at, _ = place_of(n)
                spreads[n] = spread(do_s[at, lanes])
                grads[n] = mm(vcat_s[n], spreads[n])
                dkv_s[at.start + C : at.stop + C, lanes] = unstack(
                    mm_nt(spreads.pop(n), pb_s[n])
                )
            if n >= first + 2:
                at, lanes = place_of(n - 2)
                dq_s[at, lanes] = own(kst_s[n - 2], ds_s[n - 2]).astype(BF)
                dkv_s[at, lanes] = unstack(mm_nt(qbd_s[n - 2], ds_s[n - 2]))
            if first + 1 <= n <= first + units:
                softmax_back(n - 1, grads.pop(n - 1))
            yield 340
        lanes = wides[g]
        gh_s[:, lanes] = mm(wq[...], dq_s[:, lanes])
        yield 150
        gs_s[:, lanes] = mm(wkv[...], dkv_s[:, lanes])
        yield 300
        for c in range(per_wide * g, per_wide * (g + 1)):
            cut = chunks[c]
            grad, hat = gh_s[:, cut] * QSCALE, n1_s[:, cut]
            ln_s[0] += grad * hat
            grad_dec[:, cut] = x1_s[:, cut] + normed_back(grad * column(0), hat, scale_one[c])
            yield 170
            grad, hat = gs_s[:, cut], n2_s[:, cut]
            ln_s[0] += grad * hat
            back = normed_back(grad * column(0), hat, scale_two[c]).astype(BF)
            for w in (0, 1):
                a = chosen[step * WIN + 2 * c + w]
                rank = ranks[0, step * WIN + 2 * c + w]
                owner = lax.bitwise_xor(lax.div(a, windows), mix)
                half = pltpu.roll(back, ((rank + w) & 1) * WTOK, 1)
                at = pl.ds(pl.multiple_of((rank >> 1) * 128, 128), 128)
                pick_s[owner, :, at] = jnp.where(
                    lane >> 6 == (rank & 1), half, pick_s[owner, :, at]
                )
            yield 250

    def add(ref, product):
        for n in range(ref.shape[0]):
            width = min(128, product.shape[1] - 128 * n)
            ref[n, :, 0:width] += product[:, 128 * n : 128 * n + width]

    def early_sums():
        add(a2, mm_nt(gl_s[...], dm_s[...]))
        yield 1200
        add(a1, mm_nt(hn_s[...], du_s[...]))
        yield 1200
        add(ao, mm_nt(o_s[...], da_s[...]))
        yield 400

    costs = {forward: 3500, feed: 3450, backward: 4000, early_sums: 2800}

    def interleaved(parts):
        running = [[part(*args), 0, costs[part]] for part, *args in parts]
        while running:
            now = min(running, key=lambda entry: entry[1] / entry[2])
            try:
                now[1] += next(now[0])
            except StopIteration:
                running.remove(now)

    for slot in range(PARTS + 2):
        parts = [
            (part, slot - lag)
            for lag, part in enumerate((forward, feed, backward))
            if 0 <= slot - lag < PARTS
        ]
        if slot == PARTS + 1:
            parts.append((early_sums,))
        interleaved(parts)
    add(aq, mm_nt(xn_s[...], dq_s[...]))
    add(akv, mm_nt(sn_s[...], dkv_s[...]))

    @pl.when(step == pl.num_programs(0) - 1)
    def _():
        offset = 0
        for number, ((rows, cols), ref) in enumerate(zip(SHAPES, (aq, akv, ao, a1, a2))):
            per = rows // ROWS
            tiles = -(-cols // 128)
            joined = 2 if cols % 128 else 1
            for a in range(0, per, joined):
                value = jnp.concatenate(
                    [
                        jnp.concatenate(
                            [ref[n, pl.ds(b, ROWS, stride=per), :] for n in range(tiles)], axis=1
                        )[:, 0:cols]
                        for b in range(a, a + joined)
                    ],
                    axis=1,
                )
                if number == 0:
                    value = value * QSCALE
                for n in range(joined * cols // 128):
                    block_s[tile_of((offset + a * cols) // 128 + n)] = value[
                        :, 128 * n : 128 * n + 128
                    ]
            offset += per * cols
        rows = [jnp.sum(jnp.transpose(ln_s[n]), axis=0, keepdims=True) for n in range(2)]
        def last_row(ref, at):
            row = [ref[n, at : at + 1, :] for n in range(ref.shape[0])]
            return jnp.concatenate(row, axis=1)

        def through(row, weight):
            row = jnp.broadcast_to(row, (16, row.shape[1]))
            return sum(mm_nt(part, weight[...]) for part in splits(row))[0:1]

        query_row = last_row(aq, C)[:, 0:C]
        pair_row, upper_row = last_row(akv, C), last_row(a1, C)
        flat = jnp.concatenate(
            [
                rows[0],
                through(query_row, wq) * QSCALE + through(pair_row, wkv),
                last_row(aq, C)[:, 0:C] * QSCALE,
                last_row(akv, C)[:, C:],
                last_row(ao, C)[:, 0:C],
                rows[1],
                through(upper_row, w1),
                last_row(a1, C),
                last_row(a2, HIDDEN_SIZE)[:, 0:C],
            ],
            axis=1,
        )
        big[0] = jnp.zeros((8 * WTOK, 128), F32)
        for h in range(HEADS):
            big[0, pl.ds(h, WTOK, stride=8), :] = gds_s[h]
        hot = (iota((128, 256), 1) == place(iota((128, 256), 0) & 63)).astype(BF)
        total = sum(mm(part, hot) for part in splits(big[0]))
        big[0] = total[:, 0:128]
        big[1] = total[:, 128:256]
        result = jnp.zeros((8, 384), F32)
        for j in range(WTOK):
            row = jnp.concatenate(
                [
                    big[0, 8 * j : 8 * j + 8, :],
                    big[1, 8 * j : 8 * j + 8, :],
                    jnp.zeros((8, 128), F32),
                ],
                axis=1,
            )
            turn = (place(WTOK - 1) - place(j)) % 384
            result = result + (pltpu.roll(row, turn, 1) if turn else row)
        per = VEC // ROWS
        block_s[tile_of(VEC_TILE)] = jnp.concatenate(
            [
                jnp.concatenate([flat[:, per * k : per * k + per] for k in range(ROWS)], axis=0),
                jnp.zeros((ROWS, 128 - per), F32),
            ],
            axis=1,
        )
        count = TABLE_LANES
        block_s[tile_of(SIDE_TILE)] = jnp.concatenate(
            [
                jnp.concatenate([result[:, count * n : count * n + count] for n in range(4)], axis=0),
                jnp.zeros((ROWS, 128 - count), F32),
            ],
            axis=1,
        )
        for number in range(SIDE_TILE + 1, BLOCK[0] * BLOCK_TILES):
            block_s[tile_of(number)] = jnp.zeros((ROWS, 128), F32)
        for outer in range(OUTER):
            for inner in range(INNER):
                k = inner * OUTER + lax.bitwise_xor(my_skip, outer)
                rows = pl.ds(pl.multiple_of(k * BLOCK[0], BLOCK[0]), BLOCK[0])
                for n in range(BLOCK_TILES):
                    grad_packs[outer][inner, :, 128 * n : 128 * n + 128] = block_s[
                        n, rows, :
                    ].astype(BF)
        for n in range(skip_count):
            grad_picks[n][...] = pick_s[n]


def layer_call(skip_count, chosen, extents, here, ranks, dec, cot, bias, packs, pieces):
    tokens = dec.shape[1]
    windows = tokens // WTOK
    steps = tokens // T
    share = tokens // skip_count
    block = pl.BlockSpec((C, T), lambda i: (0, i))
    smem = pl.BlockSpec(memory_space=pltpu.SMEM)
    hbm = pl.BlockSpec(memory_space=pltpu.HBM)

    def whole(shape):
        return pl.BlockSpec(shape, lambda i: (0,) * len(shape))

    scratch = [
        ((skip_count, C, share), BF),
        ((2, 8 * WTOK, 128), F32),
        ((VEC, 128), F32),
        ((C, C), BF),
        ((C, C), BF),
        ((C, 2 * C), BF),
        ((2 * C, C), BF),
        ((C, C), BF),
        ((C, C), BF),
        ((C, HIDDEN_SIZE), BF),
        ((HIDDEN_SIZE, C), BF),
        ((HIDDEN_SIZE, C), BF),
        ((C, HIDDEN_SIZE), BF),
        ((C + 16, T), BF),
        ((C + 16, T), BF),
        ((C + 16, T), BF),
        ((C + 16, T), BF),
        ((HIDDEN_SIZE + 16, T), BF),
        ((HIDDEN_SIZE, T), BF),
        ((C, T), BF),
        ((GROUPS * HEADS, GWIN * HEAD_DIM, GROUP), BF),
        ((GROUPS * HEADS, GWIN * HEAD_DIM, WTOK), BF),
        ((GROUPS * HEADS, GWIN * HEAD_DIM, WTOK), BF),
        ((GROUPS * HEADS, WTOK, GWIN * HEAD_DIM), BF),
        ((GROUPS * HEADS, WTOK, GWIN * HEAD_DIM), BF),
        ((GROUPS * HEADS, WTOK, GROUP), F32),
        ((GROUPS * HEADS, WTOK, GROUP), BF),
        ((GROUPS * HEADS, WTOK, GROUP), BF),
        ((C, T), BF),
        ((C, T), BF),
        ((C, T), BF),
        ((T // 128, HIDDEN_SIZE, 128), F32),
        ((T // 128, HIDDEN_SIZE, 128), F32),
        ((C, T), F32),
        ((C, T), F32),
        ((C, T), BF),
        ((2 * C, T), BF),
        ((C, T), F32),
        ((C, T), F32),
        ((C, T), F32),
        ((C, T), F32),
        ((HEADS, WTOK, 128), F32),
        ((2, C + 16, 128), F32),
        ((3, C + 16, 128), F32),
        ((2, C + 16, 128), F32),
        ((6, C + 16, 128), F32),
        ((2, HIDDEN_SIZE + 16, 128), F32),
        ((2, C, 128), F32),
    ]
    flops = 2 * tokens * (3 * 442368 + 12 * WTOK * C)
    return pl.pallas_call(
        functools.partial(layer_kernel, skip_count, windows, len(pieces)),
        grid=(steps,),
        in_specs=[smem, smem, smem, smem, hbm, hbm, whole(bias.shape)]
        + [pl.BlockSpec(memory_space=pl.ANY)] * (OUTER + len(pieces)),
        out_specs=[block, block, whole((ROWS, 128))]
        + [whole((C, share))] * skip_count
        + [whole((INNER, *BLOCK))] * OUTER,
        out_shape=[
            jax.ShapeDtypeStruct((C, tokens), BF),
            jax.ShapeDtypeStruct((C, tokens), F32),
            jax.ShapeDtypeStruct((ROWS, 128), jnp.int32),
        ]
        + [jax.ShapeDtypeStruct((C, share), BF)] * skip_count
        + [jax.ShapeDtypeStruct((INNER, *BLOCK), BF)] * OUTER,
        scratch_shapes=[pltpu.VMEM(shape, kind) for shape, kind in scratch]
        + [
            pltpu.VMEM((C, skip_count * tokens), BF),
            pltpu.SemaphoreType.DMA((len(pieces),)),
            pltpu.VMEM((steps, C, T), BF),
            pltpu.VMEM((steps, C, T), BF),
            pltpu.SemaphoreType.DMA((2 * steps,)),
            pltpu.VMEM((OUTER, INNER, *BLOCK), BF),
            pltpu.SemaphoreType.DMA((OUTER,)),
        ],
        compiler_params=pltpu.CompilerParams(
            dimension_semantics=("arbitrary",), vmem_limit_bytes=50 * 1024 * 1024
        ),
        cost_estimate=pl.CostEstimate(
            flops=flops, bytes_accessed=8_000_000, transcendentals=tokens * 1200
        ),
        name="layer",
    )(
        kept(chosen),
        extents,
        here,
        ranks,
        kept(dec),
        kept(cot),
        bias,
        *packs,
        kept(pieces[0]),
        *pieces[1:3],
        *[kept(piece) for piece in pieces[3:]],
    )


def pack_kernel(mat, vec, chosen, out):
    flat = jnp.concatenate(
        [
            mat[...],
            vec[...],
            jnp.zeros((1, 128 - vec.shape[1]), F32),
            chosen[...].astype(F32),
            jnp.zeros((1, BLOCK[0] * BLOCK[1] - 128 * SIDE_TILE - chosen.shape[1]), F32),
        ],
        axis=1,
    )
    block = jnp.concatenate(
        [flat[:, BLOCK[1] * j : BLOCK[1] * (j + 1)] for j in range(BLOCK[0])], axis=0
    ).astype(BF)
    for n in range(INNER):
        out[n] = block


def skip_sum_kernel(*refs):
    blocks, out = refs[:-1], refs[-1]
    for n in range(INNER):
        out[n] = sum(block[n].astype(F32) for block in blocks).astype(BF)


def split_kernel(here, *refs):
    blocks, (keep, send) = refs[:-2], refs[-2:]
    for n in range(INNER // 2):
        for odd, out in enumerate((keep, send)):
            at = lax.bitwise_xor(here[3], 2 * n + odd)
            out[n] = sum(block[at].astype(F32) for block in blocks).astype(out.dtype)


def halve_kernel(kept, came, keep, send):
    for n in range(kept.shape[0] // 2):
        keep[n] = kept[2 * n] + came[2 * n].astype(F32)
        send[n] = (kept[2 * n + 1] + came[2 * n + 1].astype(F32)).astype(BF)


def slab_sum_kernel(kept, came, mat, vec, tail):
    total = kept[0] + came[0].astype(F32)
    squares = jnp.sum(jnp.sum(total * total, axis=1, keepdims=True), axis=0, keepdims=True)
    flat = jnp.concatenate([total[j : j + 1, :] for j in range(BLOCK[0])], axis=1)
    mat[...] = flat[:, 0 : mat.shape[1]]
    vec[...] = flat[:, 128 * VEC_TILE : 128 * VEC_TILE + vec.shape[1]]
    side = flat[:, 128 * SIDE_TILE : 128 * SIDE_TILE + 128]
    side = jnp.where(iota((1, 128), 1) == TABLE_LANES, squares, side)
    tail[...] = jnp.broadcast_to(side, tail.shape)


def return_kernel(windows, row, here, everyone, after, *refs):
    del after
    received, (out, gathered, source) = refs[:-3], refs[-3:]
    skip_count = len(received)
    per = windows // skip_count
    mix = here[1]
    for d in range(skip_count):
        gathered[d] = received[d][...]
        s = lax.bitwise_xor(mix, d)

        def note(w, rank):
            a = everyone[here[3] * row + s, w]
            mine = lax.div(a, windows) == here[2]

            @pl.when(mine)
            def _():
                source[lax.rem(a, windows)] = d * per + rank

            return rank + mine.astype(jnp.int32)

        lax.fori_loop(0, windows, note, 0)
    left = iota((1, 128), 1) < WTOK
    for n in range(windows // 2):
        halves = []
        for w in (0, 1):
            place_in = source[2 * n + w]
            d, rank = lax.div(place_in, per), lax.rem(place_in, per)
            lanes = pl.ds(pl.multiple_of((rank >> 1) * 128, 128), 128)
            block = gathered[d, :, lanes].astype(F32)
            halves.append(pltpu.roll(block, ((rank + w) & 1) * WTOK, 1))
        out[:, 128 * n : 128 * n + 128] = jnp.where(left, halves[0], halves[1])


VMEM = pl.BlockSpec(memory_space=pltpu.VMEM)
SMEM = pl.BlockSpec(memory_space=pltpu.SMEM)


def small_call(kernel, name, in_specs, outs, operands, scratch=(), moved=1_000_000):
    return pl.pallas_call(
        kernel,
        in_specs=in_specs,
        out_specs=[VMEM] * len(outs),
        out_shape=outs,
        scratch_shapes=scratch,
        compiler_params=pltpu.CompilerParams(vmem_limit_bytes=16 * 1024 * 1024),
        cost_estimate=pl.CostEstimate(flops=moved, bytes_accessed=moved, transcendentals=0),
        name=name,
    )(*operands)


def repack(packed, count):
    pieces, offset = [], 0
    for rows, cols in SHAPES:
        width = rows * cols // packed.shape[0]
        pieces.append(packed[:, offset : offset + width].reshape(count, -1))
        offset += width
    return jnp.concatenate(pieces, axis=1)


def padded(value, width):
    return jnp.pad(value, ((0, 0), (0, width - value.shape[1])))


def adamw_update(master, first, second, average, grad, factor, decay):
    clipped = grad * factor
    first_new = BETA_ONE * first + (1.0 - BETA_ONE) * clipped
    second_new = BETA_TWO * second + (1.0 - BETA_TWO) * clipped * clipped
    first_hat = first_new / (1.0 - BETA_ONE**STEP)
    second_hat = second_new / (1.0 - BETA_TWO**STEP)
    master_new = master - RATE * (first_hat / (jnp.sqrt(second_hat) + ADAM_EPS) + decay * master)
    average_new = EMA_RATE * average + (1.0 - EMA_RATE) * master_new
    return (clipped, master_new, first_new, second_new, average_new, master_new.astype(BF))


def update_kernel(mat_share, vec_share, tail, *refs):
    mats, vecs, tables = refs[0:4], refs[4:8], refs[8:12]
    norm_out, outs = refs[12], refs[13:]
    squares = jnp.sum(tail[:, TABLE_LANES : TABLE_LANES + 1], axis=0, keepdims=True)
    norm = jnp.sqrt(squares)
    norm_out[...] = norm
    factor = CLIP / jnp.maximum(norm, CLIP)
    table = jnp.concatenate([tail[8 * q : 8 * q + 8, 0:TABLE_LANES] for q in range(4)], axis=1)
    work = (
        (mats, mat_share[...], MATRIX_DECAY),
        (vecs, vec_share[...], 0.0),
        (tables, table[0:HEADS, 0:REL], 0.0),
    )
    for n, (group, grad, decay) in enumerate(work):
        results = adamw_update(*[ref[...] for ref in group], grad, factor, decay)
        for ref, value in zip(outs[6 * n : 6 * n + 6], results):
            ref[...] = value


def on_device(
    decoder_tokens,
    skip_tokens,
    cotangent,
    extents,
    assignment,
    mat_master,
    mat_first,
    mat_second,
    mat_average,
    vec_master,
    vec_first,
    vec_second,
    vec_average,
    table_master,
    table_first,
    table_second,
    table_average,
):
    skip_count = lax.axis_size("skip")
    slab_count = lax.axis_size("slab")
    device_count = skip_count * slab_count
    windows = assignment.shape[1]
    mat_width, vec_width = mat_master.shape[1], vec_master.shape[1]
    me = lax.axis_index("skip")
    plain = (skip_count, slab_count) == (OUTER, INNER)

    def swap(value, axis, distance):
        count = lax.axis_size(axis)
        return lax.ppermute(value, axis, [(n, n ^ distance) for n in range(count)])

    def early_call(after):
        return pl.pallas_call(
            functools.partial(early_kernel, skip_count, windows),
            in_specs=[SMEM, VMEM, pl.BlockSpec(memory_space=pl.ANY)],
            out_specs=[VMEM, VMEM],
            out_shape=[
                jax.ShapeDtypeStruct((HEADS, WTOK, 128), F32),
                jax.ShapeDtypeStruct((1, 128), jnp.int32),
            ],
            scratch_shapes=[
                pltpu.VMEM((8, 384), F32),
                pltpu.VMEM((2, 8 * WTOK, 128), F32),
                pltpu.SMEM((skip_count,), jnp.int32),
            ],
            compiler_params=pltpu.CompilerParams(vmem_limit_bytes=16 * 1024 * 1024),
            cost_estimate=pl.CostEstimate(flops=100_000_000, bytes_accessed=1_000_000, transcendentals=0),
            name="early",
        )(kept(assignment[0]), kept(table_master.T), after)

    if plain:
        here = jnp.stack([me, me, me, lax.axis_index("slab")])
        (block,) = small_call(
            pack_kernel,
            "pack",
            [VMEM] * 3,
            [jax.ShapeDtypeStruct((INNER, *BLOCK), BF)],
            (kept(mat_master), kept(vec_master), kept(assignment)),
            moved=100_000,
        )
        own = lax.all_to_all(block, "slab", split_axis=0, concat_axis=0)
        across = swap(skip_tokens, "skip", 2)
        near = swap(skip_tokens, "skip", 1)
        packs_across = swap(own, "skip", 2)
        bias, ranks = early_call(own)
        packs_across, across, bias, ranks = lax.optimization_barrier(
            (packs_across, across, bias, ranks)
        )
        packs = [own, swap(own, "skip", 1), packs_across, swap(packs_across, "skip", 1)]
        pieces = [skip_tokens, near, across, swap(across, "skip", 1)]
    else:
        zero = jnp.zeros_like(me)
        here = jnp.stack([zero, zero, me, zero])
        low = jnp.concatenate([mat_master, vec_master], axis=1).astype(BF)
        low = lax.all_gather(low, ("slab", "skip"), axis=0, tiled=True)
        vec = padded(low[:, mat_width:].reshape(ROWS, -1), 128)
        low = padded(
            jnp.concatenate([repack(low, ROWS), vec], axis=1), BLOCK[0] * BLOCK[1]
        ).reshape(INNER, OUTER, *BLOCK)
        packs = [low[:, n] for n in range(OUTER)]
        pieces = [lax.all_gather(skip_tokens, "skip", axis=0, tiled=True)]
        bias, ranks = early_call(packs[0])

    layer_out, grad_decoder, everyone, *grads = layer_call(
        skip_count,
        assignment[0],
        extents,
        here,
        ranks,
        decoder_tokens.T,
        cotangent.T,
        bias,
        packs,
        [piece.T for piece in pieces],
    )
    grad_picks, grad_packs = grads[:skip_count], grads[skip_count:]

    def returned_call(here, everyone, after, received):
        (grad_skip,) = small_call(
            functools.partial(return_kernel, windows, OUTER),
            "returned",
            [SMEM, SMEM] + [VMEM] * (1 + skip_count),
            [jax.ShapeDtypeStruct((C, windows * WTOK), F32)],
            (here, everyone, after, *received),
            [
                pltpu.VMEM((skip_count, *received[0].shape), BF),
                pltpu.SMEM((windows,), jnp.int32),
            ],
            3_000_000,
        )
        return grad_skip

    shares = [
        jax.ShapeDtypeStruct((1, mat_width), F32),
        jax.ShapeDtypeStruct((1, vec_width), F32),
    ]
    if plain:
        far = swap(grad_packs[3], "skip", 1)
        near = swap(grad_packs[1], "skip", 1)
        (far,) = small_call(
            skip_sum_kernel,
            "core_sum",
            [VMEM] * 2,
            [jax.ShapeDtypeStruct((INNER, *BLOCK), BF)],
            (grad_packs[2], far),
        )
        keep, send = small_call(
            split_kernel,
            "skip_sum",
            [SMEM] + [VMEM] * 3,
            [
                jax.ShapeDtypeStruct((INNER // 2, *BLOCK), F32),
                jax.ShapeDtypeStruct((INNER // 2, *BLOCK), BF),
            ],
            (here, grad_packs[0], near, swap(far, "skip", 2)),
        )
        send, grad_picks = lax.optimization_barrier((send, grad_picks))
        received = [grad_picks[0]] + [swap(grad_picks[d], "skip", d) for d in range(1, OUTER)]
        for distance in (1, 2):
            half = keep.shape[0] // 2
            keep, send = small_call(
                halve_kernel,
                "slab_half",
                [VMEM] * 2,
                [
                    jax.ShapeDtypeStruct((half, *BLOCK), F32),
                    jax.ShapeDtypeStruct((half, *BLOCK), BF),
                ],
                (keep, swap(send, "slab", distance)),
                moved=300_000,
            )
        came, received = lax.optimization_barrier((swap(send, "slab", 4), received))
        mat_share, vec_share, tail = small_call(
            slab_sum_kernel,
            "slab_sum",
            [VMEM] * 2,
            shares + [jax.ShapeDtypeStruct((ROWS, 128), F32)],
            (keep, came),
            moved=300_000,
        )
        grad_skip = returned_call(here, everyone, vec_share, received)
        tail = lax.all_to_all(tail, ("slab", "skip"), split_axis=0, concat_axis=0, tiled=True)
        tail, grad_skip = lax.optimization_barrier((tail, grad_skip))
    else:
        received = list(
            lax.all_to_all(jnp.stack(grad_picks), "skip", split_axis=0, concat_axis=0)
        )
        everyone = lax.all_gather(assignment, "skip", axis=0, tiled=True)
        rows = jnp.stack(grad_packs, axis=1).reshape(ROWS, -1)
        start, side = 128 * VEC_TILE, 128 * SIDE_TILE
        rows = jnp.concatenate(
            [
                repack(rows, device_count),
                rows[:, start : start + VEC // ROWS].reshape(device_count, -1),
                rows[:, side : side + TABLE_LANES].reshape(device_count, -1),
            ],
            axis=1,
        )
        share = lax.psum_scatter(
            rows.astype(F32), ("slab", "skip"), scatter_dimension=0, tiled=True
        )
        mat_share = share[:, :mat_width]
        vec_share = share[:, mat_width : mat_width + vec_width]
        table = lax.all_gather(
            share[:, mat_width + vec_width :], ("slab", "skip"), axis=0, tiled=True
        )
        squares = lax.psum(jnp.sum(share * share), ("slab", "skip")) * (1.0 / ROWS)
        tail = jnp.concatenate(
            [table.reshape(ROWS, TABLE_LANES), jnp.full((ROWS, 128 - TABLE_LANES), squares)],
            axis=1,
        )

    if not plain:
        grad_skip = returned_call(here, everyone, vec_share, received)
    groups = (
        (mat_master, mat_first, mat_second, mat_average),
        (vec_master, vec_first, vec_second, vec_average),
        (table_master.T, table_first.T, table_second.T, table_average.T),
    )
    kinds = [jax.ShapeDtypeStruct((1, 1), F32)]
    for group in groups:
        kinds += [jax.ShapeDtypeStruct(group[0].shape, F32)] * 5
        kinds += [jax.ShapeDtypeStruct(group[0].shape, BF)]
    outs = small_call(
        update_kernel,
        "update",
        [VMEM] * 15,
        kinds,
        (mat_share, vec_share, tail, *groups[0], *groups[1], *groups[2]),
    )
    return (
        layer_out.T,
        grad_decoder.T,
        grad_skip.T,
        outs[0].reshape(()),
        *outs[1:13],
        *[value.T for value in outs[13:]],
    )


def solution(mesh):
    split = P(("slab", "skip"), None)
    return jax.shard_map(
        on_device,
        mesh=mesh,
        in_specs=(split, split, split, P("slab"), P("slab", "skip"))
        + (split,) * 8
        + (P(),) * 4,
        out_specs=(split, split, split, P()) + (split,) * 12 + (P(),) * 6,
        check_vma=False,
    )
```

```python
import functools
import math
import jax
import jax.numpy as jnp
from jax import lax
from jax.experimental import pallas as pl
from jax.experimental.pallas import tpu as pltpu
from jax.sharding import PartitionSpec as P

C = 192
HEADS = 6
HEAD_DIM = 32
HIDDEN_SIZE = 768
WS = 4
DEPTH = 16
STEP = 10
WTOK = 64
REL = 343

EPS = 1e-05
MASK_FILL = -1000000000.0
CLIP = 1.0
BETA_ONE = 0.9
BETA_TWO = 0.999
RATE = 0.3
MATRIX_DECAY = 0.05
ADAM_EPS = 1e-08
EMA_RATE = 0.9

BF = jnp.bfloat16
F32 = jnp.float32
GROUP = 256
GWIN = GROUP // WTOK
T = 1024
GROUPS = T // GROUP
WIDE = 1024
PARTS = T // WIDE
WIN = T // WTOK
QSCALE = HEAD_DIM ** (-0.5)
SHAPES = ((C, C), (C, 2 * C), (C, C), (C, HIDDEN_SIZE), (HIDDEN_SIZE, C))
VLEN = (C, C, C, C, C, C, C, HIDDEN_SIZE, C)
VOFF = tuple(sum(VLEN[:n]) for n in range(len(VLEN)))
VEC = sum(VLEN)
MAT = sum(r * c for r, c in SHAPES)
ROWS = 32
OUTER = 4
INNER = ROWS // OUTER
BLOCK = (16, 896)
BLOCK_TILES = BLOCK[1] // 128
VEC_TILE = MAT // ROWS // 128
SIDE_TILE = VEC_TILE + 1
TABLE_LANES = 8 * 384 // ROWS


def mm(a, b):
    return jnp.dot(a, b, preferred_element_type=F32)


def mm_nt(a, b):
    return lax.dot_general(a, b, (((1,), (1,)), ((), ())), preferred_element_type=F32)


def iota(shape, dim):
    return lax.broadcasted_iota(jnp.int32, shape, dim)


def kept(value):
    return pltpu.with_memory_space_constraint(value, pltpu.HBM)


def both(column, width=256):
    return jnp.concatenate([column] * (width // 128), axis=1)


def place(slot):
    span = 2 * WS - 1
    return ((slot >> 4) * span + ((slot >> 2) & 3)) * span + (slot & 3)


def splits(value):
    high = value.astype(BF)
    rest = value - high.astype(F32)
    middle = rest.astype(BF)
    return high, middle, (rest - middle.astype(F32)).astype(BF)


def normed(value):
    center = value - jnp.sum(value, axis=0, keepdims=True) * (1.0 / C)
    scale = lax.rsqrt(jnp.sum(center * center, axis=0, keepdims=True) * (1.0 / C) + EPS)
    return center * scale, scale


def normed_back(grad_hat, hat, scale):
    mean_grad = jnp.sum(grad_hat, axis=0, keepdims=True) * (1.0 / C)
    mean_both = jnp.sum(grad_hat * hat, axis=0, keepdims=True) * (1.0 / C)
    return scale * (grad_hat - mean_grad - hat * mean_both)


def fold(value):
    return sum(value[:, n : n + 128] for n in range(0, value.shape[1], 128))


def gelu_parts(u):
    t = pl.reciprocal(1.0 + (0.3275911 * 0.5**0.5) * jnp.abs(u), approx=True)
    bell = jnp.exp2((-0.5 * math.log2(math.e)) * (u * u))
    series = 0.5 * 1.061405429
    for factor in (-1.453152027, 1.421413741, -0.284496736, 0.254829592):
        series = series * t + 0.5 * factor
    tail = series * t * bell
    cdf = jnp.where(u >= 0.0, 1.0 - tail, tail)
    return u * cdf, cdf + ((0.5 / math.pi) ** 0.5 * u) * bell


def early_kernel(skip_count, windows, chosen, table, after, bias_s, ranks, tab_s, big, count_s):
    del after
    tab_s[...] = jnp.zeros_like(tab_s)
    tab_s[0:HEADS, 0:REL] = table[...]
    hot = (iota((256, 128), 0) == place(iota((256, 128), 1) & 63)).astype(BF)
    total = None
    for part in splits(tab_s[...]):
        part = part.astype(F32)
        for j in range(WTOK):
            turn = (place(j) - place(WTOK - 1)) % 384
            rolled = pltpu.roll(part, turn, 1) if turn else part
            big[0, 8 * j : 8 * j + 8, :] = rolled[:, 0:128]
            big[1, 8 * j : 8 * j + 8, :] = rolled[:, 128:256]
        product = mm(big[0].astype(BF), hot[0:128]) + mm(big[1].astype(BF), hot[128:256])
        total = product if total is None else total + product
    big[0] = total
    for h in range(HEADS):
        bias_s[h] = big[0, pl.ds(h, WTOK, stride=8), :]
    for e in range(skip_count):
        count_s[e] = 0

    def note(w, rank_row):
        owner = lax.div(chosen[w], windows)
        rank = count_s[owner]
        count_s[owner] = rank + 1
        return jnp.where(iota((1, 128), 1) == w, rank, rank_row)

    ranks[...] = lax.fori_loop(0, windows, note, jnp.zeros((1, 128), jnp.int32))


def layer_kernel(
    skip_count,
    windows,
    piece_count,
    chosen,
    extents,
    here,
    ranks,
    dec_all,
    cot_all,
    bias_s,
    *refs,
):
    step = pl.program_id(0)
    packs, refs = refs[:OUTER], refs[OUTER:]
    pieces, refs = refs[:piece_count], refs[piece_count:]
    layer_out, grad_dec, everyone, *refs = refs
    grad_picks, refs = refs[:skip_count], refs[skip_count:]
    grad_packs, refs = refs[:OUTER], refs[OUTER:]
    (
        pick_s,
        big,
        vcol,
        wq,
        wqt,
        wkv,
        wkvt,
        wo,
        wot,
        w1,
        w1t,
        w2,
        w2t,
        xn_s,
        sn_s,
        hn_s,
        o_s,
        gl_s,
        du_s,
        q_s,
        qbd_s,
        kst_s,
        vst_s,
        kcat_s,
        vcat_s,
        pf_s,
        pb_s,
        ds_s,
        da_s,
        do_s,
        dm_s,
        u_s,
        ga_s,
        gh_s,
        gs_s,
        dq_s,
        dkv_s,
        n1_s,
        n2_s,
        n3_s,
        x1_s,
        gds_s,
        aq,
        akv,
        ao,
        a1,
        a2,
        ln_s,
        slab,
        slab_sem,
        dec_s,
        cot_s,
        token_sem,
        pack_s,
        pack_sem,
    ) = refs
    dec, cot = dec_s.at[step], cot_s.at[step]
    stage, block_s = u_s, ga_s
    my_skip, mix = here[0], here[1]
    lane = iota((1, 128), 1)
    left = lane < WTOK

    def tile_of(number):
        j, n = divmod(number, BLOCK_TILES)
        return n, pl.ds(j, ROWS, stride=BLOCK[0]), slice(None)


    def token_copies(n):
        lanes = slice(T * n, T * n + T)
        return [
            pltpu.make_async_copy(dec_all.at[:, lanes], dec_s.at[n], token_sem.at[2 * n]),
            pltpu.make_async_copy(cot_all.at[:, lanes], cot_s.at[n], token_sem.at[2 * n + 1]),
        ]

    for n in range(1, windows // WIN):

        @pl.when(step == n)
        def _(n=n):
            for copy in token_copies(n):
                copy.wait()

    @pl.when(step == 0)
    def _():
        copies = token_copies(0) + [
            pltpu.make_async_copy(
                piece, slab.at[:, n * piece.shape[1] : (n + 1) * piece.shape[1]], slab_sem.at[n]
            )
            for n, piece in enumerate(pieces)
        ]
        pack_copies = [
            pltpu.make_async_copy(packs[n], pack_s.at[n], pack_sem.at[n]) for n in range(OUTER)
        ]
        for copy in pack_copies + copies + [copy for n in range(1, windows // WIN) for copy in token_copies(n)]:
            copy.start()
        for ref in (gds_s, aq, akv, ao, a1, a2, ln_s):
            ref[...] = jnp.zeros_like(ref)
        for ref, rows in ((xn_s, C), (sn_s, C), (hn_s, C), (o_s, C), (gl_s, HIDDEN_SIZE)):
            ref[rows : rows + 16, :] = jnp.ones((16, T), BF)
        for copy in pack_copies:
            copy.wait()
        for outer in range(OUTER):
            for inner in range(INNER):
                k = inner * OUTER + lax.bitwise_xor(my_skip, outer)
                rows = pl.ds(pl.multiple_of(k * BLOCK[0], BLOCK[0]), BLOCK[0])
                for n in range(BLOCK_TILES):
                    block_s[n, rows, :] = pack_s[outer, inner, :, 128 * n : 128 * n + 128].astype(
                        F32
                    )
        offset = 0
        for (rows, cols), plain, turned in zip(
            SHAPES, (wq, wkv, wo, w1, w2), (wqt, wkvt, wot, w1t, w2t)
        ):
            per = rows // ROWS
            tiles = -(-cols // 128)
            for a in range(per):
                first, shift = divmod(offset + a * cols, 128)
                for n in range(tiles):
                    piece = block_s[tile_of(first + n)]
                    if shift and n + 1 < tiles:
                        after = block_s[tile_of(first + n + 1)]
                        piece = jnp.concatenate([piece[:, shift:], after[:, :shift]], axis=1)
                    elif shift:
                        piece = pltpu.roll(piece, 128 - shift, 1)
                    stage[n, pl.ds(a, ROWS, stride=per), :] = piece
            for n in range(tiles):
                width = min(128, cols - 128 * n)
                value = stage[n, 0:rows, :].astype(BF)
                plain[:, 128 * n : 128 * n + width] = value[:, 0:width]
                turned[128 * n : 128 * n + width, :] = jnp.transpose(value)[0:width]
            offset += per * cols
        side = block_s[tile_of(VEC_TILE)]
        per = VEC // ROWS
        vec = jnp.concatenate([side[k : k + 1, 0:per] for k in range(ROWS)], axis=1)
        vcol[...] = jnp.transpose(jnp.broadcast_to(vec, (128, VEC)))
        side = block_s[tile_of(SIDE_TILE)]
        everyone[...] = side.astype(jnp.int32)
        for copy in copies:
            copy.wait()

    def column(number, first=0, last=None):
        start = VOFF[number]
        return vcol[start + first : start + (VLEN[number] if last is None else last), :]

    chunks = [slice(128 * c, 128 * c + 128) for c in range(T // 128)]
    tiles = [slice(GROUP * g, GROUP * g + GROUP) for g in range(GROUPS)]
    wides = [slice(WIDE * g, WIDE * g + WIDE) for g in range(PARTS)]
    per_wide = WIDE // 128
    groups_wide = WIDE // GROUP
    layers, valid = [], []
    for c in range(len(chunks)):
        deep = [
            jnp.clip(extents[0] - WS * (chosen[step * WIN + 2 * c + w] & 3), 0, WS) for w in (0, 1)
        ]
        layers.append(jnp.where(left, deep[0], deep[1]))
        valid.append(jnp.where((lane & 63) >> 4 < layers[c], 1.0, 0.0))

    scale_one, scale_two, scale_three = {}, {}, {}

    def stacks(rows, g, stack_ref, cat_ref):
        turned = pltpu.roll(rows, WTOK, 1)
        first, second = rows[:, 0:128], rows[:, 128:256]
        mixed, middle = turned[:, 0:128], turned[:, 128:256]
        at_left = (first, middle, second, mixed)
        at_right = (mixed, first, middle, second)
        for h in range(0, HEADS, 2):
            n = g * HEADS + h
            at = slice(HEAD_DIM * h, HEAD_DIM * h + HEAD_DIM)
            after = slice(HEAD_DIM * h + HEAD_DIM, HEAD_DIM * h + 2 * HEAD_DIM)
            pieces = []
            for w in range(GWIN):
                to = slice(HEAD_DIM * w, HEAD_DIM * w + HEAD_DIM)
                stack_ref[n, to, :] = at_left[w][at, 0:WTOK]
                stack_ref[n + 1, to, :] = at_left[w][after, 0:WTOK]
                pieces.append(jnp.where(left, at_left[w][at], at_right[w][after]))
            pair = jnp.transpose(jnp.concatenate(pieces, axis=0))
            cat_ref[n] = pair[0:WTOK]
            cat_ref[n + 1] = pair[WTOK:]

    window_mask = [
        (iota((HEAD_DIM, GROUP), 1) >> 6 == w).astype(F32).astype(BF) for w in range(GWIN)
    ]

    def spread(rows):
        return jnp.concatenate([rows * mask for mask in window_mask], axis=0)

    def own(stacked, probs):
        parts = []
        for n in range(GWIN // 2):
            cut = mm(
                stacked[2 * HEAD_DIM * n : 2 * HEAD_DIM * (n + 1)],
                probs[:, 128 * n : 128 * n + 128],
            )
            parts.append(jnp.where(left, cut[0:HEAD_DIM], cut[HEAD_DIM:]))
        return jnp.concatenate(parts, axis=1)

    def unstack(product):
        low = product.astype(BF)
        return jnp.concatenate(
            [low[HEAD_DIM * w : HEAD_DIM * w + HEAD_DIM] for w in range(GWIN)], axis=1
        )

    def filled(g):
        return jnp.concatenate(
            [
                jnp.concatenate(
                    [
                        jnp.broadcast_to(jnp.where(layers[c] > d, 0.0, MASK_FILL), (WS * WS, 128))
                        for d in range(WS)
                    ],
                    axis=0,
                )
                for c in (2 * g, 2 * g + 1)
            ],
            axis=1,
        )

    def place_of(n):
        g, h = divmod(n, HEADS)
        return slice(HEAD_DIM * h, HEAD_DIM * h + HEAD_DIM), tiles[g]

    def softmax(n, scores, fill):
        scores = scores + both(bias_s[n % HEADS]) + fill
        powers = jnp.exp(scores - jnp.max(scores, axis=0, keepdims=True))
        probs = powers * pl.reciprocal(jnp.sum(powers, axis=0, keepdims=True), approx=True)
        pf_s[n] = probs
        pb_s[n] = probs.astype(BF)

    def softmax_back(n, grad_probs):
        probs = pf_s[n]
        grad_scores = (
            probs * (grad_probs - jnp.sum(probs * grad_probs, axis=0, keepdims=True))
        ).astype(BF)
        gds_s[n % HEADS] += fold(grad_scores.astype(F32))
        ds_s[n] = grad_scores

    def forward(g):
        lanes = wides[g]
        for c in range(per_wide * g, per_wide * (g + 1)):
            cut = chunks[c]
            hat, scale_one[c] = normed(dec[:, cut].astype(F32))
            n1_s[:, cut] = hat
            xn_s[0:C, cut] = (hat * column(0) + column(1)).astype(BF)
            yield 130
            halves = []
            for w in (0, 1):
                a = chosen[step * WIN + 2 * c + w]
                at = lax.bitwise_xor(a, mix * windows) >> 1
                part = slab[:, pl.ds(pl.multiple_of(at * 128, 128), 128)]
                halves.append(pltpu.roll(part, ((a + w) & 1) * WTOK, 1))
            hat, scale_two[c] = normed(jnp.where(left, halves[0], halves[1]).astype(F32))
            n2_s[:, cut] = hat
            sn_s[0:C, cut] = (hat * column(0) + column(1)).astype(BF)
            yield 160
        query = mm(wqt[...], xn_s[0:C, lanes])
        pair = mm(wkvt[...], sn_s[0:C, lanes])
        q_s[:, lanes] = ((query + both(column(2), WIDE)) * QSCALE).astype(BF)
        for c in range(per_wide * g, per_wide * (g + 1)):
            dm_s[:, chunks[c]] = (cot[:, chunks[c]].astype(F32) * valid[c]).astype(BF)
        yield 250
        first, units = g * groups_wide * HEADS, groups_wide * HEADS
        for n in range(first, first + units):
            qbd_s[n] = spread(q_s[place_of(n)])
        keys = pair[0:C].astype(BF)
        values = (pair[C:] + both(column(3), WIDE)).astype(BF)
        for k in range(groups_wide):
            cut = slice(GROUP * k, GROUP * k + GROUP)
            stacks(keys[:, cut], groups_wide * g + k, kst_s, kcat_s)
            yield 250
            stacks(values[:, cut], groups_wide * g + k, vst_s, vcat_s)
            yield 250
        scores = {}
        for n in range(first, first + units + 2):
            if n < first + units:
                scores[n] = mm(kcat_s[n], qbd_s[n])
            if n >= first + 2:
                o_s[place_of(n - 2)] = own(vst_s[n - 2], pb_s[n - 2]).astype(BF)
            if first + 1 <= n <= first + units:
                if (n - 1) % HEADS == 0:
                    fill = filled((n - 1) // HEADS)
                softmax(n - 1, scores.pop(n - 1), fill)
            yield 180
        product = mm(w2[...], dm_s[:, lanes])
        for c in range(per_wide):
            ga_s[per_wide * g + c] = product[:, 128 * c : 128 * c + 128]
        yield 300
        x1_s[:, lanes] = mm(wot[...], o_s[0:C, lanes])
        yield 150
        for c in range(per_wide * g, per_wide * (g + 1)):
            cut = chunks[c]
            middle = dec[:, cut].astype(F32) + x1_s[:, cut] + column(4)
            x1_s[:, cut] = middle
            hat, scale_three[c] = normed(middle)
            n3_s[:, cut] = hat
            hn_s[0:C, cut] = (hat * column(5) + column(6)).astype(BF)
            yield 150

    def feed(g):
        lanes = wides[g]
        product = mm(w1t[...], hn_s[0:C, lanes])
        for c in range(per_wide):
            u_s[per_wide * g + c] = product[:, 128 * c : 128 * c + 128]
        yield 300
        piece = 32
        for start in range(0, HIDDEN_SIZE, piece):
            rows = slice(start, start + piece)
            for c in range(per_wide * g, per_wide * (g + 1)):
                active, slope = gelu_parts(u_s[c, rows, :] + column(7, start, start + piece))
                gl_s[rows, chunks[c]] = active.astype(BF)
                du_s[rows, chunks[c]] = (ga_s[c, rows, :] * slope).astype(BF)
            yield 35 * piece // 16
        gh_s[:, lanes] = mm(w1[...], du_s[:, lanes])
        yield 450
        mlp = mm(w2t[...], gl_s[0:HIDDEN_SIZE, lanes]) + both(column(8), WIDE)
        layer_out[:, lanes] = (
            jnp.concatenate(valid[per_wide * g : per_wide * (g + 1)], axis=1) * (x1_s[:, lanes] + mlp)
        ).astype(BF)
        yield 500
        for c in range(per_wide * g, per_wide * (g + 1)):
            cut = chunks[c]
            grad, hat = gh_s[:, cut], n3_s[:, cut]
            ln_s[1] += grad * hat
            back = normed_back(grad * column(5), hat, scale_three[c])
            grad_middle = cot[:, cut].astype(F32) * valid[c] + back
            x1_s[:, cut] = grad_middle
            da_s[:, cut] = grad_middle.astype(BF)
            yield 170
        do_s[:, lanes] = mm(wo[...], da_s[:, lanes]).astype(BF)
        yield 150

    def backward(g):
        lanes = wides[g]
        first, units = g * groups_wide * HEADS, groups_wide * HEADS
        spreads, grads = {}, {}
        for n in range(first, first + units + 2):
            if n < first + units:
                lanes = place_of(n)[1]
                at, _ = place_of(n)
                spreads[n] = spread(do_s[at, lanes])
                grads[n] = mm(vcat_s[n], spreads[n])
                dkv_s[at.start + C : at.stop + C, lanes] = unstack(
                    mm_nt(spreads.pop(n), pb_s[n])
                )
            if n >= first + 2:
                at, lanes = place_of(n - 2)
                dq_s[at, lanes] = own(kst_s[n - 2], ds_s[n - 2]).astype(BF)
                dkv_s[at, lanes] = unstack(mm_nt(qbd_s[n - 2], ds_s[n - 2]))
            if first + 1 <= n <= first + units:
                softmax_back(n - 1, grads.pop(n - 1))
            yield 340
        lanes = wides[g]
        gh_s[:, lanes] = mm(wq[...], dq_s[:, lanes])
        yield 150
        gs_s[:, lanes] = mm(wkv[...], dkv_s[:, lanes])
        yield 300
        for c in range(per_wide * g, per_wide * (g + 1)):
            cut = chunks[c]
            grad, hat = gh_s[:, cut] * QSCALE, n1_s[:, cut]
            ln_s[0] += grad * hat
            grad_dec[:, cut] = x1_s[:, cut] + normed_back(grad * column(0), hat, scale_one[c])
            yield 170
            grad, hat = gs_s[:, cut], n2_s[:, cut]
            ln_s[0] += grad * hat
            back = normed_back(grad * column(0), hat, scale_two[c]).astype(BF)
            for w in (0, 1):
                a = chosen[step * WIN + 2 * c + w]
                rank = ranks[0, step * WIN + 2 * c + w]
                owner = lax.bitwise_xor(lax.div(a, windows), mix)
                half = pltpu.roll(back, ((rank + w) & 1) * WTOK, 1)
                at = pl.ds(pl.multiple_of((rank >> 1) * 128, 128), 128)
                pick_s[owner, :, at] = jnp.where(
                    lane >> 6 == (rank & 1), half, pick_s[owner, :, at]
                )
            yield 250

    def add(ref, product):
        for n in range(ref.shape[0]):
            width = min(128, product.shape[1] - 128 * n)
            ref[n, :, 0:width] += product[:, 128 * n : 128 * n + width]

    def early_sums():
        add(a2, mm_nt(gl_s[...], dm_s[...]))
        yield 1200
        add(a1, mm_nt(hn_s[...], du_s[...]))
        yield 1200
        add(ao, mm_nt(o_s[...], da_s[...]))
        yield 400

    costs = {forward: 3500, feed: 3450, backward: 4000, early_sums: 2800}

    def interleaved(parts):
        running = [[part(*args), 0, costs[part]] for part, *args in parts]
        while running:
            now = min(running, key=lambda entry: entry[1] / entry[2])
            try:
                now[1] += next(now[0])
            except StopIteration:
                running.remove(now)

    for slot in range(PARTS + 2):
        parts = [
            (part, slot - lag)
            for lag, part in enumerate((forward, feed, backward))
            if 0 <= slot - lag < PARTS
        ]
        if slot == PARTS + 1:
            parts.append((early_sums,))
        interleaved(parts)
    add(aq, mm_nt(xn_s[...], dq_s[...]))
    add(akv, mm_nt(sn_s[...], dkv_s[...]))

    @pl.when(step == pl.num_programs(0) - 1)
    def _():
        offset = 0
        for number, ((rows, cols), ref) in enumerate(zip(SHAPES, (aq, akv, ao, a1, a2))):
            per = rows // ROWS
            tiles = -(-cols // 128)
            joined = 2 if cols % 128 else 1
            for a in range(0, per, joined):
                value = jnp.concatenate(
                    [
                        jnp.concatenate(
                            [ref[n, pl.ds(b, ROWS, stride=per), :] for n in range(tiles)], axis=1
                        )[:, 0:cols]
                        for b in range(a, a + joined)
                    ],
                    axis=1,
                )
                if number == 0:
                    value = value * QSCALE
                for n in range(joined * cols // 128):
                    block_s[tile_of((offset + a * cols) // 128 + n)] = value[
                        :, 128 * n : 128 * n + 128
                    ]
            offset += per * cols
        rows = [jnp.sum(jnp.transpose(ln_s[n]), axis=0, keepdims=True) for n in range(2)]
        def last_row(ref, at):
            row = [ref[n, at : at + 1, :] for n in range(ref.shape[0])]
            return jnp.concatenate(row, axis=1)

        def through(row, weight):
            row = jnp.broadcast_to(row, (16, row.shape[1]))
            return sum(mm_nt(part, weight[...]) for part in splits(row))[0:1]

        query_row = last_row(aq, C)[:, 0:C]
        pair_row, upper_row = last_row(akv, C), last_row(a1, C)
        flat = jnp.concatenate(
            [
                rows[0],
                through(query_row, wq) * QSCALE + through(pair_row, wkv),
                last_row(aq, C)[:, 0:C] * QSCALE,
                last_row(akv, C)[:, C:],
                last_row(ao, C)[:, 0:C],
                rows[1],
                through(upper_row, w1),
                last_row(a1, C),
                last_row(a2, HIDDEN_SIZE)[:, 0:C],
            ],
            axis=1,
        )
        big[0] = jnp.zeros((8 * WTOK, 128), F32)
        for h in range(HEADS):
            big[0, pl.ds(h, WTOK, stride=8), :] = gds_s[h]
        hot = (iota((128, 256), 1) == place(iota((128, 256), 0) & 63)).astype(BF)
        total = sum(mm(part, hot) for part in splits(big[0]))
        big[0] = total[:, 0:128]
        big[1] = total[:, 128:256]
        result = jnp.zeros((8, 384), F32)
        for j in range(WTOK):
            row = jnp.concatenate(
                [
                    big[0, 8 * j : 8 * j + 8, :],
                    big[1, 8 * j : 8 * j + 8, :],
                    jnp.zeros((8, 128), F32),
                ],
                axis=1,
            )
            turn = (place(WTOK - 1) - place(j)) % 384
            result = result + (pltpu.roll(row, turn, 1) if turn else row)
        per = VEC // ROWS
        block_s[tile_of(VEC_TILE)] = jnp.concatenate(
            [
                jnp.concatenate([flat[:, per * k : per * k + per] for k in range(ROWS)], axis=0),
                jnp.zeros((ROWS, 128 - per), F32),
            ],
            axis=1,
        )
        count = TABLE_LANES
        block_s[tile_of(SIDE_TILE)] = jnp.concatenate(
            [
                jnp.concatenate([result[:, count * n : count * n + count] for n in range(4)], axis=0),
                jnp.zeros((ROWS, 128 - count), F32),
            ],
            axis=1,
        )
        for number in range(SIDE_TILE + 1, BLOCK[0] * BLOCK_TILES):
            block_s[tile_of(number)] = jnp.zeros((ROWS, 128), F32)
        for outer in range(OUTER):
            for inner in range(INNER):
                k = inner * OUTER + lax.bitwise_xor(my_skip, outer)
                rows = pl.ds(pl.multiple_of(k * BLOCK[0], BLOCK[0]), BLOCK[0])
                for n in range(BLOCK_TILES):
                    grad_packs[outer][inner, :, 128 * n : 128 * n + 128] = block_s[
                        n, rows, :
                    ].astype(BF)
        for n in range(skip_count):
            grad_picks[n][...] = pick_s[n]


def layer_call(skip_count, chosen, extents, here, ranks, dec, cot, bias, packs, pieces):
    tokens = dec.shape[1]
    windows = tokens // WTOK
    steps = tokens // T
    share = tokens // skip_count
    block = pl.BlockSpec((C, T), lambda i: (0, i))
    smem = pl.BlockSpec(memory_space=pltpu.SMEM)
    hbm = pl.BlockSpec(memory_space=pltpu.HBM)

    def whole(shape):
        return pl.BlockSpec(shape, lambda i: (0,) * len(shape))

    scratch = [
        ((skip_count, C, share), BF),
        ((2, 8 * WTOK, 128), F32),
        ((VEC, 128), F32),
        ((C, C), BF),
        ((C, C), BF),
        ((C, 2 * C), BF),
        ((2 * C, C), BF),
        ((C, C), BF),
        ((C, C), BF),
        ((C, HIDDEN_SIZE), BF),
        ((HIDDEN_SIZE, C), BF),
        ((HIDDEN_SIZE, C), BF),
        ((C, HIDDEN_SIZE), BF),
        ((C + 16, T), BF),
        ((C + 16, T), BF),
        ((C + 16, T), BF),
        ((C + 16, T), BF),
        ((HIDDEN_SIZE + 16, T), BF),
        ((HIDDEN_SIZE, T), BF),
        ((C, T), BF),
        ((GROUPS * HEADS, GWIN * HEAD_DIM, GROUP), BF),
        ((GROUPS * HEADS, GWIN * HEAD_DIM, WTOK), BF),
        ((GROUPS * HEADS, GWIN * HEAD_DIM, WTOK), BF),
        ((GROUPS * HEADS, WTOK, GWIN * HEAD_DIM), BF),
        ((GROUPS * HEADS, WTOK, GWIN * HEAD_DIM), BF),
        ((GROUPS * HEADS, WTOK, GROUP), F32),
        ((GROUPS * HEADS, WTOK, GROUP), BF),
        ((GROUPS * HEADS, WTOK, GROUP), BF),
        ((C, T), BF),
        ((C, T), BF),
        ((C, T), BF),
        ((T // 128, HIDDEN_SIZE, 128), F32),
        ((T // 128, HIDDEN_SIZE, 128), F32),
        ((C, T), F32),
        ((C, T), F32),
        ((C, T), BF),
        ((2 * C, T), BF),
        ((C, T), F32),
        ((C, T), F32),
        ((C, T), F32),
        ((C, T), F32),
        ((HEADS, WTOK, 128), F32),
        ((2, C + 16, 128), F32),
        ((3, C + 16, 128), F32),
        ((2, C + 16, 128), F32),
        ((6, C + 16, 128), F32),
        ((2, HIDDEN_SIZE + 16, 128), F32),
        ((2, C, 128), F32),
    ]
    flops = 2 * tokens * (3 * 442368 + 12 * WTOK * C)
    return pl.pallas_call(
        functools.partial(layer_kernel, skip_count, windows, len(pieces)),
        grid=(steps,),
        in_specs=[smem, smem, smem, smem, hbm, hbm, whole(bias.shape)]
        + [pl.BlockSpec(memory_space=pl.ANY)] * (OUTER + len(pieces)),
        out_specs=[block, block, whole((ROWS, 128))]
        + [whole((C, share))] * skip_count
        + [whole((INNER, *BLOCK))] * OUTER,
        out_shape=[
            jax.ShapeDtypeStruct((C, tokens), BF),
            jax.ShapeDtypeStruct((C, tokens), F32),
            jax.ShapeDtypeStruct((ROWS, 128), jnp.int32),
        ]
        + [jax.ShapeDtypeStruct((C, share), BF)] * skip_count
        + [jax.ShapeDtypeStruct((INNER, *BLOCK), BF)] * OUTER,
        scratch_shapes=[pltpu.VMEM(shape, kind) for shape, kind in scratch]
        + [
            pltpu.VMEM((C, skip_count * tokens), BF),
            pltpu.SemaphoreType.DMA((len(pieces),)),
            pltpu.VMEM((steps, C, T), BF),
            pltpu.VMEM((steps, C, T), BF),
            pltpu.SemaphoreType.DMA((2 * steps,)),
            pltpu.VMEM((OUTER, INNER, *BLOCK), BF),
            pltpu.SemaphoreType.DMA((OUTER,)),
        ],
        compiler_params=pltpu.CompilerParams(
            dimension_semantics=("arbitrary",), vmem_limit_bytes=50 * 1024 * 1024
        ),
        cost_estimate=pl.CostEstimate(
            flops=flops, bytes_accessed=8_000_000, transcendentals=tokens * 1200
        ),
        name="layer",
    )(
        kept(chosen),
        extents,
        here,
        ranks,
        kept(dec),
        kept(cot),
        bias,
        *packs,
        kept(pieces[0]),
        *pieces[1:3],
        *[kept(piece) for piece in pieces[3:]],
    )


def pack_kernel(mat, vec, chosen, out):
    flat = jnp.concatenate(
        [
            mat[...],
            vec[...],
            jnp.zeros((1, 128 - vec.shape[1]), F32),
            chosen[...].astype(F32),
            jnp.zeros((1, BLOCK[0] * BLOCK[1] - 128 * SIDE_TILE - chosen.shape[1]), F32),
        ],
        axis=1,
    )
    block = jnp.concatenate(
        [flat[:, BLOCK[1] * j : BLOCK[1] * (j + 1)] for j in range(BLOCK[0])], axis=0
    ).astype(BF)
    for n in range(INNER):
        out[n] = block


def skip_sum_kernel(*refs):
    blocks, out = refs[:-1], refs[-1]
    for n in range(INNER):
        out[n] = sum(block[n].astype(F32) for block in blocks).astype(BF)


def split_kernel(here, *refs):
    blocks, (keep, send) = refs[:-2], refs[-2:]
    for n in range(INNER // 2):
        for odd, out in enumerate((keep, send)):
            at = lax.bitwise_xor(here[3], 2 * n + odd)
            out[n] = sum(block[at].astype(F32) for block in blocks).astype(out.dtype)


def halve_kernel(kept, came, keep, send):
    for n in range(kept.shape[0] // 2):
        keep[n] = kept[2 * n] + came[2 * n].astype(F32)
        send[n] = (kept[2 * n + 1] + came[2 * n + 1].astype(F32)).astype(BF)


def slab_sum_kernel(kept, came, mat, vec, tail):
    total = kept[0] + came[0].astype(F32)
    squares = jnp.sum(jnp.sum(total * total, axis=1, keepdims=True), axis=0, keepdims=True)
    flat = jnp.concatenate([total[j : j + 1, :] for j in range(BLOCK[0])], axis=1)
    mat[...] = flat[:, 0 : mat.shape[1]]
    vec[...] = flat[:, 128 * VEC_TILE : 128 * VEC_TILE + vec.shape[1]]
    side = flat[:, 128 * SIDE_TILE : 128 * SIDE_TILE + 128]
    side = jnp.where(iota((1, 128), 1) == TABLE_LANES, squares, side)
    tail[...] = jnp.broadcast_to(side, tail.shape)


def return_kernel(windows, row, here, everyone, after, *refs):
    del after
    received, (out, gathered, source) = refs[:-3], refs[-3:]
    skip_count = len(received)
    per = windows // skip_count
    mix = here[1]
    for d in range(skip_count):
        gathered[d] = received[d][...]
        s = lax.bitwise_xor(mix, d)

        def note(w, rank):
            a = everyone[here[3] * row + s, w]
            mine = lax.div(a, windows) == here[2]

            @pl.when(mine)
            def _():
                source[lax.rem(a, windows)] = d * per + rank

            return rank + mine.astype(jnp.int32)

        lax.fori_loop(0, windows, note, 0)
    left = iota((1, 128), 1) < WTOK
    for n in range(windows // 2):
        halves = []
        for w in (0, 1):
            place_in = source[2 * n + w]
            d, rank = lax.div(place_in, per), lax.rem(place_in, per)
            lanes = pl.ds(pl.multiple_of((rank >> 1) * 128, 128), 128)
            block = gathered[d, :, lanes].astype(F32)
            halves.append(pltpu.roll(block, ((rank + w) & 1) * WTOK, 1))
        out[:, 128 * n : 128 * n + 128] = jnp.where(left, halves[0], halves[1])


VMEM = pl.BlockSpec(memory_space=pltpu.VMEM)
SMEM = pl.BlockSpec(memory_space=pltpu.SMEM)


def small_call(kernel, name, in_specs, outs, operands, scratch=(), moved=1_000_000):
    return pl.pallas_call(
        kernel,
        in_specs=in_specs,
        out_specs=[VMEM] * len(outs),
        out_shape=outs,
        scratch_shapes=scratch,
        compiler_params=pltpu.CompilerParams(vmem_limit_bytes=16 * 1024 * 1024),
        cost_estimate=pl.CostEstimate(flops=moved, bytes_accessed=moved, transcendentals=0),
        name=name,
    )(*operands)


def repack(packed, count):
    pieces, offset = [], 0
    for rows, cols in SHAPES:
        width = rows * cols // packed.shape[0]
        pieces.append(packed[:, offset : offset + width].reshape(count, -1))
        offset += width
    return jnp.concatenate(pieces, axis=1)


def padded(value, width):
    return jnp.pad(value, ((0, 0), (0, width - value.shape[1])))


def adamw_update(master, first, second, average, grad, factor, decay):
    clipped = grad * factor
    first_new = BETA_ONE * first + (1.0 - BETA_ONE) * clipped
    second_new = BETA_TWO * second + (1.0 - BETA_TWO) * clipped * clipped
    first_hat = first_new / (1.0 - BETA_ONE**STEP)
    second_hat = second_new / (1.0 - BETA_TWO**STEP)
    master_new = master - RATE * (first_hat / (jnp.sqrt(second_hat) + ADAM_EPS) + decay * master)
    average_new = EMA_RATE * average + (1.0 - EMA_RATE) * master_new
    return (clipped, master_new, first_new, second_new, average_new, master_new.astype(BF))


def update_kernel(mat_share, vec_share, tail, *refs):
    mats, vecs, tables = refs[0:4], refs[4:8], refs[8:12]
    norm_out, outs = refs[12], refs[13:]
    squares = jnp.sum(tail[:, TABLE_LANES : TABLE_LANES + 1], axis=0, keepdims=True)
    norm = jnp.sqrt(squares)
    norm_out[...] = norm
    factor = CLIP / jnp.maximum(norm, CLIP)
    table = jnp.concatenate([tail[8 * q : 8 * q + 8, 0:TABLE_LANES] for q in range(4)], axis=1)
    work = (
        (mats, mat_share[...], MATRIX_DECAY),
        (vecs, vec_share[...], 0.0),
        (tables, table[0:HEADS, 0:REL], 0.0),
    )
    for n, (group, grad, decay) in enumerate(work):
        results = adamw_update(*[ref[...] for ref in group], grad, factor, decay)
        for ref, value in zip(outs[6 * n : 6 * n + 6], results):
            ref[...] = value


def on_device(
    decoder_tokens,
    skip_tokens,
    cotangent,
    extents,
    assignment,
    mat_master,
    mat_first,
    mat_second,
    mat_average,
    vec_master,
    vec_first,
    vec_second,
    vec_average,
    table_master,
    table_first,
    table_second,
    table_average,
):
    skip_count = lax.axis_size("skip")
    slab_count = lax.axis_size("slab")
    device_count = skip_count * slab_count
    windows = assignment.shape[1]
    mat_width, vec_width = mat_master.shape[1], vec_master.shape[1]
    me = lax.axis_index("skip")
    plain = (skip_count, slab_count) == (OUTER, INNER)

    def swap(value, axis, distance):
        count = lax.axis_size(axis)
        return lax.ppermute(value, axis, [(n, n ^ distance) for n in range(count)])

    def early_call(after):
        return pl.pallas_call(
            functools.partial(early_kernel, skip_count, windows),
            in_specs=[SMEM, VMEM, pl.BlockSpec(memory_space=pl.ANY)],
            out_specs=[VMEM, VMEM],
            out_shape=[
                jax.ShapeDtypeStruct((HEADS, WTOK, 128), F32),
                jax.ShapeDtypeStruct((1, 128), jnp.int32),
            ],
            scratch_shapes=[
                pltpu.VMEM((8, 384), F32),
                pltpu.VMEM((2, 8 * WTOK, 128), F32),
                pltpu.SMEM((skip_count,), jnp.int32),
            ],
            compiler_params=pltpu.CompilerParams(vmem_limit_bytes=16 * 1024 * 1024),
            cost_estimate=pl.CostEstimate(flops=100_000_000, bytes_accessed=1_000_000, transcendentals=0),
            name="early",
        )(kept(assignment[0]), kept(table_master.T), after)

    if plain:
        here = jnp.stack([me, me, me, lax.axis_index("slab")])
        (block,) = small_call(
            pack_kernel,
            "pack",
            [VMEM] * 3,
            [jax.ShapeDtypeStruct((INNER, *BLOCK), BF)],
            (kept(mat_master), kept(vec_master), kept(assignment)),
            moved=100_000,
        )
        block, skip_tokens = lax.optimization_barrier((block, skip_tokens))
        own = lax.all_to_all(block, "slab", split_axis=0, concat_axis=0)
        across = swap(skip_tokens, "skip", 2)
        near = swap(skip_tokens, "skip", 1)
        packs_across = swap(own, "skip", 2)
        bias, ranks = early_call(own)
        packs_across, across, bias, ranks = lax.optimization_barrier(
            (packs_across, across, bias, ranks)
        )
        packs = [own, swap(own, "skip", 1), packs_across, swap(packs_across, "skip", 1)]
        pieces = [skip_tokens, near, across, swap(across, "skip", 1)]
    else:
        zero = jnp.zeros_like(me)
        here = jnp.stack([zero, zero, me, zero])
        low = jnp.concatenate([mat_master, vec_master], axis=1).astype(BF)
        low = lax.all_gather(low, ("slab", "skip"), axis=0, tiled=True)
        vec = padded(low[:, mat_width:].reshape(ROWS, -1), 128)
        low = padded(
            jnp.concatenate([repack(low, ROWS), vec], axis=1), BLOCK[0] * BLOCK[1]
        ).reshape(INNER, OUTER, *BLOCK)
        packs = [low[:, n] for n in range(OUTER)]
        pieces = [lax.all_gather(skip_tokens, "skip", axis=0, tiled=True)]
        bias, ranks = early_call(packs[0])

    layer_out, grad_decoder, everyone, *grads = layer_call(
        skip_count,
        assignment[0],
        extents,
        here,
        ranks,
        decoder_tokens.T,
        cotangent.T,
        bias,
        packs,
        [piece.T for piece in pieces],
    )
    grad_picks, grad_packs = grads[:skip_count], grads[skip_count:]

    def returned_call(here, everyone, after, received):
        (grad_skip,) = small_call(
            functools.partial(return_kernel, windows, OUTER),
            "returned",
            [SMEM, SMEM] + [VMEM] * (1 + skip_count),
            [jax.ShapeDtypeStruct((C, windows * WTOK), F32)],
            (here, everyone, after, *received),
            [
                pltpu.VMEM((skip_count, *received[0].shape), BF),
                pltpu.SMEM((windows,), jnp.int32),
            ],
            3_000_000,
        )
        return grad_skip

    shares = [
        jax.ShapeDtypeStruct((1, mat_width), F32),
        jax.ShapeDtypeStruct((1, vec_width), F32),
    ]
    if plain:
        far = swap(grad_packs[3], "skip", 1)
        near = swap(grad_packs[1], "skip", 1)
        (far,) = small_call(
            skip_sum_kernel,
            "core_sum",
            [VMEM] * 2,
            [jax.ShapeDtypeStruct((INNER, *BLOCK), BF)],
            (grad_packs[2], far),
        )
        keep, send = small_call(
            split_kernel,
            "skip_sum",
            [SMEM] + [VMEM] * 3,
            [
                jax.ShapeDtypeStruct((INNER // 2, *BLOCK), F32),
                jax.ShapeDtypeStruct((INNER // 2, *BLOCK), BF),
            ],
            (here, grad_packs[0], near, swap(far, "skip", 2)),
        )
        send, grad_picks = lax.optimization_barrier((send, grad_picks))
        received = [grad_picks[0]] + [swap(grad_picks[d], "skip", d) for d in range(1, OUTER)]
        for distance in (1, 2):
            half = keep.shape[0] // 2
            keep, send = small_call(
                halve_kernel,
                "slab_half",
                [VMEM] * 2,
                [
                    jax.ShapeDtypeStruct((half, *BLOCK), F32),
                    jax.ShapeDtypeStruct((half, *BLOCK), BF),
                ],
                (keep, swap(send, "slab", distance)),
                moved=300_000,
            )
        came, received = lax.optimization_barrier((swap(send, "slab", 4), received))
        mat_share, vec_share, tail = small_call(
            slab_sum_kernel,
            "slab_sum",
            [VMEM] * 2,
            shares + [jax.ShapeDtypeStruct((ROWS, 128), F32)],
            (keep, came),
            moved=300_000,
        )
        grad_skip = returned_call(here, everyone, vec_share, received)
        tail = lax.all_to_all(tail, ("slab", "skip"), split_axis=0, concat_axis=0, tiled=True)
        tail, grad_skip = lax.optimization_barrier((tail, grad_skip))
    else:
        received = list(
            lax.all_to_all(jnp.stack(grad_picks), "skip", split_axis=0, concat_axis=0)
        )
        everyone = lax.all_gather(assignment, "skip", axis=0, tiled=True)
        rows = jnp.stack(grad_packs, axis=1).reshape(ROWS, -1)
        start, side = 128 * VEC_TILE, 128 * SIDE_TILE
        rows = jnp.concatenate(
            [
                repack(rows, device_count),
                rows[:, start : start + VEC // ROWS].reshape(device_count, -1),
                rows[:, side : side + TABLE_LANES].reshape(device_count, -1),
            ],
            axis=1,
        )
        share = lax.psum_scatter(
            rows.astype(F32), ("slab", "skip"), scatter_dimension=0, tiled=True
        )
        mat_share = share[:, :mat_width]
        vec_share = share[:, mat_width : mat_width + vec_width]
        table = lax.all_gather(
            share[:, mat_width + vec_width :], ("slab", "skip"), axis=0, tiled=True
        )
        squares = lax.psum(jnp.sum(share * share), ("slab", "skip")) * (1.0 / ROWS)
        tail = jnp.concatenate(
            [table.reshape(ROWS, TABLE_LANES), jnp.full((ROWS, 128 - TABLE_LANES), squares)],
            axis=1,
        )

    if not plain:
        grad_skip = returned_call(here, everyone, vec_share, received)
    groups = (
        (mat_master, mat_first, mat_second, mat_average),
        (vec_master, vec_first, vec_second, vec_average),
        (table_master.T, table_first.T, table_second.T, table_average.T),
    )
    kinds = [jax.ShapeDtypeStruct((1, 1), F32)]
    for group in groups:
        kinds += [jax.ShapeDtypeStruct(group[0].shape, F32)] * 5
        kinds += [jax.ShapeDtypeStruct(group[0].shape, BF)]
    outs = small_call(
        update_kernel,
        "update",
        [VMEM] * 15,
        kinds,
        (mat_share, vec_share, tail, *groups[0], *groups[1], *groups[2]),
    )
    return (
        layer_out.T,
        grad_decoder.T,
        grad_skip.T,
        outs[0].reshape(()),
        *outs[1:13],
        *[value.T for value in outs[13:]],
    )


def solution(mesh):
    split = P(("slab", "skip"), None)
    return jax.shard_map(
        on_device,
        mesh=mesh,
        in_specs=(split, split, split, P("slab"), P("slab", "skip"))
        + (split,) * 8
        + (P(),) * 4,
        out_specs=(split, split, split, P()) + (split,) * 12 + (P(),) * 6,
        check_vma=False,
    )
```
